32 devices in a mesh: rep: 8 (over y, x, core), grp: 4 (over z).
Axes of the slice: x: 2, y: 2, z: 4, core: 2. Of those that a mesh axis runs over, the one named last changes fastest.
Arguments:
- tokens: bfloat16 [2, 6144, 1024], P(None, ('rep', 'grp'))
- w_qkv: bfloat16 [1024, 3072], P('grp'), may hold values from -0.1875 to 0.1875
- w_out: bfloat16 [1024, 1024], P('grp'), may hold values from -2 to 2
- router: bfloat16 [1024, 4], P('grp'), may hold values from -0.375 to 0.375
- gains: bfloat16 [1024, 2], P('grp'), may hold values from 0.5 to 1.5
- rel_bias: bfloat16 [16, 32], P('grp'), may hold values from -4 to 4
- w_gate: bfloat16 [4, 1024, 2816], P('grp'), may hold values from -0.1875 to 0.1875
- w_up: bfloat16 [4, 1024, 2816], P('grp'), may hold values from -0.1875 to 0.1875
- w_down: bfloat16 [4, 2816, 1024], P('grp'), may hold values from -0.75 to 0.75
- lengths: int32 [2, 32], P(None, ('rep', 'grp')), may hold values from 144 to 192, as said below
- choices: int32 [2, 6144, 2], P(None, ('rep', 'grp')), may hold values from 0 to 3, all different within a row
- priority: int32 [2, 6144], P(None, ('rep', 'grp')), may hold values from 0 to 191, as said below
- cotangent: bfloat16 [2, 6144, 1024], P(None, ('rep', 'grp')), may hold values from -6 to 6
Outputs:
- mixed: bfloat16 [2, 6144, 1024], P(None, ('rep', 'grp'))
- tokens_grad: float32 [2, 6144, 1024], P(None, ('rep', 'grp'))
- w_qkv_grad: float32 [1024, 3072], P('grp')
- w_out_grad: float32 [1024, 1024], P('grp')
- router_grad: float32 [1024, 4], P('grp')
- gains_grad: float32 [1024, 2], P('grp')
- rel_bias_grad: float32 [16, 32], P('grp')
- w_gate_grad: float32 [4, 1024, 2816], P('grp')
- w_up_grad: float32 [4, 1024, 2816], P('grp')
- w_down_grad: float32 [4, 2816, 1024], P('grp')
The draws below stay inside these ranges and needn't reach their ends.
Inputs may be any that keep to these rules, and one draw needn't show every extreme that they name: `lengths`: each device holds one sequence of each micro-batch; in every micro-batch some sequence fills all 192 slots. `choices`: the two experts of a token differ. `priority`: within each micro-batch, the entries of the 192 slots of one sequence are a permutation of 0 to 191.
All inputs are finite; a program needn't handle non-finite values.
Results may differ from the reference program's by a relative error of at most 0.02.
Values may be sent and summed in bfloat16 or wider, within the bound.
No kernel may reach another device: no remote copies, remote signals or barrier semaphores. Data moves between devices by JAX's collectives and lax.ppermute only.
A program may use at most 256 MiB of HBM per device.

```python
import math
import jax
import jax.numpy as jnp
import numpy as np
from jax import lax

D = 1024
HEADS = 16
HEAD_DIM = 64
EXPERTS = 4
BUCKETS = 32
MAX_DIST = 128
MICRO = 2
SLOT = 192
TOKENS = 6144
SPLIT = 1
HALF = 2816
CAP = 120
N_GRP = 4


def draw_tokens(key, part):
    key = jax.random.fold_in(key, 11)
    base_key, row_key, col_key = jax.random.split(key, 3)
    row_scale = jnp.exp(jax.random.uniform(row_key, (MICRO, TOKENS, 1), jnp.float32, math.log(0.35), math.log(3.5)))
    col_scale = jnp.exp(jax.random.uniform(col_key, (1, 1, D), jnp.float32, math.log(0.5), math.log(2.5)))
    base = jax.random.normal(base_key, (MICRO, TOKENS, D), jnp.float32)
    return (base * row_scale * col_scale).astype(jnp.bfloat16)


def draw_lengths(key, part):
    key = jax.random.fold_in(key, 5)
    value_key, full_key = jax.random.split(key, 2)
    seq_count = TOKENS // SLOT
    values_drawn = jax.random.randint(value_key, (MICRO, seq_count), 3 * SLOT // 4, SLOT + 1)
    full_slot = jax.random.randint(full_key, (MICRO, 1), 0, seq_count)
    filled = jnp.where(jnp.arange(seq_count)[None, :] == full_slot, SLOT, values_drawn)
    return filled.astype(jnp.int32)


def draw_priority(key, part):
    key = jax.random.fold_in(key, 7)
    seq_count = TOKENS // SLOT
    raw_scores = jax.random.randint(key, (MICRO, seq_count, SLOT), 0, 1 << 20) * SLOT + jnp.arange(SLOT)[None, None, :]
    ranks = jnp.argsort(raw_scores, axis=-1)
    return ranks.astype(jnp.int32).reshape(MICRO, TOKENS)


def block_scale(key, extent, shards, smallest, high):
    loudness = 1.0
    for axis_at, shards_of in shards:
        heights = jax.random.uniform(jax.random.fold_in(jax.random.fold_in(key, 6), axis_at), (shards_of,), jnp.float32, smallest / len(shards), high / len(shards))
        loudness = loudness * jnp.repeat(jnp.exp(heights), extent[axis_at] // shards_of).reshape((-1,) + (1,) * (len(extent) - 1 - axis_at))
    return loudness


def choose_distinct(stream_key, rows, number_of, top, lift):
    ranking = jax.random.permutation(jax.random.fold_in(stream_key, 1), number_of)
    boost = ranking
    for power in range(3):
        boost = boost * boost // number_of
    boost = boost * lift // number_of
    chance = jax.random.randint(jax.random.fold_in(stream_key, 2), (rows, number_of), 0, 4096) + boost
    fixed_rows = jax.random.permutation(jax.random.fold_in(stream_key, 3), rows)[jnp.arange(number_of) % rows]
    chance = jnp.where(jnp.arange(rows)[:, None] == fixed_rows[None, :], 1 << 14, chance)
    score = chance * number_of + jnp.arange(number_of)
    return lax.top_k(score.astype(jnp.int32), top)[1].astype(jnp.int32)


def noise(rng, dims, scale, reach, cuts=(), kind=jnp.bfloat16):
    gain = block_scale(rng, dims, cuts, -0.22, 0.18) if cuts else 1.0
    entries = jax.random.normal(rng, dims, jnp.float32) * scale * gain
    return jnp.minimum(jnp.maximum(entries, -reach), reach).astype(kind)


def setup_inputs(seed: int = 0) -> dict:
    keys = jax.random.split(jax.random.key(seed), 14)
    tokens = draw_tokens(jax.random.fold_in(keys[13], 71), 0)
    w_qkv = noise(keys[1], (D, 3 * D), D ** -0.5, 0.1875, ((0, 4),))
    w_out = noise(keys[2], (D, D), 0.15, 2.0, ((0, 4),))
    router = noise(keys[3], (D, EXPERTS), 0.025, 0.375, ((0, 4),))
    gains = jnp.clip(1.0 + 0.1 * jax.random.normal(keys[4], (D, 2), jnp.float32), 0.5, 1.5).astype(jnp.bfloat16)
    rel_bias = noise(keys[5], (HEADS, BUCKETS), 1.0, 4.0, ((0, 4),))
    w_gate = noise(keys[6], (N_GRP, D, HALF), D ** -0.5, 0.1875, ((0, 4),))
    w_up = noise(keys[7], (N_GRP, D, HALF), D ** -0.5, 0.1875, ((0, 4),))
    w_down = noise(keys[8], (N_GRP, HALF, D), 0.05, 0.75, ((0, 4),))
    lengths = draw_lengths(jax.random.fold_in(keys[13], 71), 0)
    choices = choose_distinct(keys[10], MICRO * TOKENS, EXPERTS, 2, 4096).reshape((MICRO, TOKENS, 2))
    priority = draw_priority(jax.random.fold_in(keys[13], 71), 0)
    cotangent = noise(keys[12], (MICRO, TOKENS, D), 1.0, 6.0, ((1, 32),))
    return dict(tokens=tokens, w_qkv=w_qkv, w_out=w_out, router=router, gains=gains, rel_bias=rel_bias, w_gate=w_gate, w_up=w_up, w_down=w_down, lengths=lengths, choices=choices, priority=priority, cotangent=cotangent)


HIGHEST = lax.Precision.HIGHEST

@jax.custom_vjp
def low(v):
    return lax.optimization_barrier(v.astype(jnp.bfloat16)).astype(jnp.float32)

@jax.custom_vjp
def low_back(v):
    return v

def low_keep(v):
    return (low(v), None)

def low_pass(kept, grad):
    return (grad,)

def back_keep(v):
    return (v, None)

def back_low(kept, grad):
    return (low(grad),)
low.defvjp(low_keep, low_pass)
low_back.defvjp(back_keep, back_low)

def bucket_matrix():
    distance = np.arange(SLOT)
    exact_count = BUCKETS // 2
    safe_span = np.maximum(distance, 1) / exact_count
    log_bucket = exact_count + np.floor(np.log(safe_span) / np.log(MAX_DIST / exact_count) * (BUCKETS - exact_count)).astype(np.int32)
    bucket_of = np.where(distance < exact_count, distance, np.minimum(log_bucket, BUCKETS - 1))
    offsets = np.maximum(distance[:, None] - distance[None, :], 0)
    return bucket_of[offsets].astype(np.int32)

def rms_norm(values_in, gain_vec):
    return values_in * lax.rsqrt(lax.optimization_barrier(jnp.mean(values_in * values_in, axis=-1, keepdims=True)) + 1e-06) * gain_vec

def geglu(gate_pre, up_pre):
    return jax.nn.gelu(gate_pre, approximate=True) * up_pre

def routing(expert_pick, priority_row, length):
    live_mask = (jnp.arange(SLOT) < length).astype(jnp.float32)
    pick_hits = (expert_pick[:, :, None] == jnp.arange(EXPERTS)[None, None, :]).astype(jnp.float32)
    expert_hits = lax.optimization_barrier(jnp.sum(pick_hits, axis=1)) * live_mask[:, None]
    before = (priority_row[None, :] < priority_row[:, None]).astype(jnp.float32)
    ahead_count = jnp.dot(before, expert_hits, precision=HIGHEST)
    return expert_hits * (ahead_count < CAP - 0.5).astype(jnp.float32)

def sequence(inputs_f, params, kept, length):
    w_qkv, w_out, router, gains, rel_bias, w_gate, w_up, w_down = params
    positions = jnp.arange(SLOT)
    allowed = (positions[None, :] <= positions[:, None]) & (positions[None, :] < length)
    xn_first = low(rms_norm(inputs_f, gains[:, 0]))
    qkv_rows = low(low_back(jnp.dot(xn_first, w_qkv, precision=HIGHEST)))
    queries = qkv_rows[:, :D].reshape(SLOT, HEADS, HEAD_DIM)
    keys_all = qkv_rows[:, D:2 * D].reshape(SLOT, HEADS, HEAD_DIM)
    values_all = qkv_rows[:, 2 * D:].reshape(SLOT, HEADS, HEAD_DIM)
    scores = jnp.einsum('ihd,jhd->hij', queries, keys_all, precision=HIGHEST) * HEAD_DIM ** (-0.5)
    scores = scores + rel_bias[:, bucket_matrix()]
    scores = low_back(jnp.where(allowed[None], scores, -1e+30))
    attn_probs = low(jax.nn.softmax(scores, axis=-1))
    heads_out = jnp.einsum('hij,jhd->ihd', attn_probs, values_all, precision=HIGHEST).reshape(SLOT, D)
    heads_out = low(low_back(heads_out))
    hidden = inputs_f + low_back(jnp.dot(heads_out, w_out, precision=HIGHEST))
    xn_second = low(rms_norm(hidden, gains[:, 1]))
    logits = low_back(jnp.dot(xn_second, router, precision=HIGHEST))
    gate_dense = jax.nn.softmax(logits, axis=-1) * kept
    result = hidden
    for expert_id in range(EXPERTS):
        summed = jnp.zeros((SLOT, D), jnp.float32)
        for half_id in range(SPLIT):
            block_id = expert_id * SPLIT + half_id
            inputs = low_back(xn_second)
            gate_pre = low_back(jnp.dot(inputs, w_gate[block_id], precision=HIGHEST))
            up_pre = low_back(jnp.dot(inputs, w_up[block_id], precision=HIGHEST))
            activated = low(geglu(gate_pre, up_pre))
            summed = summed + low(jnp.dot(activated, w_down[block_id], precision=HIGHEST))
        result = result + gate_dense[:, expert_id:expert_id + 1] * low_back(summed)
    return result

def reference(tokens, w_qkv, w_out, router, gains, rel_bias, w_gate, w_up, w_down, lengths, choices, priority, cotangent):
    params = (w_qkv.astype(jnp.float32), w_out.astype(jnp.float32), router.astype(jnp.float32), gains.astype(jnp.float32), rel_bias.astype(jnp.float32), w_gate.astype(jnp.float32), w_up.astype(jnp.float32), w_down.astype(jnp.float32))
    seq_count = TOKENS // SLOT
    seq_inputs = tokens.astype(jnp.float32).reshape(MICRO * seq_count, SLOT, D)
    seq_cots = cotangent.astype(jnp.float32).reshape(MICRO * seq_count, SLOT, D)
    seq_lens = lengths.reshape(MICRO * seq_count)
    seq_picks = choices.reshape(MICRO * seq_count, SLOT, 2)
    seq_order = priority.reshape(MICRO * seq_count, SLOT)

    def seq_step(totals, seq_item):
        inputs_f, seq_cot, length, expert_pick, priority_row = seq_item
        kept = routing(expert_pick, priority_row, length)
        layer_out, pull_back = jax.vjp(lambda v, p: sequence(v, p, kept, length), inputs_f, params)
        grad_input, grad_params = pull_back(seq_cot)
        totals = jax.tree.map(lambda a, b: a + b, totals, grad_params)
        return (totals, (layer_out.astype(jnp.bfloat16), grad_input))
    zero_grads = jax.tree.map(jnp.zeros_like, params)
    totals, (layer_outs, input_grads) = lax.scan(seq_step, zero_grads, (seq_inputs, seq_cots, seq_lens, seq_picks, seq_order))
    return (layer_outs.reshape(MICRO, TOKENS, D), input_grads.reshape(MICRO, TOKENS, D), totals[0], totals[1], totals[2], totals[3], totals[4], totals[5], totals[6], totals[7])
```

```python
import functools

import jax
import jax.numpy as jnp
import numpy as np
from jax import lax
from jax.experimental import pallas as pl
from jax.experimental.pallas import tpu as pltpu
from jax.sharding import PartitionSpec as P

D = 1024
HEADS = 16
HEAD_DIM = 64
EXPERTS = 4
BUCKETS = 32
MAX_DIST = 128
MICRO = 2
SLOT = 192
CAP = 120
VMEM_LIMIT = 56 * 1024 * 1024


HIGHEST = lax.Precision.HIGHEST


def bucket_matrix():
    distance = np.arange(SLOT)
    exact_count = BUCKETS // 2
    safe_span = np.maximum(distance, 1) / exact_count
    log_bucket = exact_count + np.floor(
        np.log(safe_span) / np.log(MAX_DIST / exact_count) * (BUCKETS - exact_count)
    ).astype(np.int32)
    bucket_of = np.where(distance < exact_count, distance, np.minimum(log_bucket, BUCKETS - 1))
    offsets = np.maximum(distance[:, None] - distance[None, :], 0)
    return bucket_of[offsets].astype(np.int32)


def rms_norm(values_in, gain_vec):
    return (
        values_in
        * lax.rsqrt(jnp.mean(values_in * values_in, axis=-1, keepdims=True) + 1e-06)
        * gain_vec
    )


def geglu(gate_pre, up_pre):
    return jax.nn.gelu(gate_pre, approximate=True) * up_pre


def dot(left, right):
    return jnp.dot(left, right, preferred_element_type=jnp.float32)


def contract_last(left, right):
    return lax.dot_general(
        left, right, (((1,), (1,)), ((), ())), preferred_element_type=jnp.float32
    )


def contract_first(left, right):
    return lax.dot_general(
        left, right, (((0,), (0,)), ((), ())), preferred_element_type=jnp.float32
    )


def expert_slots(expert_pick, priority_row, length):
    live_mask = (jnp.arange(SLOT) < length).astype(jnp.float32)
    pick_hits = (expert_pick[:, :, None] == jnp.arange(EXPERTS)[None, None, :]).astype(jnp.float32)
    expert_hits = jnp.sum(pick_hits, axis=1) * live_mask[:, None]
    before = (priority_row[None, :] < priority_row[:, None]).astype(jnp.bfloat16)
    ahead_count = dot(before, expert_hits.astype(jnp.bfloat16))
    place_pos = jnp.sum(pick_hits * ahead_count[:, None, :], axis=2)
    kept_mask = live_mask[:, None] * (place_pos < CAP - 0.5).astype(jnp.float32)
    slot_index = jnp.where(
        kept_mask > 0.5, expert_pick * CAP + place_pos.astype(jnp.int32), EXPERTS * CAP
    )
    return (pick_hits, kept_mask, slot_index)


def attention_scores(queries, keys_all, bias_full, allowed, score_scale):
    scores = (
        jnp.einsum("ihd,jhd->hij", queries, keys_all, preferred_element_type=jnp.float32)
        * score_scale
        + bias_full
    )
    return jnp.where(allowed[None], scores, -1e30)


def exchange(block, axis, mask):
    return lax.ppermute(block, axis, [(i, i ^ mask) for i in range(lax.axis_size(axis))])


def masks_of(count):
    return [1 << bit for bit in range(count.bit_length() - 1)]


def spread(own, axis, masks):
    held = [(0, own)]
    for mask in masks:
        held += [(far ^ mask, exchange(block, axis, mask)) for far, block in held]
    return held


def swap_blocks(blocks):
    groups = lax.axis_size("grp")
    moved = [blocks[:CAP]]
    for mask in range(1, groups):
        moved.append(exchange(blocks[mask * CAP : (mask + 1) * CAP], "grp", mask))
    return jnp.concatenate(moved, axis=0)


def bit_of(index, mask):
    return (index & mask) // mask


def halve_and_add(block, masks, dim):
    place = lax.axis_index("rep")
    for mask in masks:
        half = block.shape[dim] // 2
        bit = bit_of(place, mask)
        theirs = lax.dynamic_slice_in_dim(block, (1 - bit) * half, half, dim)
        mine = lax.dynamic_slice_in_dim(block, bit * half, half, dim)
        got = exchange(theirs, "rep", mask)
        block = (mine.astype(jnp.float32) + got.astype(jnp.float32)).astype(block.dtype)
    return block


def rep_masks():
    masks = masks_of(lax.axis_size("rep"))
    return masks[3:], masks[:3]


def order_of(which, masks):
    return masks[:1] + (masks[1:] if which == 0 else masks[:0:-1])


def reduce_block(block, which, dim):
    extra, masks = rep_masks()
    for mask in extra:
        block = block + exchange(block, "rep", mask)
    return halve_and_add(block, order_of(which, masks), dim)


def widen(block, which):
    masks = order_of(which, rep_masks()[1])
    pairs = jnp.stack([block, exchange(block, "rep", masks[-1])])
    held = [pairs]
    for mask in masks[-2::-1]:
        held += [exchange(pair, "rep", mask) for pair in held]
    return held


def place_in(which):
    masks = order_of(which, rep_masks()[1])
    place = lax.axis_index("rep")
    index = 0
    for mask in masks:
        index = 2 * index + bit_of(place, mask)
    return index


def assemble(first, second, dim):
    count = 2 * len(first)
    rows, cols = first[0].shape[1:]
    places = jnp.stack([place_in(0), place_in(1)]).astype(jnp.int32)

    def body(place_ref, *refs):
        out_ref = refs[-1]
        half = pl.program_id(0)
        far = pl.program_id(1) ^ place_ref[half]
        for at, ref in enumerate(refs[:-1]):
            of_half, pair = at // len(first), at % len(first)

            @pl.when((half == of_half) & (far // 2 == pair))
            def _():
                out_ref[...] = ref[0].astype(jnp.float32)

    def piece_spec(of_half, pair):
        def index(half, step, place_ref):
            far = step ^ place_ref[half]
            chosen = (half == of_half) & (far // 2 == pair)
            return (jnp.where(chosen, far % 2, 0), 0, 0)

        return pl.BlockSpec((1, rows, cols), index)

    if dim == 0:
        out_shape = (2 * count * rows, cols)
        out_spec = pl.BlockSpec((rows, cols), lambda half, step, place_ref: (half * count + step, 0))
    else:
        out_shape = (count * rows, 2 * cols)
        out_spec = pl.BlockSpec((rows, cols), lambda half, step, place_ref: (step, half))
    return pl.pallas_call(
        body,
        grid_spec=pltpu.PrefetchScalarGridSpec(
            num_scalar_prefetch=1,
            grid=(2, count),
            in_specs=[piece_spec(h, p) for h in range(2) for p in range(len(first))],
            out_specs=out_spec,
        ),
        out_shape=jax.ShapeDtypeStruct(out_shape, jnp.float32),
        compiler_params=pltpu.CompilerParams(vmem_limit_bytes=VMEM_LIMIT),
        cost_estimate=pl.CostEstimate(
            flops=0, bytes_accessed=6 * out_shape[0] * out_shape[1], transcendentals=0
        ),
        name="assemble",
    )(places, *first, *second)


def gather_weights(w_qkv, w_out):
    slices = min(lax.axis_size("rep"), 8)
    eighth = lax.axis_index("rep") % slices
    width = D // slices
    parts = [w_qkv[:, i * D : (i + 1) * D] for i in range(3)] + [w_out]
    own = jnp.concatenate(
        [lax.dynamic_slice_in_dim(part, eighth * width, width, 1) for part in parts], axis=1
    )
    over_grp = spread(own, "grp", masks_of(lax.axis_size("grp"))[::-1])
    half = len(over_grp) // 2
    masks = masks_of(slices)
    pieces = []
    for which in range(2):
        mine = over_grp[which * half : (which + 1) * half]
        block = jnp.stack([b for _, b in mine])
        order = masks[1:] if which == 0 else masks[:0:-1]
        for far, piece in spread(block, "rep", order + masks[:1]):
            pieces.append((far, [m for m, _ in mine], piece))
    return pieces


def project_kernel(plan, place_ref, tokens_ref, gain_ref, *refs):
    count = len(plan)
    pieces = refs[:count]
    xn_ref, qkv_ref, wqkv_ref, wout_ref = refs[count:]
    width = pieces[0].shape[2] // 4
    depth = pieces[0].shape[1]
    for micro in range(MICRO):
        x = tokens_ref[micro].astype(jnp.float32)
        scale = lax.rsqrt(jnp.mean(x * x, axis=-1, keepdims=True) + 1e-06)
        xn_ref[micro] = (x * scale * gain_ref[...]).astype(jnp.bfloat16)
    by_far = {}
    for (far, over_grp), piece in zip(plan, pieces):
        for at, m in enumerate(over_grp):
            by_far.setdefault(far, []).append((m, piece, at))
    for far, listed in by_far.items():
        column = pl.multiple_of((place_ref[0] ^ far) * width, width)
        total = None
        for m, piece, at in listed:
            row = pl.multiple_of((place_ref[1] ^ m) * depth, depth)
            weight = piece[at]
            for part in range(3):
                wqkv_ref[pl.ds(row, depth), pl.ds(column + part * D, width)] = weight[
                    :, part * width : (part + 1) * width
                ]
            wout_ref[pl.ds(row, depth), pl.ds(column, width)] = weight[:, 3 * width :]
            xs = xn_ref[:, :, pl.ds(row, depth)].reshape(MICRO * SLOT, depth)
            term = dot(xs, weight[:, : 3 * width])
            total = term if total is None else total + term
        for part in range(3):
            qkv_ref[:, :, pl.ds(column + part * D, width)] = (
                total[:, part * width : (part + 1) * width]
                .astype(jnp.bfloat16)
                .reshape(MICRO, SLOT, width)
            )


def project(tokens, gain_first, pieces):
    slices = min(lax.axis_size("rep"), 8)
    places = jnp.stack([lax.axis_index("rep") % slices, lax.axis_index("grp")]).astype(jnp.int32)
    plan = [(far, over_grp) for far, over_grp, _ in pieces]
    vmem = pl.BlockSpec(memory_space=pltpu.VMEM)
    return pl.pallas_call(
        functools.partial(project_kernel, plan),
        in_specs=[pl.BlockSpec(memory_space=pltpu.SMEM)] + [vmem] * (2 + len(pieces)),
        out_specs=[vmem] * 4,
        out_shape=[
            jax.ShapeDtypeStruct((MICRO, SLOT, D), jnp.bfloat16),
            jax.ShapeDtypeStruct((MICRO, SLOT, 3 * D), jnp.bfloat16),
            jax.ShapeDtypeStruct((D, 3 * D), jnp.bfloat16),
            jax.ShapeDtypeStruct((D, D), jnp.bfloat16),
        ],
        compiler_params=pltpu.CompilerParams(vmem_limit_bytes=VMEM_LIMIT),
        cost_estimate=pl.CostEstimate(
            flops=6 * MICRO * SLOT * D * D, bytes_accessed=20 * D * D, transcendentals=0
        ),
        name="project",
    )(places, tokens, gain_first.reshape(1, D), *[piece for _, _, piece in pieces])


def gather_small(router, gains, rel_bias):
    groups = lax.axis_size("grp")
    flat = jnp.concatenate([router.reshape(-1), gains.reshape(-1), rel_bias.reshape(-1)])
    padded = -(-flat.size // 2048) * 2048
    own = jnp.pad(flat, (0, padded - flat.size)).reshape(-1, 128)
    place = lax.axis_index("grp")
    blocks = [own] + [exchange(own, "grp", m) for m in range(1, groups)]
    rows = []
    for at in range(groups):
        row = blocks[0].astype(jnp.float32)
        for m in range(1, groups):
            row = jnp.where(place ^ m == at, blocks[m].astype(jnp.float32), row)
        rows.append(row.reshape(-1))
    every = jnp.stack(rows)
    a, b = router.size, router.size + gains.size
    return (
        every[:, :a].reshape(-1, router.shape[1]).astype(jnp.bfloat16),
        every[:, a:b].reshape(-1, gains.shape[1]),
        every[:, b : flat.size].reshape(-1, rel_bias.shape[1]),
    )


def per_device(
    tokens,
    w_qkv,
    w_out,
    router,
    gains,
    rel_bias,
    w_gate,
    w_up,
    w_down,
    lengths,
    choices,
    priority,
    cotangent,
):
    groups = lax.axis_size("grp")
    split_count = groups // EXPERTS
    place = lax.axis_index("grp")
    my_expert = place // split_count
    pieces = gather_weights(w_qkv, w_out)
    router_weight, gain_full, bias_table = gather_small(router, gains, rel_bias)
    gate_weight = w_gate[0]
    up_weight = w_up[0]
    down_weight = w_down[0]
    score_scale = HEAD_DIM ** (-0.5)
    positions = jnp.arange(SLOT)
    bucket_hits = (
        jnp.asarray(bucket_matrix())[:, :, None] == jnp.arange(BUCKETS)[None, None, :]
    ).astype(jnp.float32)
    bias_full = jnp.einsum("hk,ijk->hij", bias_table, bucket_hits, precision=HIGHEST)

    target = (
        ((place ^ jnp.arange(groups)) // split_count)[:, None] * CAP + jnp.arange(CAP)[None, :]
    ).reshape(-1)
    routes = []
    for micro in range(MICRO):
        pick_hits, kept_mask, slot_index = expert_slots(
            choices[micro], priority[micro], lengths[micro, 0]
        )
        hits = [
            (target[:, None] == slot_index[None, :, k]).astype(jnp.bfloat16) for k in range(2)
        ]
        spots = hits[0] + hits[1]
        grad_rows = swap_blocks(dot(spots, cotangent[micro]).astype(jnp.bfloat16))
        routes.append((pick_hits, kept_mask, hits, spots, grad_rows))

    xn_all, qkv_all, qkv_weight, out_weight = project(tokens, gain_full[:, 0], pieces)

    forward = []
    for micro in range(MICRO):
        pick_hits, kept_mask, hits, spots, grad_rows = routes[micro]
        inputs_f = tokens[micro].astype(jnp.float32)
        length = lengths[micro, 0]
        allowed = (positions[None, :] <= positions[:, None]) & (positions[None, :] < length)
        qkv_rows = qkv_all[micro]
        queries = qkv_rows[:, :D].reshape(SLOT, HEADS, HEAD_DIM)
        keys_all = qkv_rows[:, D : 2 * D].reshape(SLOT, HEADS, HEAD_DIM)
        values_all = qkv_rows[:, 2 * D :].reshape(SLOT, HEADS, HEAD_DIM)
        scores = attention_scores(queries, keys_all, bias_full, allowed, score_scale)
        row_max = jnp.max(scores, axis=-1, keepdims=True)
        weights_exp = jnp.exp(scores - row_max)
        row_total = jnp.sum(weights_exp, axis=-1, keepdims=True)
        log_total = row_max + jnp.log(row_total)
        probs_low = (weights_exp / row_total).astype(jnp.bfloat16)
        heads_out = jnp.einsum(
            "hij,jhd->ihd", probs_low, values_all, preferred_element_type=jnp.float32
        )
        heads_out = heads_out.reshape(SLOT, D).astype(jnp.bfloat16)
        hidden = inputs_f + dot(heads_out, out_weight)
        xn_second = rms_norm(hidden, gain_full[:, 1]).astype(jnp.bfloat16)
        rows = swap_blocks(dot(spots, xn_second).astype(jnp.bfloat16))
        forward.append(
            (inputs_f, allowed, queries, keys_all, values_all, log_total, heads_out, hidden, xn_second, rows)
        )

    expert = []
    for micro in range(MICRO):
        rows, grad_rows = forward[micro][-1], routes[micro][-1]
        gate_pre = dot(rows, gate_weight)
        up_pre = dot(rows, up_weight)
        act_full, act_back = jax.vjp(geglu, gate_pre, up_pre)
        act = act_full.astype(jnp.bfloat16)
        returned = swap_blocks(dot(act, down_weight).astype(jnp.bfloat16))
        route_rows = jax.nn.softmax(dot(rows, router_weight), axis=-1)
        gate_rows = jnp.sum(
            jnp.where(jnp.arange(EXPERTS)[None, :] == my_expert, route_rows, 0.0), axis=1, keepdims=True
        )
        grad_out_rows = (gate_rows * grad_rows.astype(jnp.float32)).astype(jnp.bfloat16)
        grad_gate_pre, grad_up_pre = act_back(contract_last(grad_out_rows, down_weight))
        gate_low = grad_gate_pre.astype(jnp.bfloat16)
        up_low = grad_up_pre.astype(jnp.bfloat16)
        row_back = (contract_last(gate_low, gate_weight) + contract_last(up_low, up_weight)).astype(
            jnp.bfloat16
        )
        returned_grad = swap_blocks(row_back)
        expert.append((rows, grad_out_rows, act, gate_low, up_low, returned, returned_grad))

    rows, grad_out_rows, act, gate_low, up_low = (
        jnp.concatenate([expert[micro][i] for micro in range(MICRO)], axis=0) for i in range(5)
    )
    down_grad = contract_first(act, grad_out_rows).astype(jnp.bfloat16)
    gate_grad = contract_first(rows, gate_low).astype(jnp.bfloat16)
    up_grad = contract_first(rows, up_low).astype(jnp.bfloat16)
    expert_grads = []
    for grad, dim in ((gate_grad, 0), (up_grad, 0), (down_grad, 1)):
        half = grad.shape[dim] // 2
        halves = [lax.slice_in_dim(grad, w * half, (w + 1) * half, axis=dim) for w in range(2)]
        lists = [widen(reduce_block(h, w, 0), w) for w, h in enumerate(halves)]
        expert_grads.append(assemble(lists[0], lists[1], dim)[None])

    outputs_list = []
    token_grads = []
    back = []
    for micro in range(MICRO):
        pick_hits, kept_mask, hits, spots, _ = routes[micro]
        (inputs_f, allowed, queries, keys_all, values_all, log_total, heads_out, hidden, xn_second, _) = (
            forward[micro]
        )
        returned, returned_grad = expert[micro][-2:]
        logits = dot(xn_second, router_weight)
        route_prob = jax.nn.softmax(logits, axis=-1)
        gate_pair = jnp.sum(pick_hits * route_prob[:, None, :], axis=2) * kept_mask
        grad_out = cotangent[micro].astype(jnp.float32)
        layer_out = hidden
        grad_route = jnp.zeros((SLOT, EXPERTS), jnp.float32)
        for k in range(2):
            pair_out = contract_first(hits[k], returned)
            layer_out = layer_out + gate_pair[:, k, None] * pair_out
            grad_gate = jnp.sum(grad_out * pair_out, axis=1) * kept_mask[:, k]
            grad_route = grad_route + pick_hits[:, k] * grad_gate[:, None]
        outputs_list.append(layer_out.astype(jnp.bfloat16))
        grad_logits = (
            route_prob * (grad_route - jnp.sum(route_prob * grad_route, axis=-1, keepdims=True))
        ).astype(jnp.bfloat16)
        router_grad = contract_first(xn_second, grad_logits)
        grad_xn_second = contract_last(grad_logits, router_weight) + contract_first(
            spots, returned_grad
        )
        second_back = jax.vjp(rms_norm, hidden, gain_full[:, 1])[1]
        grad_hidden_norm, grad_gain_second = second_back(grad_xn_second)
        grad_hidden = grad_out + grad_hidden_norm
        grad_attn = grad_hidden.astype(jnp.bfloat16)
        grad_heads = (
            contract_last(grad_attn, out_weight).astype(jnp.bfloat16).reshape(SLOT, HEADS, HEAD_DIM)
        )
        scores_again = attention_scores(queries, keys_all, bias_full, allowed, score_scale)
        probs_full = jnp.exp(scores_again - log_total)
        probs_again = probs_full.astype(jnp.bfloat16)
        grad_values = jnp.einsum(
            "hij,ihd->jhd", probs_again, grad_heads, preferred_element_type=jnp.float32
        )
        grad_probs = jnp.einsum(
            "ihd,jhd->hij", grad_heads, values_all, preferred_element_type=jnp.float32
        )
        grad_scores = probs_full * (
            grad_probs - jnp.sum(probs_full * grad_probs, axis=-1, keepdims=True)
        )
        grad_scores = grad_scores.astype(jnp.bfloat16)
        grad_queries = (
            jnp.einsum("hij,jhd->ihd", grad_scores, keys_all, preferred_element_type=jnp.float32)
            * score_scale
        )
        grad_keys = (
            jnp.einsum("hij,ihd->jhd", grad_scores, queries, preferred_element_type=jnp.float32)
            * score_scale
        )
        grad_qkv = jnp.concatenate(
            [
                grad_queries.reshape(SLOT, D),
                grad_keys.reshape(SLOT, D),
                grad_values.reshape(SLOT, D),
            ],
            axis=1,
        ).astype(jnp.bfloat16)
        grad_xn_first = contract_last(grad_qkv, qkv_weight)
        first_back = jax.vjp(rms_norm, inputs_f, gain_full[:, 0])[1]
        grad_input_norm, grad_gain_first = first_back(grad_xn_first)
        token_grads.append(grad_hidden + grad_input_norm)
        back.append(
            (grad_qkv, heads_out, grad_attn, router_grad, grad_gain_first, grad_gain_second, grad_scores)
        )

    stacked = [jnp.concatenate([back[micro][i] for micro in range(MICRO)], axis=0) for i in range(3)]
    qkv_grad = contract_first(xn_all.reshape(MICRO * SLOT, D), stacked[0]).astype(jnp.bfloat16)
    out_grad = contract_first(stacked[1], stacked[2]).astype(jnp.bfloat16)
    depth = D // groups
    both = jnp.concatenate([qkv_grad, out_grad], axis=1).reshape(groups, depth, 4 * D)
    lists = []
    for which in range(2):
        block = reduce_block(both[:, :, which * 2 * D : (which + 1) * 2 * D], which, 1)
        total = lax.dynamic_index_in_dim(block, place, 0, keepdims=False).astype(jnp.float32)
        for m in range(1, groups):
            total = total + exchange(
                lax.dynamic_index_in_dim(block, place ^ m, 0, keepdims=False), "grp", m
            ).astype(jnp.float32)
        lists.append(widen(total.astype(jnp.bfloat16), which))
    attn_grad = assemble(lists[0], lists[1], 1)

    bias_grad = sum(
        jnp.einsum("hij,ijk->hk", back[micro][6].astype(jnp.float32), bucket_hits, precision=HIGHEST)
        for micro in range(MICRO)
    )
    small = [
        sum(back[micro][3] for micro in range(MICRO)).reshape(-1),
        jnp.stack([sum(back[micro][i] for micro in range(MICRO)) for i in (4, 5)], axis=1).reshape(-1),
        bias_grad.reshape(-1),
    ]
    flat = jnp.concatenate(small)
    flat = jnp.pad(flat, (0, -flat.size % 1024)).reshape(-1, 128)
    for axis in ("grp", "rep"):
        for mask in masks_of(lax.axis_size(axis)):
            flat = flat + exchange(flat, axis, mask)
    flat = flat.reshape(-1)
    outs = []
    start = 0
    for whole in ((D, EXPERTS), (D, 2), (HEADS, BUCKETS)):
        size = whole[0] * whole[1]
        rows_here = whole[0] // groups
        outs.append(
            lax.dynamic_slice_in_dim(
                flat[start : start + size].reshape(whole), place * rows_here, rows_here, 0
            )
        )
        start += size
    return (
        jnp.stack(outputs_list),
        jnp.stack(token_grads),
        attn_grad[:, : 3 * D],
        attn_grad[:, 3 * D :],
        outs[0],
        outs[1],
        outs[2],
        expert_grads[0],
        expert_grads[1],
        expert_grads[2],
    )


def solution(mesh):
    placed = (
        P(None, ("rep", "grp"), None),
        P("grp", None),
        P("grp", None),
        P("grp", None),
        P("grp", None),
        P("grp", None),
        P("grp", None, None),
        P("grp", None, None),
        P("grp", None, None),
        P(None, ("rep", "grp")),
        P(None, ("rep", "grp"), None),
        P(None, ("rep", "grp")),
        P(None, ("rep", "grp"), None),
    )
    return jax.shard_map(
        per_device,
        mesh=mesh,
        in_specs=placed,
        out_specs=(
            P(None, ("rep", "grp"), None),
            P(None, ("rep", "grp"), None),
            P("grp", None),
            P("grp", None),
            P("grp", None),
            P("grp", None),
            P("grp", None),
            P("grp", None, None),
            P("grp", None, None),
            P("grp", None, None),
        ),
        check_vma=False,
    )
```

```python
import functools

import jax
import jax.numpy as jnp
import numpy as np
from jax import lax
from jax.experimental import pallas as pl
from jax.experimental.pallas import tpu as pltpu
from jax.sharding import PartitionSpec as P

D = 1024
HEADS = 16
HEAD_DIM = 64
EXPERTS = 4
BUCKETS = 32
MAX_DIST = 128
MICRO = 2
SLOT = 192
CAP = 120
VMEM_LIMIT = 56 * 1024 * 1024
SHORT = pl.CostEstimate(flops=1, bytes_accessed=1, transcendentals=0)


VMEM = pl.BlockSpec(memory_space=pltpu.VMEM)
SMEM = pl.BlockSpec(memory_space=pltpu.SMEM)
ANY = pl.BlockSpec(memory_space=pl.ANY)


def params():
    return pltpu.CompilerParams(vmem_limit_bytes=VMEM_LIMIT)


def bucket_matrix():
    distance = np.arange(SLOT)
    exact_count = BUCKETS // 2
    safe_span = np.maximum(distance, 1) / exact_count
    log_bucket = exact_count + np.floor(
        np.log(safe_span) / np.log(MAX_DIST / exact_count) * (BUCKETS - exact_count)
    ).astype(np.int32)
    bucket_of = np.where(distance < exact_count, distance, np.minimum(log_bucket, BUCKETS - 1))
    offsets = np.maximum(distance[:, None] - distance[None, :], 0)
    return bucket_of[offsets].astype(np.int32)


def dot(left, right):
    return jnp.dot(left, right, preferred_element_type=jnp.float32)


def contract_last(left, right):
    return lax.dot_general(
        left, right, (((1,), (1,)), ((), ())), preferred_element_type=jnp.float32
    )


def contract_first(left, right):
    return lax.dot_general(
        left, right, (((0,), (0,)), ((), ())), preferred_element_type=jnp.float32
    )


def expert_slots(expert_pick, priority_row, length):
    live_mask = (jnp.arange(SLOT) < length).astype(jnp.float32)
    pick_hits = (expert_pick[:, :, None] == jnp.arange(EXPERTS)[None, None, :]).astype(jnp.float32)
    expert_hits = jnp.sum(pick_hits, axis=1) * live_mask[:, None]
    before = (priority_row[None, :] < priority_row[:, None]).astype(jnp.bfloat16)
    ahead_count = dot(before, expert_hits.astype(jnp.bfloat16))
    place_pos = jnp.sum(pick_hits * ahead_count[:, None, :], axis=2)
    kept_mask = live_mask[:, None] * (place_pos < CAP - 0.5).astype(jnp.float32)
    slot_index = jnp.where(
        kept_mask > 0.5, expert_pick * CAP + place_pos.astype(jnp.int32), EXPERTS * CAP
    )
    return (pick_hits, kept_mask, slot_index)


def exchange(block, axis, mask):
    return lax.ppermute(block, axis, [(i, i ^ mask) for i in range(lax.axis_size(axis))])


def masks_of(count):
    return [1 << bit for bit in range(count.bit_length() - 1)]


def spread(own, axis, masks):
    held = [(0, own)]
    for mask in masks:
        held += [(far ^ mask, exchange(block, axis, mask)) for far, block in held]
    return held


def to_experts(blocks):
    groups, rows, width = blocks.shape
    moved = lax.all_to_all(blocks, "grp", split_axis=0, concat_axis=0, tiled=True)
    return moved.reshape(groups * rows, width)


def bit_of(index, mask):
    return (index & mask) // mask


def tie(values, *after):
    return lax.optimization_barrier((tuple(values), after))[0]


def rep_masks():
    masks = masks_of(lax.axis_size("rep"))
    return masks[3:], masks[:3]


def order_of(which):
    masks = rep_masks()[1]
    return masks[:1] + (masks[1:] if which == 0 else masks[:0:-1])


def halves_of(block, mask, dim):
    half = block.shape[dim] // 2
    bit = bit_of(lax.axis_index("rep"), mask)
    return (
        lax.dynamic_slice_in_dim(block, (1 - bit) * half, half, dim),
        lax.dynamic_slice_in_dim(block, bit * half, half, dim),
    )


def add_low(left, right):
    return (left.astype(jnp.float32) + right.astype(jnp.float32)).astype(jnp.bfloat16)


class Halving:
    def __init__(self, which, dim):
        self.which, self.dim = which, dim
        self.masks = order_of(which)
        self.kept = self.moving = None
        self.held = None

    def start(self, send, keep, at):
        self.kept, self.moving = keep, exchange(send, "rep", self.masks[at])

    def land(self, *after):
        kept, got = tie((self.kept, self.moving), *after)
        return add_low(kept, got)

    def halve(self, at, *after):
        kept, got = tie((self.kept, self.moving), *after)
        kept, got = (halves_of(x, self.masks[at], self.dim) for x in (kept, got))
        self.start(*(add_low(k, g) for k, g in zip(kept, got)), at)
        return self.kept

    def own(self, *after):
        total = self.land(*after)
        for mask in rep_masks()[0]:
            total = add_low(total, exchange(total, "rep", mask))
        return total

    def back(self, piece):
        self.kept, self.moving = piece, exchange(piece, "rep", self.masks[-1])

    def back_pair(self, *after):
        kept, got = tie((self.kept, self.moving), *after)
        self.held = [jnp.stack([kept, got])]
        self.moving = [exchange(self.held[0], "rep", self.masks[-2])]
        return self.held[0]

    def back_rest(self, *after):
        self.held = list(tie([*self.held, *self.moving], *after))
        self.moving = [exchange(pair, "rep", self.masks[0]) for pair in self.held]
        return self.held[-1]

    def pieces(self, *after):
        return list(tie([*self.held, *self.moving], *after))

    def place(self):
        index = 0
        for mask in self.masks:
            index = 2 * index + bit_of(lax.axis_index("rep"), mask)
        return index


def assemble(pair_of_halves):
    lists = [half.pieces() for half in pair_of_halves]
    places = jnp.stack([half.place() for half in pair_of_halves]).astype(jnp.int32)
    each = len(lists[0])
    rows, cols = lists[0][0].shape[1:]
    deep = each // 2
    cut_cores = cols % 128 != 0

    def body(place_ref, *refs):
        half, core, step = (pl.program_id(i) for i in range(3))
        place = place_ref[half]
        far = (core * deep + step) ^ (place // 2)
        for at, ref in enumerate(refs[:-1]):
            for odd in range(2):

                @pl.when((half == at // each) & (far == at % each) & (place % 2 == odd))
                def _():
                    out = refs[-1].at[0] if cut_cores else refs[-1]
                    out[:rows] = ref[odd].astype(jnp.float32)
                    out[rows:] = ref[1 - odd].astype(jnp.float32)

    whole = pl.BlockSpec((2, rows, cols), lambda half, core, step, place_ref: (0, 0, 0))
    out_shape = (4 * deep * rows, 2 * cols)
    out_spec = pl.BlockSpec(
        (2 * rows, cols), lambda half, core, step, place_ref: (half * deep + step, core)
    )
    if cut_cores:
        out_shape = (2, 4 * deep * rows, cols)
        out_spec = pl.BlockSpec(
            (1, 2 * rows, cols), lambda half, core, step, place_ref: (core, half * deep + step, 0)
        )
    out = pl.pallas_call(
        body,
        grid_spec=pltpu.PrefetchScalarGridSpec(
            num_scalar_prefetch=1,
            grid=(2, 2, deep),
            in_specs=[whole] * (2 * each),
            out_specs=out_spec,
        ),
        out_shape=jax.ShapeDtypeStruct(out_shape, jnp.float32),
        compiler_params=params(),
        cost_estimate=SHORT,
        name="assemble",
    )(places, *lists[0], *lists[1])
    return jnp.concatenate([out[0], out[1]], axis=1) if cut_cores else out


def assemble_attention(pair_of_halves):
    lists = [half.pieces() for half in pair_of_halves]
    places = jnp.stack([half.place() for half in pair_of_halves]).astype(jnp.int32)
    each = len(lists[0])
    rows = lists[0][0].shape[1]

    def body(place_ref, *refs):
        qkv_ref, out_ref = refs[-2:]
        for at, ref in enumerate(refs[:-2]):
            for i in range(2):
                where = (2 * (at % each) + i) ^ place_ref[at // each]
                span = pl.ds(pl.multiple_of(where * rows, rows), rows)
                values = ref[i].astype(jnp.float32)
                if at < each:
                    qkv_ref[span, : 2 * D] = values
                else:
                    qkv_ref[span, 2 * D :] = values[:, :D]
                    out_ref[span, :] = values[:, D:]

    depth = 2 * each * rows
    return pl.pallas_call(
        body,
        in_specs=[SMEM] + [VMEM] * (2 * each),
        out_specs=[VMEM] * 2,
        out_shape=[
            jax.ShapeDtypeStruct((depth, 3 * D), jnp.float32),
            jax.ShapeDtypeStruct((depth, D), jnp.float32),
        ],
        compiler_params=params(),
        cost_estimate=SHORT,
        name="assemble_attention",
    )(places, *lists[0], *lists[1])


def gather_weights(w_qkv, w_out):
    slices = min(lax.axis_size("rep"), 8)
    eighth = lax.axis_index("rep") % slices
    width = D // slices
    parts = [w_qkv[:, i * D : (i + 1) * D] for i in range(3)] + [w_out]
    own = jnp.concatenate(
        [lax.dynamic_slice_in_dim(part, eighth * width, width, 1) for part in parts], axis=1
    )
    masks = masks_of(slices)
    over_grp = spread(own, "grp", masks_of(lax.axis_size("grp"))[::-1])
    half = len(over_grp) // 2
    pieces = []
    for which in range(2):
        mine = over_grp[which * half : (which + 1) * half]
        order = masks[1:] if which == 0 else masks[:0:-1]
        block = jnp.stack([piece for _, piece in mine])
        for far, piece in spread(block, "rep", order + masks[:1]):
            pieces.append((far, [m for m, _ in mine], piece))
    return pieces, [piece for _, piece in over_grp]


def norm_rows(x, gain):
    return x * lax.rsqrt(jnp.mean(x * x, axis=-1, keepdims=True) + 1e-06) * gain


def each_piece(plan, pieces, far):
    for (this, members), piece in zip(plan, pieces):
        if this == far:
            yield from ((m, piece, at) for at, m in enumerate(members))


def project_kernel(plan, place_ref, tokens_ref, gain_ref, *refs):
    count = len(plan)
    pieces = refs[:count]
    xn_ref, qkv0_ref, qkv1_ref, wout_ref = refs[-4:]
    depth = pieces[0].shape[1]
    width = pieces[0].shape[2] // 4
    for micro in range(MICRO):
        xn_ref[micro * SLOT : (micro + 1) * SLOT] = norm_rows(
            tokens_ref[micro].astype(jnp.float32), gain_ref[...]
        ).astype(jnp.bfloat16)
    for far in sorted({far for far, _ in plan}):
        column = pl.multiple_of((place_ref[0] ^ far) * width, width)
        total = None
        for m, piece, at in each_piece(plan, pieces, far):
            row = pl.multiple_of((place_ref[1] ^ m) * depth, depth)
            wout_ref[pl.ds(row, depth), pl.ds(column, width)] = piece[at, :, 3 * width :]
            term = dot(xn_ref[:, pl.ds(row, depth)], piece[at, :, : 3 * width])
            total = term if total is None else total + term
        for part in range(3):
            low = total[:, part * width : (part + 1) * width].astype(jnp.bfloat16)
            qkv0_ref[:, pl.ds(column + part * D, width)] = low[:SLOT]
            qkv1_ref[:, pl.ds(column + part * D, width)] = low[SLOT:]


def places_of():
    slices = min(lax.axis_size("rep"), 8)
    return jnp.stack([lax.axis_index("rep") % slices, lax.axis_index("grp")]).astype(jnp.int32)


def project(tokens, gain_first, pieces, waits):
    plan = [(far, m) for far, m, _ in pieces]
    return pl.pallas_call(
        functools.partial(project_kernel, plan),
        in_specs=[SMEM] + [VMEM] * (2 + len(pieces)) + [ANY] * len(waits),
        out_specs=[VMEM] * 4,
        out_shape=[
            jax.ShapeDtypeStruct((MICRO * SLOT, D), jnp.bfloat16),
            jax.ShapeDtypeStruct((SLOT, 3 * D), jnp.bfloat16),
            jax.ShapeDtypeStruct((SLOT, 3 * D), jnp.bfloat16),
            jax.ShapeDtypeStruct((D, D), jnp.bfloat16),
        ],
        compiler_params=params(),
        cost_estimate=SHORT,
        name="project",
    )(places_of(), tokens, gain_first.reshape(1, D), *[piece for _, _, piece in pieces], *waits)


def join_kernel(plan, place_ref, *refs):
    pieces, out_ref = refs[: len(plan)], refs[-1]
    depth = pieces[0].shape[1]
    width = pieces[0].shape[2] // 4
    for far in sorted({far for far, _ in plan}):
        column = pl.multiple_of((place_ref[0] ^ far) * width, width)
        for m, piece, at in each_piece(plan, pieces, far):
            row = pl.multiple_of((place_ref[1] ^ m) * depth, depth)
            for part in range(3):
                out_ref[pl.ds(row, depth), pl.ds(column + part * D, width)] = piece[
                    at, :, part * width : (part + 1) * width
                ]


def join_qkv(pieces, waits):
    plan = [(far, m) for far, m, _ in pieces]
    return pl.pallas_call(
        functools.partial(join_kernel, plan),
        in_specs=[SMEM] + [VMEM] * len(pieces) + [ANY] * len(waits),
        out_specs=VMEM,
        out_shape=jax.ShapeDtypeStruct((D, 3 * D), jnp.bfloat16),
        compiler_params=params(),
        cost_estimate=SHORT,
        name="join",
    )(places_of(), *[piece for _, _, piece in pieces], *waits)


def allowed_pairs(length):
    row = lax.broadcasted_iota(jnp.int32, (SLOT, SLOT), 0)
    column = lax.broadcasted_iota(jnp.int32, (SLOT, SLOT), 1)
    return (column <= row) & (column < length)


def attend_kernel(groups, length_ref, qkv_ref, tokens_ref, bias_ref, wout_ref, gain_ref, spots_ref, *refs):
    heads_ref, hidden_ref, xn_ref, rows_ref = refs[-4:]
    allowed = allowed_pairs(length_ref[0])
    scale = HEAD_DIM ** (-0.5)
    for pair in range(HEADS // 2):
        outs = []
        for head in (2 * pair, 2 * pair + 1):
            at = head * HEAD_DIM
            scores = contract_last(
                qkv_ref[:, at : at + HEAD_DIM], qkv_ref[:, D + at : D + at + HEAD_DIM]
            )
            scores = jnp.where(allowed, scores * scale + bias_ref[head].astype(jnp.float32), -1e30)
            weights = jnp.exp(scores - jnp.max(scores, axis=-1, keepdims=True))
            probs = weights / jnp.sum(weights, axis=-1, keepdims=True)
            outs.append(
                dot(probs.astype(jnp.bfloat16), qkv_ref[:, 2 * D + at : 2 * D + at + HEAD_DIM])
            )
        heads_ref[:, pair * 128 : (pair + 1) * 128] = jnp.concatenate(outs, axis=1).astype(jnp.bfloat16)
    hidden = tokens_ref[0].astype(jnp.float32) + dot(heads_ref[...], wout_ref[...])
    hidden_ref[...] = hidden
    xn = norm_rows(hidden, gain_ref[...]).astype(jnp.bfloat16)
    xn_ref[...] = xn
    for m in range(groups):
        rows_ref[m] = dot(spots_ref[m], xn).astype(jnp.bfloat16)


def attend(micro, length, qkv_rows, tokens, bias_full, out_weight, gain_second, spots, waits):
    groups = spots.shape[0]
    whole = lambda *shape: pl.BlockSpec(shape, lambda i: (0,) * len(shape))
    low = jax.ShapeDtypeStruct((SLOT, D), jnp.bfloat16)
    out_shape = [
        low,
        jax.ShapeDtypeStruct((SLOT, D), jnp.float32),
        low,
        jax.ShapeDtypeStruct((groups, CAP, D), jnp.bfloat16),
    ]
    return pl.pallas_call(
        functools.partial(attend_kernel, groups),
        grid=(1,),
        in_specs=[
            SMEM,
            whole(SLOT, 3 * D),
            pl.BlockSpec((1, SLOT, D), lambda i: (micro, 0, 0)),
            whole(HEADS, SLOT, SLOT),
            whole(D, D),
            whole(1, D),
            whole(groups, CAP, SLOT),
        ]
        + [ANY] * len(waits),
        out_specs=[whole(*o.shape) for o in out_shape],
        out_shape=out_shape,
        compiler_params=params(),
        cost_estimate=SHORT,
        name="attend",
    )(length.reshape(1), qkv_rows, tokens, bias_full, out_weight, gain_second.reshape(1, D), spots, *waits)


def gelu_parts(v):
    c = np.float32(np.sqrt(2 / np.pi))
    t = jnp.tanh(c * (v + np.float32(0.044715) * (v * v * v)))
    half = 0.5 * (1.0 + t)
    slope = half + 0.5 * v * (1.0 - t * t) * (c * (1.0 + np.float32(3 * 0.044715) * (v * v)))
    return v * half, slope


def expert_kernel(groups, expert_ref, rows_ref, grads_ref, router_ref, wg_ref, wu_ref, wd_ref, *refs):
    dout_ref, act_ref, dgate_ref, dup_ref, part_ref, total_ref = refs[-6:]
    step = pl.program_id(0)

    @pl.when(step == 0)
    def _():
        logits = dot(rows_ref[...], router_ref[...])
        lane = lax.broadcasted_iota(jnp.int32, logits.shape, 1)
        logits = jnp.where(lane < EXPERTS, logits, -1e30)
        weights = jnp.exp(logits - jnp.max(logits, axis=-1, keepdims=True))
        route = weights / jnp.sum(weights, axis=-1, keepdims=True)
        gate = jnp.sum(jnp.where(lane == expert_ref[0], route, 0.0), axis=-1, keepdims=True)
        dout_ref[...] = (gate * grads_ref[...].astype(jnp.float32)).astype(jnp.bfloat16)

    gate_pre = dot(rows_ref[...], wg_ref[0])
    up_pre = dot(rows_ref[...], wu_ref[0])
    gelu, slope = gelu_parts(gate_pre)
    act = (gelu * up_pre).astype(jnp.bfloat16)
    act_ref[...] = act
    grad_act = contract_last(dout_ref[...], wd_ref[0])
    dgate_ref[...] = (grad_act * up_pre * slope).astype(jnp.bfloat16)
    dup_ref[...] = (grad_act * gelu).astype(jnp.bfloat16)
    part = dot(act, wd_ref[0])

    @pl.when(step == 0)
    def _():
        total_ref[...] = part

    @pl.when(step > 0)
    def _():
        total_ref[...] += part

    @pl.when(step == pl.num_programs(0) - 1)
    def _():
        for m in range(groups):
            part_ref[m] = total_ref[m * CAP : (m + 1) * CAP].astype(jnp.bfloat16)


def run_expert(expert, rows, grad_rows, router_pad, w_gate, w_up, w_down, waits):
    count = rows.shape[0]
    groups = count // CAP
    hidden = w_gate.shape[2]
    chunk = 256 if hidden % 256 == 0 else 128
    whole = lambda *shape: pl.BlockSpec(shape, lambda i: (0,) * len(shape))
    wide = jax.ShapeDtypeStruct((count, hidden), jnp.bfloat16)
    block = pl.BlockSpec((count, chunk), lambda i: (0, i))
    return pl.pallas_call(
        functools.partial(expert_kernel, groups),
        grid=(hidden // chunk,),
        in_specs=[
            SMEM,
            whole(count, D),
            whole(count, D),
            whole(D, 128),
            pl.BlockSpec((1, D, chunk), lambda i: (0, 0, i)),
            pl.BlockSpec((1, D, chunk), lambda i: (0, 0, i)),
            pl.BlockSpec((1, chunk, D), lambda i: (0, i, 0)),
        ]
        + [ANY] * len(waits),
        out_specs=[whole(count, D), block, block, block, whole(groups, CAP, D)],
        out_shape=[jax.ShapeDtypeStruct((count, D), jnp.bfloat16), wide, wide, wide]
        + [jax.ShapeDtypeStruct((groups, CAP, D), jnp.bfloat16)],
        scratch_shapes=[pltpu.VMEM((count, D), jnp.float32)],
        compiler_params=params(),
        cost_estimate=SHORT,
        name="expert",
    )(jnp.reshape(expert, (1,)).astype(jnp.int32), rows, grad_rows, router_pad, w_gate, w_up, w_down, *waits)


def products_kernel(wide, bits_ref, left0, left1, right0, right1, *refs):
    total = contract_first(left0[...], right0[...]) + contract_first(left1[...], right1[...])
    if not wide:
        refs[-1][0] = total.astype(jnp.bfloat16)
        return
    total = (total + refs[0][0].astype(jnp.float32)).astype(jnp.bfloat16)
    half = total.shape[0] // 2
    step = pl.program_id(0)
    for which in range(2):
        send_ref, keep_ref = refs[-4 + 2 * which : len(refs) - 2 + 2 * which]
        for bit in range(2):

            @pl.when((step == which) & (bits_ref[1 + which] == bit))
            def _():
                keep_ref[...] = total[bit * half : (bit + 1) * half]
                send_ref[...] = total[(1 - bit) * half : (2 - bit) * half]


def products(left, right, arrived=None, waits=()):
    place = lax.axis_index("rep")
    wide = arrived is not None
    core = bit_of(place, 1)
    bits = jnp.stack(
        [core if wide else 1 - core] + [bit_of(place, order_of(w)[1]) for w in range(2)]
    ).astype(jnp.int32)
    count = left[0].shape[0]
    rows, cols = left[0].shape[1] // 2, right[0].shape[1] // 2
    if rows % 128 or cols % 128:
        return products_plain(left, right, arrived)
    piece = pl.BlockSpec((1, rows, cols), lambda h, b: (h, 0, 0))
    if wide:
        out_specs = [pl.BlockSpec((rows // 2, cols), lambda h, b: (0, 0))] * 4
        out_shape = [jax.ShapeDtypeStruct((rows // 2, cols), jnp.bfloat16)] * 4
    else:
        out_specs = [piece]
        out_shape = [jax.ShapeDtypeStruct((2, rows, cols), jnp.bfloat16)]
    return pl.pallas_call(
        functools.partial(products_kernel, wide),
        grid_spec=pltpu.PrefetchScalarGridSpec(
            num_scalar_prefetch=1,
            grid=(2,),
            in_specs=[pl.BlockSpec((count, rows), lambda h, b: (0, h))] * 2
            + [pl.BlockSpec((count, cols), lambda h, b: (0, b[0]))] * 2
            + ([piece] if wide else [])
            + [ANY] * len(waits),
            out_specs=out_specs,
        ),
        out_shape=out_shape,
        compiler_params=params(),
        cost_estimate=SHORT,
        name="products",
    )(bits, *left, *right, *([arrived] if wide else []), *waits)


def products_plain(left, right, arrived):
    total = contract_first(left[0], right[0]) + contract_first(left[1], right[1])
    theirs, mine = halves_of(total, 1, 1)
    if arrived is None:
        return [jnp.stack(jnp.split(theirs, 2, axis=0)).astype(jnp.bfloat16)]
    mine = jnp.stack(jnp.split(mine, 2, axis=0))
    mine = (mine + arrived.astype(jnp.float32)).astype(jnp.bfloat16)
    return [cut for w in range(2) for cut in halves_of(mine[w], order_of(w)[1], 0)]


def back_kernel(groups, dgate_ref, dup_ref, wg_ref, wu_ref, *refs):
    out_ref = refs[-1]
    total = contract_last(dgate_ref[...], wg_ref[0]) + contract_last(dup_ref[...], wu_ref[0])
    for m in range(groups):
        out_ref[m] = total[m * CAP : (m + 1) * CAP].astype(jnp.bfloat16)


def back_to_rows(groups, dgate, dup, w_gate, w_up, waits):
    count, hidden = dgate.shape
    quarter = D // 4
    return pl.pallas_call(
        functools.partial(back_kernel, groups),
        grid=(4,),
        in_specs=[pl.BlockSpec((count, hidden), lambda i: (0, 0))] * 2
        + [pl.BlockSpec((1, quarter, hidden), lambda i: (0, i, 0))] * 2
        + [ANY] * len(waits),
        out_specs=pl.BlockSpec((groups, CAP, quarter), lambda i: (0, 0, i)),
        out_shape=jax.ShapeDtypeStruct((groups, CAP, D), jnp.bfloat16),
        compiler_params=params(),
        cost_estimate=SHORT,
        name="back",
    )(dgate, dup, w_gate, w_up, *waits)


def norm_back(x, gain, grad):
    scale = lax.rsqrt(jnp.mean(x * x, axis=-1, keepdims=True) + 1e-06)
    plain = x * scale
    inner = grad * gain
    by_x = scale * (inner - plain * jnp.mean(inner * plain, axis=-1, keepdims=True))
    return by_x, jnp.sum(grad * plain, axis=0, keepdims=True)


def unwind_kernel(
    length_ref, part_ref, rows_ref, hit0_ref, hit1_ref, picks_ref, kept_ref, hidden_ref, xn_ref, cot_ref,
    router_ref, gain_ref, wout_ref, qkv_ref, bias_ref, *refs
):
    mixed_ref, dhidden_ref, dattn_ref, dqkv_ref, drouter_ref, dgain_ref, dscores_ref, dheads_ref = refs[-8:]
    xn = xn_ref[...]
    hidden = hidden_ref[...]
    grad_out = cot_ref[0].astype(jnp.float32)
    logits = dot(xn, router_ref[...])
    lane = lax.broadcasted_iota(jnp.int32, logits.shape, 1)
    logits = jnp.where(lane < EXPERTS, logits, -1e30)
    weights = jnp.exp(logits - jnp.max(logits, axis=-1, keepdims=True))
    route = weights / jnp.sum(weights, axis=-1, keepdims=True)
    mixed = hidden
    grad_route = jnp.zeros_like(route)
    for k, hit_ref in enumerate((hit0_ref, hit1_ref)):
        pair = dot(hit_ref[...], part_ref[...])
        pick = jnp.where(lane == picks_ref[:, k : k + 1], kept_ref[:, k : k + 1], 0.0)
        mixed = mixed + jnp.sum(route * pick, axis=-1, keepdims=True) * pair
        grad_route = grad_route + pick * jnp.sum(grad_out * pair, axis=-1, keepdims=True)
    mixed_ref[...] = mixed.astype(jnp.bfloat16)
    grad_logits = route * (grad_route - jnp.sum(route * grad_route, axis=-1, keepdims=True))
    grad_logits = grad_logits.astype(jnp.bfloat16)
    drouter_ref[...] = contract_first(xn, grad_logits)
    grad_xn = contract_last(grad_logits, router_ref[...]) + dot(hit0_ref[...] + hit1_ref[...], rows_ref[...])
    by_hidden, by_gain = norm_back(hidden, gain_ref[...], grad_xn)
    dgain_ref[...] = by_gain
    grad_hidden = grad_out + by_hidden
    dhidden_ref[...] = grad_hidden
    grad_attn = grad_hidden.astype(jnp.bfloat16)
    dattn_ref[...] = grad_attn
    dheads_ref[...] = contract_last(grad_attn, wout_ref[...]).astype(jnp.bfloat16)
    allowed = allowed_pairs(length_ref[0])
    scale = HEAD_DIM ** (-0.5)
    for pair in range(HEADS // 2):
        outs = [[], [], []]
        for head in (2 * pair, 2 * pair + 1):
            at = head * HEAD_DIM
            query = qkv_ref[:, at : at + HEAD_DIM]
            key = qkv_ref[:, D + at : D + at + HEAD_DIM]
            value = qkv_ref[:, 2 * D + at : 2 * D + at + HEAD_DIM]
            grad_head = dheads_ref[:, at : at + HEAD_DIM]
            scores = contract_last(query, key)
            scores = jnp.where(allowed, scores * scale + bias_ref[head].astype(jnp.float32), -1e30)
            weights = jnp.exp(scores - jnp.max(scores, axis=-1, keepdims=True))
            probs = weights / jnp.sum(weights, axis=-1, keepdims=True)
            grad_probs = contract_last(grad_head, value)
            grad_scores = probs * (grad_probs - jnp.sum(probs * grad_probs, axis=-1, keepdims=True))
            grad_scores = grad_scores.astype(jnp.bfloat16)
            dscores_ref[head] = grad_scores
            outs[0].append(dot(grad_scores, key) * scale)
            outs[1].append(contract_first(grad_scores, query) * scale)
            outs[2].append(contract_first(probs.astype(jnp.bfloat16), grad_head))
        for i in range(3):
            dqkv_ref[:, i * D + pair * 128 : i * D + (pair + 1) * 128] = jnp.concatenate(
                outs[i], axis=1
            ).astype(jnp.bfloat16)


def unwind(
    micro, length, part, rows, hits, picks, kept, hidden, xn_second, cotangent, router_pad, gain_second,
    out_weight, qkv_rows, bias_full, waits
):
    whole = lambda a: pl.BlockSpec(a.shape, lambda i: (0,) * a.ndim)
    gain_row = gain_second.reshape(1, D)
    ins = [part, rows, hits[0], hits[1], picks, kept, hidden, xn_second, cotangent, router_pad, gain_row, out_weight, qkv_rows, bias_full]
    specs = [whole(a) for a in ins]
    specs[8] = pl.BlockSpec((1, SLOT, D), lambda i: (micro, 0, 0))
    out_shape = [
        jax.ShapeDtypeStruct((SLOT, D), jnp.bfloat16),
        jax.ShapeDtypeStruct((SLOT, D), jnp.float32),
        jax.ShapeDtypeStruct((SLOT, D), jnp.bfloat16),
        jax.ShapeDtypeStruct((SLOT, 3 * D), jnp.bfloat16),
        jax.ShapeDtypeStruct((D, 128), jnp.float32),
        jax.ShapeDtypeStruct((1, D), jnp.float32),
        jax.ShapeDtypeStruct((HEADS, SLOT, SLOT), jnp.bfloat16),
    ]
    return pl.pallas_call(
        unwind_kernel,
        grid=(1,),
        in_specs=[SMEM] + specs + [ANY] * len(waits),
        out_specs=[whole(o) for o in out_shape],
        out_shape=out_shape,
        scratch_shapes=[pltpu.VMEM((SLOT, D), jnp.bfloat16)],
        compiler_params=params(),
        cost_estimate=SHORT,
        name="unwind",
    )(length.reshape(1), *ins, *waits)


def weights_kernel(core_ref, xn_ref, dqkv0, dqkv1, heads0, heads1, dattn0, dattn1, *refs):
    xn = [xn_ref[:SLOT], xn_ref[SLOT:]]
    half = refs[0].shape[1]

    def write(which, start, total):
        low = total.astype(jnp.bfloat16)
        for core in range(2):

            @pl.when(core_ref[0] == core)
            def _():
                refs[2 * which][0, :, start : start + D] = low[(1 - core) * half : (2 - core) * half]
                refs[2 * which + 1][0, :, start : start + D] = low[core * half : (core + 1) * half]

    for part in range(3):
        span = slice(part * D, (part + 1) * D)
        write(part // 2, part % 2 * D, contract_first(xn[0], dqkv0[:, span]) + contract_first(xn[1], dqkv1[:, span]))
    write(1, D, contract_first(heads0[...], dattn0[...]) + contract_first(heads1[...], dattn1[...]))


def weight_grads(groups, xn_all, dqkv, heads, dattn):
    depth = D // groups
    column = lambda rows: pl.BlockSpec((rows, depth), lambda i: (0, i))
    whole = lambda a: pl.BlockSpec(a.shape, lambda i: (0,) * a.ndim)
    out = jax.ShapeDtypeStruct((groups, depth // 2, 2 * D), jnp.bfloat16)
    return pl.pallas_call(
        weights_kernel,
        grid=(groups,),
        in_specs=[SMEM, column(MICRO * SLOT)]
        + [whole(a) for a in dqkv]
        + [column(SLOT)] * 2
        + [whole(a) for a in dattn],
        out_specs=[pl.BlockSpec((1, depth // 2, 2 * D), lambda i: (i, 0, 0))] * 4,
        out_shape=[out] * 4,
        compiler_params=params(),
        cost_estimate=SHORT,
        name="weights",
    )(bit_of(lax.axis_index("rep"), 1).reshape(1).astype(jnp.int32), xn_all, *dqkv, *heads, *dattn)


def finish_kernel(tokens_ref, gain_ref, wqkv_ref, dqkv0, dqkv1, dhidden0, dhidden1, out_ref, dgain_ref):
    total = None
    for micro, (dqkv, dhidden) in enumerate(((dqkv0, dhidden0), (dqkv1, dhidden1))):
        grad = contract_last(dqkv[...], wqkv_ref[...])
        by_x, by_gain = norm_back(tokens_ref[micro].astype(jnp.float32), gain_ref[...], grad)
        out_ref[micro] = dhidden[...] + by_x
        total = by_gain if total is None else total + by_gain
    dgain_ref[...] = total


def finish(tokens, gain_first, qkv_weight, dqkv, dhidden):
    return pl.pallas_call(
        finish_kernel,
        in_specs=[VMEM] * 7,
        out_specs=[VMEM] * 2,
        out_shape=[
            jax.ShapeDtypeStruct((MICRO, SLOT, D), jnp.float32),
            jax.ShapeDtypeStruct((1, D), jnp.float32),
        ],
        compiler_params=params(),
        cost_estimate=SHORT,
        name="finish",
    )(tokens, gain_first.reshape(1, D), qkv_weight, *dqkv, *dhidden)


def gather_small(router, gains, rel_bias):
    groups = lax.axis_size("grp")
    flat = jnp.concatenate([router.reshape(-1), gains.reshape(-1), rel_bias.reshape(-1)])
    padded = -(-flat.size // 2048) * 2048
    own = jnp.pad(flat, (0, padded - flat.size)).reshape(-1, 128)
    place = lax.axis_index("grp")
    blocks = [own] + [exchange(own, "grp", m) for m in range(1, groups)]
    rows = []
    for at in range(groups):
        row = blocks[0].astype(jnp.float32)
        for m in range(1, groups):
            row = jnp.where(place ^ m == at, blocks[m].astype(jnp.float32), row)
        rows.append(row.reshape(-1))
    every = jnp.stack(rows)
    a, b = router.size, router.size + gains.size
    return (
        every[:, :a].reshape(-1, router.shape[1]).astype(jnp.bfloat16),
        every[:, a:b].reshape(-1, gains.shape[1]),
        every[:, b : flat.size].reshape(-1, rel_bias.shape[1]),
    )


def per_device(
    tokens,
    w_qkv,
    w_out,
    router,
    gains,
    rel_bias,
    w_gate,
    w_up,
    w_down,
    lengths,
    choices,
    priority,
    cotangent,
):
    groups = lax.axis_size("grp")
    split_count = groups // EXPERTS
    place = lax.axis_index("grp")
    my_expert = place // split_count
    pieces, over_grp = gather_weights(w_qkv, w_out)
    router_weight, gain_full, bias_table = gather_small(router, gains, rel_bias)
    router_pad = jnp.pad(router_weight, ((0, 0), (0, 128 - EXPERTS)))
    bucket_hits = (
        jnp.asarray(bucket_matrix())[:, :, None] == jnp.arange(BUCKETS)[None, None, :]
    ).astype(jnp.bfloat16)
    bias_full = jnp.einsum(
        "hk,ijk->hij", bias_table.astype(jnp.bfloat16), bucket_hits, preferred_element_type=jnp.float32
    ).astype(jnp.bfloat16)

    target = (
        (jnp.arange(groups) // split_count)[:, None] * CAP + jnp.arange(CAP)[None, :]
    ).reshape(-1)
    after = [*over_grp, gain_full]
    routes = []
    for micro in range(MICRO):
        _, kept_mask, slot_index = expert_slots(choices[micro], priority[micro], lengths[micro, 0])
        hits = [(slot_index[:, k, None] == target[None, :]).astype(jnp.bfloat16) for k in range(2)]
        spots = (
            (target[:, None] == slot_index[None, :, 0]) | (target[:, None] == slot_index[None, :, 1])
        ).astype(jnp.bfloat16)
        (sent,) = tie([cotangent[micro]], *after)
        blocks = dot(spots, sent).astype(jnp.bfloat16).reshape(groups, CAP, D)
        grad_rows = to_experts(blocks)
        after = [pieces[-1][2], pieces[len(pieces) // 2 - 1][2]]
        routes.append((kept_mask, hits, spots.reshape(groups, CAP, SLOT), grad_rows))

    xn_all, *qkv_all, out_weight = project(tokens, gain_full[:, 0], pieces, [routes[0][-1], bias_full, router_pad])
    forward = []
    for micro in range(MICRO):
        waits = [routes[1][-1], forward[0][0]] if micro else []
        forward.append(
            attend(
                micro, lengths[micro], qkv_all[micro], tokens, bias_full, out_weight, gain_full[:, 1],
                routes[micro][2], waits,
            )
        )
    rows0 = to_experts(forward[0][3])
    qkv_weight = join_qkv(pieces, [forward[1][0]])
    blocks1, _ = tie([forward[1][3], rows0], qkv_weight)
    rows = [rows0, to_experts(blocks1)]

    def expert(micro, waits):
        return run_expert(
            my_expert, rows[micro], routes[micro][-1], router_pad, w_gate, w_up, w_down, waits
        )

    def back_rows(micro, *after):
        return back_to_rows(groups, inner[micro][2], inner[micro][3], w_gate, w_up, after)

    inner = [expert(0, [qkv_weight])]
    part0 = to_experts(inner[0][4])
    back0 = back_rows(0)
    inner.append(expert(1, [back0]))
    drows0 = to_experts(tie([back0], part0)[0])
    doutput, act, dgate, dup = ([inner[micro][i] for micro in range(MICRO)] for i in range(4))

    def launch(left, right, waits):
        (theirs,) = products(left, right, None, waits)
        return theirs, exchange(theirs, "rep", 1)

    def settle(left, right, arrived, waits):
        outs = products(left, right, arrived, waits)
        pair = [Halving(w, 0) for w in range(2)]
        for w in range(2):
            pair[w].start(outs[2 * w], outs[2 * w + 1], 1)
        return pair, outs[1]

    tok, down_came = launch(act, doutput, [part0])
    tok, gate_came = launch(rows, dgate, [tok])
    down, tok = settle(act, doutput, down_came, [tok])
    tok, up_came = launch(rows, dup, [tok])
    part1 = to_experts(tie([inner[1][4]], drows0)[0])
    gate, tok = settle(rows, dgate, gate_came, [tok, drows0])
    up, tok = settle(rows, dup, up_came, [tok])
    back1 = back_rows(1, tok)
    tok = [h.halve(2, back1) for h in down]
    tok = [h.halve(2, *tok) for h in gate]

    def unwound(micro, part, drows, waits):
        kept_mask, hits, _, _ = routes[micro]
        heads, hidden, xn_second, _ = forward[micro]
        return unwind(
            micro, lengths[micro], part, drows, hits, choices[micro], kept_mask, hidden, xn_second, cotangent,
            router_pad, gain_full[:, 1], out_weight, qkv_all[micro], bias_full, waits,
        )

    un0 = unwound(0, part0, drows0, [*tok, part1])
    drows1 = to_experts(tie([back1], part1)[0])
    for half in down:
        half.back(half.own(un0[0]))
    tok = [h.halve(2, *[d.kept for d in down]) for h in up]
    for half in gate:
        half.back(half.own(*tok))
    tok = [h.back_pair(*[g.kept for g in gate]) for h in down]
    un1 = unwound(1, part1, drows1, tok)
    un = (un0, un1)
    grads = weight_grads(
        groups, xn_all, [u[3] for u in un], [forward[m][0] for m in range(MICRO)], [u[2] for u in un]
    )
    attn = [Halving(w, 1) for w in range(2)]
    for w in range(2):
        attn[w].start(grads[2 * w], grads[2 * w + 1], 0)
    for half in up:
        half.back(half.own(grads[0]))
    tok = [h.back_pair(*[u.kept for u in up]) for h in gate]
    tok = [h.halve(1, *tok) for h in attn]
    tok = [h.back_rest(*tok) for h in down]
    token_grads, dgain_first = finish(
        tie([tokens], *tok)[0], gain_full[:, 0], qkv_weight, [u[3] for u in un], [u[1] for u in un]
    )
    dscores = tie([u[6] for u in un], token_grads)
    bias_grad = sum(
        jnp.einsum("hij,ijk->hk", d, bucket_hits, preferred_element_type=jnp.float32) for d in dscores
    )
    small = [
        (un0[4] + un1[4])[:, :EXPERTS].reshape(-1),
        jnp.stack([dgain_first[0], un0[5][0] + un1[5][0]], axis=1).reshape(-1),
        bias_grad.reshape(-1),
    ]
    flat = jnp.concatenate(small)
    flat = jnp.pad(flat, (0, -flat.size % 1024)).reshape(-1, 128)
    tok = [h.back_pair(flat) for h in up]
    tok = [h.halve(2, *tok) for h in attn]
    steps = [("grp", m) for m in masks_of(groups)] + [("rep", m) for m in masks_of(lax.axis_size("rep"))]
    flat = tie([flat], *tok)[0]
    for axis, mask in steps[:2]:
        flat = flat + exchange(flat, axis, mask)
    tok = [h.back_rest(flat) for h in gate]
    down_grad = assemble(down)
    reduced = []
    for half in attn:
        block = half.own(*tok, down_grad)
        total = lax.dynamic_index_in_dim(block, place, 0, keepdims=False).astype(jnp.float32)
        reduced.append((half, block, total))
    sums = []
    for half, block, total in reduced:
        for m in range(1, groups):
            total = total + exchange(
                lax.dynamic_index_in_dim(block, place ^ m, 0, keepdims=False), "grp", m
            ).astype(jnp.float32)
        sums.append(total.astype(jnp.bfloat16))
    for axis, mask in steps[2:]:
        flat = flat + exchange(flat, axis, mask)
    tok = [h.back_rest(*tok) for h in up]
    gate_grad = assemble(gate)
    sums = tie(sums, *tok)
    for half, total in zip(attn, sums):
        half.back(total)
    tok = [h.back_pair(gate_grad) for h in attn]
    up_grad = assemble(up)
    tok = [h.back_rest(up_grad) for h in attn]
    qkv_grad, out_grad = assemble_attention(attn)

    flat = flat.reshape(-1)
    outs = []
    start = 0
    for whole in ((D, EXPERTS), (D, 2), (HEADS, BUCKETS)):
        size = whole[0] * whole[1]
        rows_here = whole[0] // groups
        outs.append(
            lax.dynamic_slice_in_dim(
                flat[start : start + size].reshape(whole), place * rows_here, rows_here, 0
            )
        )
        start += size
    return (
        jnp.stack([u[0] for u in un]),
        token_grads,
        qkv_grad,
        out_grad,
        outs[0],
        outs[1],
        outs[2],
        gate_grad[None],
        up_grad[None],
        down_grad[None],
    )


def solution(mesh):
    placed = (
        P(None, ("rep", "grp"), None),
        P("grp", None),
        P("grp", None),
        P("grp", None),
        P("grp", None),
        P("grp", None),
        P("grp", None, None),
        P("grp", None, None),
        P("grp", None, None),
        P(None, ("rep", "grp")),
        P(None, ("rep", "grp"), None),
        P(None, ("rep", "grp")),
        P(None, ("rep", "grp"), None),
    )
    return jax.shard_map(
        per_device,
        mesh=mesh,
        in_specs=placed,
        out_specs=(
            P(None, ("rep", "grp"), None),
            P(None, ("rep", "grp"), None),
            P("grp", None),
            P("grp", None),
            P("grp", None),
            P("grp", None),
            P("grp", None),
            P("grp", None, None),
            P("grp", None, None),
            P("grp", None, None),
        ),
        check_vma=False,
    )
```

```python
import functools

import jax
import jax.numpy as jnp
import numpy as np
from jax import lax
from jax.experimental import pallas as pl
from jax.experimental.pallas import tpu as pltpu
from jax.sharding import PartitionSpec as P

D = 1024
HEADS = 16
HEAD_DIM = 64
EXPERTS = 4
BUCKETS = 32
MAX_DIST = 128
MICRO = 2
SLOT = 192
CAP = 120
VMEM_LIMIT = 56 * 1024 * 1024
PART = 0.001


def lasts(us):
    return pl.CostEstimate(flops=int(us * PART * 1.15e9), bytes_accessed=1, transcendentals=0)


VMEM = pl.BlockSpec(memory_space=pltpu.VMEM)
SMEM = pl.BlockSpec(memory_space=pltpu.SMEM)
ANY = pl.BlockSpec(memory_space=pl.ANY)


def params():
    return pltpu.CompilerParams(vmem_limit_bytes=VMEM_LIMIT)


def bucket_matrix():
    distance = np.arange(SLOT)
    exact_count = BUCKETS // 2
    safe_span = np.maximum(distance, 1) / exact_count
    log_bucket = exact_count + np.floor(
        np.log(safe_span) / np.log(MAX_DIST / exact_count) * (BUCKETS - exact_count)
    ).astype(np.int32)
    bucket_of = np.where(distance < exact_count, distance, np.minimum(log_bucket, BUCKETS - 1))
    offsets = np.maximum(distance[:, None] - distance[None, :], 0)
    return bucket_of[offsets].astype(np.int32)


def dot(left, right):
    return jnp.dot(left, right, preferred_element_type=jnp.float32)


def contract_last(left, right):
    return lax.dot_general(
        left, right, (((1,), (1,)), ((), ())), preferred_element_type=jnp.float32
    )


def contract_first(left, right):
    return lax.dot_general(
        left, right, (((0,), (0,)), ((), ())), preferred_element_type=jnp.float32
    )


def expert_slots(expert_pick, priority_row, length):
    live_mask = (jnp.arange(SLOT) < length).astype(jnp.float32)
    pick_hits = (expert_pick[:, :, None] == jnp.arange(EXPERTS)[None, None, :]).astype(jnp.float32)
    expert_hits = jnp.sum(pick_hits, axis=1) * live_mask[:, None]
    before = (priority_row[None, :] < priority_row[:, None]).astype(jnp.bfloat16)
    ahead_count = dot(before, expert_hits.astype(jnp.bfloat16))
    place_pos = jnp.sum(pick_hits * ahead_count[:, None, :], axis=2)
    kept_mask = live_mask[:, None] * (place_pos < CAP - 0.5).astype(jnp.float32)
    slot_index = jnp.where(
        kept_mask > 0.5, expert_pick * CAP + place_pos.astype(jnp.int32), EXPERTS * CAP
    )
    return (pick_hits, kept_mask, slot_index)


def exchange(block, axis, mask):
    return lax.ppermute(block, axis, [(i, i ^ mask) for i in range(lax.axis_size(axis))])


def masks_of(count):
    return [1 << bit for bit in range(count.bit_length() - 1)]


def spread(own, axis, masks):
    held = [(0, own)]
    for mask in masks:
        held += [(far ^ mask, exchange(block, axis, mask)) for far, block in held]
    return held


def to_experts(blocks):
    return lax.all_to_all(blocks, "grp", split_axis=0, concat_axis=0, tiled=True)


def bit_of(index, mask):
    return (index & mask) // mask


def tie(values, *after):
    return lax.optimization_barrier((tuple(values), after))[0]


def rep_masks():
    masks = masks_of(lax.axis_size("rep"))
    return masks[3:], masks[:3]


def order_of(which):
    masks = rep_masks()[1]
    return masks[:1] + (masks[1:] if which == 0 else masks[:0:-1])


def halves_of(block, mask, dim):
    half = block.shape[dim] // 2
    bit = bit_of(lax.axis_index("rep"), mask)
    return (
        lax.dynamic_slice_in_dim(block, (1 - bit) * half, half, dim),
        lax.dynamic_slice_in_dim(block, bit * half, half, dim),
    )


def add_low(left, right):
    return (left.astype(jnp.float32) + right.astype(jnp.float32)).astype(jnp.bfloat16)


class Halving:
    def __init__(self, which, dim):
        self.which, self.dim = which, dim
        self.masks = order_of(which)
        self.kept = self.moving = None
        self.held = None

    def start(self, send, keep, at):
        self.kept, self.moving = keep, exchange(send, "rep", self.masks[at])

    def halve(self, at):
        kept, got = (halves_of(x, self.masks[at], self.dim) for x in (self.kept, self.moving))
        self.start(*(add_low(k, g) for k, g in zip(kept, got)), at)

    def own(self):
        total = add_low(self.kept, self.moving)
        for mask in rep_masks()[0]:
            total = add_low(total, exchange(total, "rep", mask))
        self.kept, self.moving = total, None

    def back(self):
        self.moving = exchange(self.kept, "rep", self.masks[-1])

    def back_pair(self):
        self.kept = jnp.stack([self.kept, self.moving])
        self.moving = exchange(self.kept, "rep", self.masks[-2])

    def place(self):
        index = 0
        for mask in self.masks:
            index = 2 * index + bit_of(lax.axis_index("rep"), mask)
        return index


def land(halvings, *after):
    flat = [x for h in halvings for x in (h.kept, h.moving) if x is not None]
    flat = list(tie(flat, *after))
    for h in halvings:
        h.kept = flat.pop(0)
        if h.moving is not None:
            h.moving = flat.pop(0)


def swap_cores(pair):
    own = jnp.concatenate([x for h in pair for x in (h.kept, h.moving)], axis=0)
    return own, exchange(own, "rep", 1)


def assemble(pair_of_halves, own, got):
    places = jnp.stack([half.place() for half in pair_of_halves]).astype(jnp.int32)
    pieces, rows, cols = own.shape
    deep = pieces // 4
    cut_cores = cols % 128 != 0

    def body(place_ref, own_ref, got_ref, out_ref):
        half, core, step = (pl.program_id(i) for i in range(3))
        place = place_ref[half]
        far = (core * deep + step) ^ (place // 2)
        at = 2 * (half * deep + far % deep)
        out = out_ref.at[0] if cut_cores else out_ref
        for other, ref in enumerate((own_ref, got_ref)):

            @pl.when(far // deep == other)
            def _():
                out[:rows] = ref[at + place % 2].astype(jnp.float32)
                out[rows:] = ref[at + 1 - place % 2].astype(jnp.float32)

    whole = pl.BlockSpec((pieces, rows, cols), lambda half, core, step, place_ref: (0, 0, 0))
    out_shape = (4 * deep * rows, 2 * cols)
    out_spec = pl.BlockSpec(
        (2 * rows, cols), lambda half, core, step, place_ref: (half * deep + step, core)
    )
    if cut_cores:
        out_shape = (2, 4 * deep * rows, cols)
        out_spec = pl.BlockSpec(
            (1, 2 * rows, cols), lambda half, core, step, place_ref: (core, half * deep + step, 0)
        )
    out = pl.pallas_call(
        body,
        grid_spec=pltpu.PrefetchScalarGridSpec(
            num_scalar_prefetch=1,
            grid=(2, 2, deep),
            in_specs=[whole] * 2,
            out_specs=out_spec,
        ),
        out_shape=jax.ShapeDtypeStruct(out_shape, jnp.float32),
        compiler_params=params(),
        cost_estimate=lasts(9),
        name="assemble",
    )(places, own, got)
    return jnp.concatenate([out[0], out[1]], axis=1) if cut_cores else out


def assemble_attention(pair_of_halves, own, got):
    places = jnp.stack([half.place() for half in pair_of_halves]).astype(jnp.int32)
    pieces, rows, _ = own.shape
    each = pieces // 2

    def body(place_ref, own_ref, got_ref, qkv_ref, out_ref):
        for other, ref in enumerate((own_ref, got_ref)):
            for at in range(pieces):
                where = (other * each + at % each) ^ place_ref[at // each]
                span = pl.ds(pl.multiple_of(where * rows, rows), rows)
                values = ref[at].astype(jnp.float32)
                if at < each:
                    qkv_ref[span, : 2 * D] = values
                else:
                    qkv_ref[span, 2 * D :] = values[:, :D]
                    out_ref[span, :] = values[:, D:]

    depth = 2 * each * rows
    return pl.pallas_call(
        body,
        in_specs=[SMEM] + [VMEM] * 2,
        out_specs=[VMEM] * 2,
        out_shape=[
            jax.ShapeDtypeStruct((depth, 3 * D), jnp.float32),
            jax.ShapeDtypeStruct((depth, D), jnp.float32),
        ],
        compiler_params=params(),
        cost_estimate=lasts(4),
        name="assemble_attention",
    )(places, own, got)


def gather_weights(w_qkv, w_out, small):
    slices = min(lax.axis_size("rep"), 8)
    eighth = lax.axis_index("rep") % slices
    width = D // slices
    parts = [w_qkv[:, i * D : (i + 1) * D] for i in range(3)] + [w_out]
    own = jnp.concatenate(
        [lax.dynamic_slice_in_dim(part, eighth * width, width, 1) for part in parts], axis=1
    )
    depth = own.shape[0]
    small = small.reshape(-1)
    lines = -(-small.size // (16 * own.shape[1])) * 16
    small = jnp.pad(small, (0, lines * own.shape[1] - small.size)).reshape(lines, -1)
    masks = masks_of(slices)
    held = spread(jnp.concatenate([own, small]), "grp", masks_of(lax.axis_size("grp"))[::-1])
    over_grp = [(m, block[:depth]) for m, block in held]
    half = len(over_grp) // 2
    chains = []
    for which in range(2):
        mine = over_grp[which * half : (which + 1) * half]
        order = masks[1:] if which == 0 else masks[:0:-1]
        block = jnp.stack([piece for _, piece in mine])
        chains.append(([m for m, _ in mine], spread(block, "rep", order)))
    return chains, {m: block[depth:].reshape(-1) for m, block in held}


def gather_cores(chains, *after):
    pieces = []
    for members, held in chains:
        blocks = tie([block for _, block in held], *after)
        for (far, _), block in zip(held, blocks):
            pieces += [(far, members, block), (far ^ 1, members, exchange(block, "rep", 1))]
    return pieces


def norm_rows(x, gain):
    return x * lax.rsqrt(jnp.mean(x * x, axis=-1, keepdims=True) + 1e-06) * gain


def each_piece(plan, pieces, far):
    for (this, members), piece in zip(plan, pieces):
        if this == far:
            yield from ((m, piece, at) for at, m in enumerate(members))


def project_kernel(plan, place_ref, tokens_ref, gain_ref, *refs):
    count = len(plan)
    pieces = refs[:count]
    xn_ref, qkv0_ref, qkv1_ref, wout_ref = refs[-4:]
    depth = pieces[0].shape[1]
    width = pieces[0].shape[2] // 4
    for micro in range(MICRO):
        xn_ref[micro * SLOT : (micro + 1) * SLOT] = norm_rows(
            tokens_ref[micro].astype(jnp.float32), gain_ref[...]
        ).astype(jnp.bfloat16)
    for far in sorted({far for far, _ in plan}):
        column = pl.multiple_of((place_ref[0] ^ far) * width, width)
        total = None
        for m, piece, at in each_piece(plan, pieces, far):
            row = pl.multiple_of((place_ref[1] ^ m) * depth, depth)
            wout_ref[pl.ds(row, depth), pl.ds(column, width)] = piece[at, :, 3 * width :]
            term = dot(xn_ref[:, pl.ds(row, depth)], piece[at, :, : 3 * width])
            total = term if total is None else total + term
        for part in range(3):
            low = total[:, part * width : (part + 1) * width].astype(jnp.bfloat16)
            qkv0_ref[:, pl.ds(column + part * D, width)] = low[:SLOT]
            qkv1_ref[:, pl.ds(column + part * D, width)] = low[SLOT:]


def places_of():
    slices = min(lax.axis_size("rep"), 8)
    return jnp.stack([lax.axis_index("rep") % slices, lax.axis_index("grp")]).astype(jnp.int32)


def project(tokens, gain_first, pieces, waits):
    plan = [(far, m) for far, m, _ in pieces]
    return pl.pallas_call(
        functools.partial(project_kernel, plan),
        in_specs=[SMEM] + [VMEM] * (2 + len(pieces)) + [ANY] * len(waits),
        out_specs=[VMEM] * 4,
        out_shape=[
            jax.ShapeDtypeStruct((MICRO * SLOT, D), jnp.bfloat16),
            jax.ShapeDtypeStruct((SLOT, 3 * D), jnp.bfloat16),
            jax.ShapeDtypeStruct((SLOT, 3 * D), jnp.bfloat16),
            jax.ShapeDtypeStruct((D, D), jnp.bfloat16),
        ],
        compiler_params=params(),
        cost_estimate=lasts(10),
        name="project",
    )(places_of(), tokens, gain_first.reshape(1, D), *[piece for _, _, piece in pieces], *waits)


def join_kernel(plan, place_ref, *refs):
    pieces, out_ref = refs[: len(plan)], refs[-1]
    depth = pieces[0].shape[1]
    width = pieces[0].shape[2] // 4
    for far in sorted({far for far, _ in plan}):
        column = pl.multiple_of((place_ref[0] ^ far) * width, width)
        for m, piece, at in each_piece(plan, pieces, far):
            row = pl.multiple_of((place_ref[1] ^ m) * depth, depth)
            for part in range(3):
                out_ref[pl.ds(row, depth), pl.ds(column + part * D, width)] = piece[
                    at, :, part * width : (part + 1) * width
                ]


def join_qkv(pieces, waits):
    plan = [(far, m) for far, m, _ in pieces]
    return pl.pallas_call(
        functools.partial(join_kernel, plan),
        in_specs=[SMEM] + [VMEM] * len(pieces) + [ANY] * len(waits),
        out_specs=VMEM,
        out_shape=jax.ShapeDtypeStruct((D, 3 * D), jnp.bfloat16),
        compiler_params=params(),
        cost_estimate=lasts(8),
        name="join",
    )(places_of(), *[piece for _, _, piece in pieces], *waits)


def allowed_pairs(length):
    row = lax.broadcasted_iota(jnp.int32, (SLOT, SLOT), 0)
    column = lax.broadcasted_iota(jnp.int32, (SLOT, SLOT), 1)
    return (column <= row) & (column < length)


def attend_kernel(groups, length_ref, qkv_ref, tokens_ref, bias_ref, wout_ref, gain_ref, spots_ref, *refs):
    heads_ref, hidden_ref, xn_ref, rows_ref = refs[-4:]
    allowed = allowed_pairs(length_ref[0])
    scale = HEAD_DIM ** (-0.5)
    for pair in range(HEADS // 2):
        outs = []
        for head in (2 * pair, 2 * pair + 1):
            at = head * HEAD_DIM
            scores = contract_last(
                qkv_ref[:, at : at + HEAD_DIM], qkv_ref[:, D + at : D + at + HEAD_DIM]
            )
            scores = jnp.where(allowed, scores * scale + bias_ref[head].astype(jnp.float32), -1e30)
            weights = jnp.exp(scores - jnp.max(scores, axis=-1, keepdims=True))
            probs = weights / jnp.sum(weights, axis=-1, keepdims=True)
            outs.append(
                dot(probs.astype(jnp.bfloat16), qkv_ref[:, 2 * D + at : 2 * D + at + HEAD_DIM])
            )
        heads_ref[:, pair * 128 : (pair + 1) * 128] = jnp.concatenate(outs, axis=1).astype(jnp.bfloat16)
    hidden = tokens_ref[0].astype(jnp.float32) + dot(heads_ref[...], wout_ref[...])
    hidden_ref[...] = hidden
    xn = norm_rows(hidden, gain_ref[...]).astype(jnp.bfloat16)
    xn_ref[...] = xn
    for m in range(groups):
        rows_ref[m] = dot(spots_ref[m], xn).astype(jnp.bfloat16)


def attend(micro, length, qkv_rows, tokens, bias_full, out_weight, gain_second, spots, waits):
    groups = spots.shape[0]
    whole = lambda *shape: pl.BlockSpec(shape, lambda i: (0,) * len(shape))
    low = jax.ShapeDtypeStruct((SLOT, D), jnp.bfloat16)
    out_shape = [
        low,
        jax.ShapeDtypeStruct((SLOT, D), jnp.float32),
        low,
        jax.ShapeDtypeStruct((groups, CAP, D), jnp.bfloat16),
    ]
    return pl.pallas_call(
        functools.partial(attend_kernel, groups),
        grid=(1,),
        in_specs=[
            SMEM,
            whole(SLOT, 3 * D),
            pl.BlockSpec((1, SLOT, D), lambda i: (micro, 0, 0)),
            whole(HEADS, SLOT, SLOT),
            whole(D, D),
            whole(1, D),
            whole(groups, CAP, SLOT),
        ]
        + [ANY] * len(waits),
        out_specs=[whole(*o.shape) for o in out_shape],
        out_shape=out_shape,
        compiler_params=params(),
        cost_estimate=lasts(9.3),
        name="attend",
    )(length.reshape(1), qkv_rows, tokens, bias_full, out_weight, gain_second.reshape(1, D), spots, *waits)


def gelu_parts(v):
    c = np.float32(np.sqrt(2 / np.pi))
    t = jnp.tanh(c * (v + np.float32(0.044715) * (v * v * v)))
    half = 0.5 * (1.0 + t)
    slope = half + 0.5 * v * (1.0 - t * t) * (c * (1.0 + np.float32(3 * 0.044715) * (v * v)))
    return v * half, slope


def expert_kernel(groups, chunk, expert_ref, rows_ref, grads_ref, router_ref, wg_hbm, wu_hbm, wd_hbm, *refs):
    dout_ref, act_hbm, dgate_hbm, dup_hbm, back_ref = refs[-13:-8]
    wg, wu, wd, act, dgate, dup, came, went = refs[-8:]
    hidden = act.shape[1]
    steps = hidden // chunk

    def incoming(c):
        span = pl.ds(pl.multiple_of(c * chunk, chunk), chunk)
        return [
            pltpu.make_async_copy(wg_hbm.at[0, :, span], wg.at[:, span], came.at[0, c]),
            pltpu.make_async_copy(wu_hbm.at[0, :, span], wu.at[:, span], came.at[1, c]),
            pltpu.make_async_copy(wd_hbm.at[0, span, :], wd.at[span, :], came.at[2, c]),
        ]

    def outgoing(c):
        span = pl.ds(pl.multiple_of(c * chunk, chunk), chunk)
        return [
            pltpu.make_async_copy(vmem.at[:, span], hbm.at[:, span], went.at[i, c])
            for i, (vmem, hbm) in enumerate(((act, act_hbm), (dgate, dgate_hbm), (dup, dup_hbm)))
        ]

    @pl.loop(0, steps)
    def _(c):
        for copy in incoming(c):
            copy.start()

    logits = dot(rows_ref[...], router_ref[...])
    lane = lax.broadcasted_iota(jnp.int32, logits.shape, 1)
    logits = jnp.where(lane < EXPERTS, logits, -1e30)
    weights = jnp.exp(logits - jnp.max(logits, axis=-1, keepdims=True))
    route = weights / jnp.sum(weights, axis=-1, keepdims=True)
    gate = jnp.sum(jnp.where(lane == expert_ref[0], route, 0.0), axis=-1, keepdims=True)
    dout_ref[...] = (gate * grads_ref[...].astype(jnp.float32)).astype(jnp.bfloat16)

    @pl.loop(0, steps)
    def _(c):
        span = pl.ds(pl.multiple_of(c * chunk, chunk), chunk)
        for copy in incoming(c):
            copy.wait()
        gate_pre = dot(rows_ref[...], wg[:, span])
        up_pre = dot(rows_ref[...], wu[:, span])
        gelu, slope = gelu_parts(gate_pre)
        act[:, span] = (gelu * up_pre).astype(jnp.bfloat16)
        grad_act = contract_last(dout_ref[...], wd[span, :])
        dgate[:, span] = (grad_act * up_pre * slope).astype(jnp.bfloat16)
        dup[:, span] = (grad_act * gelu).astype(jnp.bfloat16)
        for copy in outgoing(c):
            copy.start()

    part = dot(act[...], wd[...])
    for m in range(groups):
        back_ref[m, 0] = part[m * CAP : (m + 1) * CAP].astype(jnp.bfloat16)
    grad_rows = contract_last(dgate[...], wg[...]) + contract_last(dup[...], wu[...])
    for m in range(groups):
        back_ref[m, 1] = grad_rows[m * CAP : (m + 1) * CAP].astype(jnp.bfloat16)

    @pl.loop(0, steps)
    def _(c):
        for copy in outgoing(c):
            copy.wait()


def run_expert(expert, rows, grad_rows, router_pad, w_gate, w_up, w_down, waits):
    count = rows.shape[0]
    groups = count // CAP
    hidden = w_gate.shape[2]
    chunk = 256 if hidden % 256 == 0 else 128
    steps = hidden // chunk
    wide = jax.ShapeDtypeStruct((count, hidden), jnp.bfloat16)
    low = lambda *shape: pltpu.VMEM(shape, jnp.bfloat16)
    return pl.pallas_call(
        functools.partial(expert_kernel, groups, chunk),
        in_specs=[SMEM] + [VMEM] * 3 + [ANY] * (3 + len(waits)),
        out_specs=[VMEM] + [ANY] * 3 + [VMEM],
        out_shape=[
            jax.ShapeDtypeStruct((count, D), jnp.bfloat16),
            wide,
            wide,
            wide,
            jax.ShapeDtypeStruct((groups, 2, CAP, D), jnp.bfloat16),
        ],
        scratch_shapes=[
            low(D, hidden),
            low(D, hidden),
            low(hidden, D),
            low(count, hidden),
            low(count, hidden),
            low(count, hidden),
            pltpu.SemaphoreType.DMA((3, steps)),
            pltpu.SemaphoreType.DMA((3, steps)),
        ],
        compiler_params=params(),
        cost_estimate=lasts(22),
        name="expert",
    )(jnp.reshape(expert, (1,)).astype(jnp.int32), rows, grad_rows, router_pad, w_gate, w_up, w_down, *waits)


def products_kernel(wide, bits_ref, left0, left1, right0, right1, *refs):
    total = contract_first(left0[...], right0[...]) + contract_first(left1[...], right1[...])
    for which in range(2):

        @pl.when(pl.program_id(0) == which)
        def _():
            if not wide:
                refs[which - 2][...] = total.astype(jnp.bfloat16)
                return
            total_ref = refs[-1]
            total_ref[...] = (total + refs[which][...].astype(jnp.float32)).astype(jnp.bfloat16)
            send_ref, keep_ref = refs[-5 + 2 * which : len(refs) - 3 + 2 * which]
            bit = bits_ref[1 + which]
            half = send_ref.shape[0]
            keep_ref[...] = total_ref[pl.ds(pl.multiple_of(bit * half, half), half)]
            send_ref[...] = total_ref[pl.ds(pl.multiple_of((1 - bit) * half, half), half)]


def products(left, right, arrived=None, waits=()):
    place = lax.axis_index("rep")
    wide = arrived is not None
    core = bit_of(place, 1)
    bits = jnp.stack(
        [core if wide else 1 - core] + [bit_of(place, order_of(w)[1]) for w in range(2)]
    ).astype(jnp.int32)
    count = left[0].shape[0]
    rows, cols = left[0].shape[1] // 2, right[0].shape[1] // 2
    if rows % 128 or cols % 128:
        return products_plain(left, right, arrived)
    deep, number = (rows // 2, 4) if wide else (rows, 2)
    return pl.pallas_call(
        functools.partial(products_kernel, wide),
        grid_spec=pltpu.PrefetchScalarGridSpec(
            num_scalar_prefetch=1,
            grid=(2,),
            in_specs=[pl.BlockSpec((count, rows), lambda h, b: (0, h))] * 2
            + [pl.BlockSpec((count, cols), lambda h, b: (0, b[0]))] * 2
            + ([pl.BlockSpec((rows, cols), lambda h, b: (0, 0))] * 2 if wide else [])
            + [ANY] * len(waits),
            out_specs=[pl.BlockSpec((deep, cols), lambda h, b: (0, 0))] * number,
            scratch_shapes=[pltpu.VMEM((rows, cols), jnp.bfloat16)] if wide else [],
        ),
        out_shape=[jax.ShapeDtypeStruct((deep, cols), jnp.bfloat16)] * number,
        compiler_params=params(),
        cost_estimate=lasts(8),
        name="products",
    )(bits, *left, *right, *(arrived if wide else []), *waits)


def products_plain(left, right, arrived):
    total = contract_first(left[0], right[0]) + contract_first(left[1], right[1])
    theirs, mine = halves_of(total, 1, 1)
    if arrived is None:
        return jnp.split(theirs.astype(jnp.bfloat16), 2, axis=0)
    mine = [
        (m + a.astype(jnp.float32)).astype(jnp.bfloat16)
        for m, a in zip(jnp.split(mine, 2, axis=0), arrived)
    ]
    return [cut for w in range(2) for cut in halves_of(mine[w], order_of(w)[1], 0)]


def norm_back(x, gain, grad):
    scale = lax.rsqrt(jnp.mean(x * x, axis=-1, keepdims=True) + 1e-06)
    plain = x * scale
    inner = grad * gain
    by_x = scale * (inner - plain * jnp.mean(inner * plain, axis=-1, keepdims=True))
    return by_x, jnp.sum(grad * plain, axis=0, keepdims=True)


def unwind_kernel(
    length_ref, back_ref, hit0_ref, hit1_ref, picks_ref, kept_ref, hidden_ref, xn_ref, cot_ref,
    router_ref, gain_ref, wout_ref, qkv_ref, bias_ref, *refs
):
    mixed_ref, dhidden_ref, dattn_ref, dqkv_ref, drouter_ref, dgain_ref, dscores_ref, dheads_ref = refs[-8:]
    xn = xn_ref[...]
    hidden = hidden_ref[...]
    grad_out = cot_ref[0].astype(jnp.float32)
    logits = dot(xn, router_ref[...])
    lane = lax.broadcasted_iota(jnp.int32, logits.shape, 1)
    logits = jnp.where(lane < EXPERTS, logits, -1e30)
    weights = jnp.exp(logits - jnp.max(logits, axis=-1, keepdims=True))
    route = weights / jnp.sum(weights, axis=-1, keepdims=True)
    mixed = hidden
    grad_route = jnp.zeros_like(route)
    for k, hit_ref in enumerate((hit0_ref, hit1_ref)):
        pair = sum(dot(hit_ref[m], back_ref[m, 0]) for m in range(back_ref.shape[0]))
        pick = jnp.where(lane == picks_ref[:, k : k + 1], kept_ref[:, k : k + 1], 0.0)
        mixed = mixed + jnp.sum(route * pick, axis=-1, keepdims=True) * pair
        grad_route = grad_route + pick * jnp.sum(grad_out * pair, axis=-1, keepdims=True)
    mixed_ref[...] = mixed.astype(jnp.bfloat16)
    grad_logits = route * (grad_route - jnp.sum(route * grad_route, axis=-1, keepdims=True))
    grad_logits = grad_logits.astype(jnp.bfloat16)
    drouter_ref[...] = contract_first(xn, grad_logits)
    grad_xn = contract_last(grad_logits, router_ref[...]) + sum(
        dot(hit0_ref[m] + hit1_ref[m], back_ref[m, 1]) for m in range(back_ref.shape[0])
    )
    by_hidden, by_gain = norm_back(hidden, gain_ref[...], grad_xn)
    dgain_ref[...] = by_gain
    grad_hidden = grad_out + by_hidden
    dhidden_ref[...] = grad_hidden
    grad_attn = grad_hidden.astype(jnp.bfloat16)
    dattn_ref[...] = grad_attn
    dheads_ref[...] = contract_last(grad_attn, wout_ref[...]).astype(jnp.bfloat16)
    allowed = allowed_pairs(length_ref[0])
    scale = HEAD_DIM ** (-0.5)
    for pair in range(HEADS // 2):
        outs = [[], [], []]
        for head in (2 * pair, 2 * pair + 1):
            at = head * HEAD_DIM
            query = qkv_ref[:, at : at + HEAD_DIM]
            key = qkv_ref[:, D + at : D + at + HEAD_DIM]
            value = qkv_ref[:, 2 * D + at : 2 * D + at + HEAD_DIM]
            grad_head = dheads_ref[:, at : at + HEAD_DIM]
            scores = contract_last(query, key)
            scores = jnp.where(allowed, scores * scale + bias_ref[head].astype(jnp.float32), -1e30)
            weights = jnp.exp(scores - jnp.max(scores, axis=-1, keepdims=True))
            probs = weights / jnp.sum(weights, axis=-1, keepdims=True)
            grad_probs = contract_last(grad_head, value)
            grad_scores = probs * (grad_probs - jnp.sum(probs * grad_probs, axis=-1, keepdims=True))
            grad_scores = grad_scores.astype(jnp.bfloat16)
            dscores_ref[head] = grad_scores
            outs[0].append(dot(grad_scores, key) * scale)
            outs[1].append(contract_first(grad_scores, query) * scale)
            outs[2].append(contract_first(probs.astype(jnp.bfloat16), grad_head))
        for i in range(3):
            dqkv_ref[:, i * D + pair * 128 : i * D + (pair + 1) * 128] = jnp.concatenate(
                outs[i], axis=1
            ).astype(jnp.bfloat16)


def unwind(
    micro, length, back, hits, picks, kept, hidden, xn_second, cotangent, router_pad, gain_second,
    out_weight, qkv_rows, bias_full, waits
):
    whole = lambda a: pl.BlockSpec(a.shape, lambda i: (0,) * a.ndim)
    gain_row = gain_second.reshape(1, D)
    ins = [back, hits[0], hits[1], picks, kept, hidden, xn_second, cotangent, router_pad, gain_row, out_weight, qkv_rows, bias_full]
    specs = [whole(a) for a in ins]
    specs[7] = pl.BlockSpec((1, SLOT, D), lambda i: (micro, 0, 0))
    out_shape = [
        jax.ShapeDtypeStruct((SLOT, D), jnp.bfloat16),
        jax.ShapeDtypeStruct((SLOT, D), jnp.float32),
        jax.ShapeDtypeStruct((SLOT, D), jnp.bfloat16),
        jax.ShapeDtypeStruct((SLOT, 3 * D), jnp.bfloat16),
        jax.ShapeDtypeStruct((D, 128), jnp.float32),
        jax.ShapeDtypeStruct((1, D), jnp.float32),
        jax.ShapeDtypeStruct((HEADS, SLOT, SLOT), jnp.bfloat16),
    ]
    return pl.pallas_call(
        unwind_kernel,
        grid=(1,),
        in_specs=[SMEM] + specs + [ANY] * len(waits),
        out_specs=[whole(o) for o in out_shape],
        out_shape=out_shape,
        scratch_shapes=[pltpu.VMEM((SLOT, D), jnp.bfloat16)],
        compiler_params=params(),
        cost_estimate=lasts(17),
        name="unwind",
    )(length.reshape(1), *ins, *waits)


def weights_kernel(groups, wide, bits_ref, xn_ref, dqkv0, dqkv1, heads0, heads1, dattn0, dattn1, *refs):
    count = xn_ref.shape[1] // groups // 2

    def rows_of(ref, start):
        return jnp.concatenate(
            [
                ref[start : start + SLOT, pl.ds(pl.multiple_of((2 * g + bits_ref[0]) * count, count), count)]
                for g in range(groups)
            ],
            axis=1,
        )

    left = [rows_of(xn_ref, 0), rows_of(xn_ref, SLOT)]
    heads = [rows_of(heads0, 0), rows_of(heads1, 0)]
    half = count // 2
    for part in range(4):
        if part < 3:
            span = slice(part * D, (part + 1) * D)
            total = contract_first(left[0], dqkv0[:, span]) + contract_first(left[1], dqkv1[:, span])
        else:
            total = contract_first(heads[0], dattn0[...]) + contract_first(heads[1], dattn1[...])
        total = total.reshape(groups, count, D)
        which, span = part // 2, slice(part % 2 * D, (part % 2 + 1) * D)
        if not wide:
            refs[-1][which, :, :, span] = total.astype(jnp.bfloat16)
            continue
        total = total + refs[0][which, :, :, span].astype(jnp.float32)
        total_ref = refs[-1]
        total_ref[...] = total.astype(jnp.bfloat16)
        send_ref, keep_ref = refs[-5 + 2 * which : len(refs) - 3 + 2 * which]
        bit = bits_ref[1 + which]
        keep_ref[:, :, span] = total_ref[:, pl.ds(pl.multiple_of(bit * half, half), half)]
        send_ref[:, :, span] = total_ref[:, pl.ds(pl.multiple_of((1 - bit) * half, half), half)]


def weight_grads(groups, xn_all, dqkv, heads, dattn, arrived=None):
    place = lax.axis_index("rep")
    wide = arrived is not None
    core = bit_of(place, 1)
    bits = jnp.stack(
        [core if wide else 1 - core] + [bit_of(place, order_of(w)[1]) for w in range(2)]
    ).astype(jnp.int32)
    count = D // groups // 2
    if count % 128:
        return weight_grads_plain(groups, xn_all, dqkv, heads, dattn, arrived)
    shapes = [(groups, count // 2, 2 * D)] * 4 if wide else [(2, groups, count, 2 * D)]
    return pl.pallas_call(
        functools.partial(weights_kernel, groups, wide),
        in_specs=[SMEM] + [VMEM] * (8 if wide else 7),
        out_specs=[VMEM] * len(shapes),
        out_shape=[jax.ShapeDtypeStruct(shape, jnp.bfloat16) for shape in shapes],
        scratch_shapes=[pltpu.VMEM((groups, count, D), jnp.bfloat16)] if wide else [],
        compiler_params=params(),
        cost_estimate=lasts(6),
        name="weights",
    )(bits, xn_all, *dqkv, *heads, *dattn, *([arrived] if wide else []))


def weight_grads_plain(groups, xn_all, dqkv, heads, dattn, arrived):
    total = jnp.concatenate(
        [
            contract_first(xn_all, jnp.concatenate(dqkv, axis=0)),
            contract_first(jnp.concatenate(heads, axis=0), jnp.concatenate(dattn, axis=0)),
        ],
        axis=1,
    ).reshape(groups, D // groups, 4 * D)
    theirs, mine = halves_of(total, 1, 1)
    if arrived is None:
        return [jnp.stack(jnp.split(theirs.astype(jnp.bfloat16), 2, axis=2))]
    mine = [
        (m + a.astype(jnp.float32)).astype(jnp.bfloat16)
        for m, a in zip(jnp.split(mine, 2, axis=2), arrived)
    ]
    return [cut for w in range(2) for cut in halves_of(mine[w], order_of(w)[1], 1)]


def finish_kernel(tokens_ref, gain_ref, wqkv_ref, dqkv0, dqkv1, dhidden0, dhidden1, out_ref, dgain_ref):
    total = None
    for micro, (dqkv, dhidden) in enumerate(((dqkv0, dhidden0), (dqkv1, dhidden1))):
        grad = contract_last(dqkv[...], wqkv_ref[...])
        by_x, by_gain = norm_back(tokens_ref[micro].astype(jnp.float32), gain_ref[...], grad)
        out_ref[micro] = dhidden[...] + by_x
        total = by_gain if total is None else total + by_gain
    dgain_ref[...] = total


def finish(tokens, gain_first, qkv_weight, dqkv, dhidden):
    return pl.pallas_call(
        finish_kernel,
        in_specs=[VMEM] * 7,
        out_specs=[VMEM] * 2,
        out_shape=[
            jax.ShapeDtypeStruct((MICRO, SLOT, D), jnp.float32),
            jax.ShapeDtypeStruct((1, D), jnp.float32),
        ],
        compiler_params=params(),
        cost_estimate=lasts(10),
        name="finish",
    )(tokens, gain_first.reshape(1, D), qkv_weight, *dqkv, *dhidden)


def join_small(by_distance, router, gains, rel_bias):
    groups = lax.axis_size("grp")
    place = lax.axis_index("grp")
    a, b = router.size, router.size + gains.size
    size = b + rel_bias.size
    blocks = [by_distance[m][:size].astype(jnp.float32) for m in range(groups)]
    rows = []
    for at in range(groups):
        row = blocks[0]
        for m in range(1, groups):
            row = jnp.where(place ^ m == at, blocks[m], row)
        rows.append(row)
    every = jnp.stack(rows)
    return (
        every[:, :a].reshape(-1, router.shape[1]).astype(jnp.bfloat16),
        every[:, a:b].reshape(-1, gains.shape[1]),
        every[:, b:].reshape(-1, rel_bias.shape[1]),
    )


def per_device(
    tokens,
    w_qkv,
    w_out,
    router,
    gains,
    rel_bias,
    w_gate,
    w_up,
    w_down,
    lengths,
    choices,
    priority,
    cotangent,
):
    groups = lax.axis_size("grp")
    split_count = groups // EXPERTS
    place = lax.axis_index("grp")
    my_expert = place // split_count
    small = jnp.concatenate([router.reshape(-1), gains.reshape(-1), rel_bias.reshape(-1)])
    chains, came_along = gather_weights(w_qkv, w_out, small)
    after = [chains[1][1][0][1]]
    router_weight, gain_full, bias_table = join_small(came_along, router, gains, rel_bias)
    router_pad = jnp.pad(router_weight, ((0, 0), (0, 128 - EXPERTS)))
    bucket_hits = (
        jnp.asarray(bucket_matrix())[:, :, None] == jnp.arange(BUCKETS)[None, None, :]
    ).astype(jnp.bfloat16)
    bias_full = jnp.einsum(
        "hk,ijk->hij", bias_table.astype(jnp.bfloat16), bucket_hits, preferred_element_type=jnp.float32
    ).astype(jnp.bfloat16)

    target = (
        (jnp.arange(groups) // split_count)[:, None] * CAP + jnp.arange(CAP)[None, :]
    ).reshape(-1)
    routes = []
    for micro in range(MICRO):
        _, kept_mask, slot_index = expert_slots(choices[micro], priority[micro], lengths[micro, 0])
        hits = [
            (slot_index[None, :, k, None] == target.reshape(groups, 1, CAP)).astype(jnp.bfloat16)
            for k in range(2)
        ]
        spots = (
            (target[:, None] == slot_index[None, :, 0]) | (target[:, None] == slot_index[None, :, 1])
        ).astype(jnp.bfloat16)
        routes.append([kept_mask, hits, spots])
    spots1 = routes[1][2]
    pieces = gather_cores(chains, bias_full, router_pad, gain_full, spots1)
    for micro in range(MICRO):
        spots = routes[micro][2]
        (sent,) = tie([cotangent[micro]], *after)
        blocks = dot(spots, sent).astype(jnp.bfloat16).reshape(groups, CAP, D)
        routes[micro][2] = spots.reshape(groups, CAP, SLOT)
        routes[micro].append(to_experts(blocks).reshape(groups * CAP, D))
        after = [piece for _, _, piece in pieces]

    xn_all, *qkv_all, out_weight = project(tokens, gain_full[:, 0], pieces, [routes[0][-1], bias_full, router_pad])
    forward = []
    for micro in range(MICRO):
        waits = [routes[1][-1], forward[0][0]] if micro else []
        forward.append(
            attend(
                micro, lengths[micro], qkv_all[micro], tokens, bias_full, out_weight, gain_full[:, 1],
                routes[micro][2], waits,
            )
        )
    rows0 = to_experts(forward[0][3]).reshape(groups * CAP, D)
    qkv_weight = join_qkv(pieces, [forward[1][0]])
    blocks1, _ = tie([forward[1][3], rows0], qkv_weight)
    rows = [rows0, to_experts(blocks1).reshape(groups * CAP, D)]

    def expert(micro, waits):
        return run_expert(
            my_expert, rows[micro], routes[micro][-1], router_pad, w_gate, w_up, w_down, waits
        )

    inner = [expert(0, [qkv_weight])]
    home0 = to_experts(inner[0][4])
    inner.append(expert(1, [inner[0][0]]))
    home1 = to_experts(inner[1][4])
    doutput, act, dgate, dup = ([inner[micro][i] for micro in range(MICRO)] for i in range(4))

    def launch(left, right, waits):
        theirs = products(left, right, None, waits)
        return theirs[0], [exchange(half, "rep", 1) for half in theirs]

    def settle(left, right, arrived, waits):
        outs = products(left, right, arrived, waits)
        pair = [Halving(w, 0) for w in range(2)]
        for w in range(2):
            pair[w].start(outs[2 * w], outs[2 * w + 1], 1)
        return pair, outs[1]

    def unwound(micro, home, waits):
        kept_mask, hits, _, _ = routes[micro]
        heads, hidden, xn_second, _ = forward[micro]
        return unwind(
            micro, lengths[micro], home, hits, choices[micro], kept_mask, hidden, xn_second, cotangent,
            router_pad, gain_full[:, 1], out_weight, qkv_all[micro], bias_full, waits,
        )

    tok, down_came = launch(act, doutput, [])
    tok, gate_came = launch(rows, dgate, [tok])
    down, tok = settle(act, doutput, down_came, [tok, home0])
    tok, up_came = launch(rows, dup, [tok])
    gate, tok = settle(rows, dgate, gate_came, [tok])
    land(down, tok)
    for half in down:
        half.halve(2)
    up, tok = settle(rows, dup, up_came, [half.kept for half in down])
    land([*gate, *down], tok)
    for half in gate:
        half.halve(2)
    for half in down:
        half.own()
        half.back()
    un0 = unwound(0, home0, [half.kept for half in (*gate, *down)])
    land([*up, *down, *gate], un0[0])
    for half in up:
        half.halve(2)
    for half in down:
        half.back_pair()
    for half in gate:
        half.own()
    un1 = unwound(1, home1, [half.kept for half in (*up, *down, *gate)])
    un = (un0, un1)

    def attention_grads(xn_in, arrived=None):
        return weight_grads(
            groups, xn_in, [u[3] for u in un], [forward[m][0] for m in range(MICRO)], [u[2] for u in un], arrived
        )

    (theirs,) = attention_grads(xn_all)
    land([*up, *down], theirs)
    came = exchange(tie([theirs], up[0].kept)[0], "rep", 1)
    for half in up:
        half.own()
        half.back()
    for half in gate:
        half.back()
    dscores = tie([u[6] for u in un], *[half.kept for half in up])
    bias_grad = sum(
        jnp.einsum("hij,ijk->hk", d, bucket_hits, preferred_element_type=jnp.float32) for d in dscores
    )
    outs = attention_grads(tie([xn_all], bias_grad, *[half.kept for half in (*up, *gate)])[0], came)
    attn = [Halving(w, 1) for w in range(2)]
    for w in range(2):
        attn[w].start(outs[2 * w], outs[2 * w + 1], 1)
    land([*up, *gate, *down], outs[0])
    down_own, down_got = swap_cores(down)
    token_grads, dgain_first = finish(
        tie([tokens], down_own)[0], gain_full[:, 0], qkv_weight, [u[3] for u in un], [u[1] for u in un]
    )

    small = [
        (un0[4] + un1[4])[:, :EXPERTS].reshape(-1),
        jnp.stack([dgain_first[0], un0[5][0] + un1[5][0]], axis=1).reshape(-1),
        bias_grad.reshape(-1),
    ]
    flat = jnp.concatenate(small)
    flat = jnp.pad(flat, (0, -flat.size % 1024)).reshape(-1, 128)
    steps = [("rep", m) for m in masks_of(lax.axis_size("rep"))] + [("grp", m) for m in masks_of(groups)]
    small_sum = Halving(0, 0)
    small_sum.kept = flat

    def add_small():
        if small_sum.moving is not None:
            small_sum.kept, small_sum.moving = small_sum.kept + small_sum.moving, None
        if steps:
            small_sum.moving = exchange(small_sum.kept, *steps.pop(0))

    add_small()
    down_grad = assemble(down, *tie([down_own, down_got], small_sum.kept))
    land([*attn, small_sum], down_grad)
    for half in attn:
        half.halve(2)
    add_small()
    land([*attn, small_sum])
    for half in attn:
        half.own()
    zsum = Halving(0, 0)
    zsum.kept = to_experts(jnp.stack([half.kept for half in attn], axis=1))
    for half in (*gate, *up):
        half.kept, half.moving = tie([half.kept, half.moving], *[a.kept for a in attn])
        half.back_pair()
    add_small()
    land([zsum, *gate, *up, small_sum])
    total = jnp.sum(zsum.kept.astype(jnp.float32), axis=0).astype(jnp.bfloat16)
    for w in range(2):
        attn[w].kept = total[w]
        attn[w].back()
    land([*gate, *up], total)
    gate_own, gate_got = swap_cores(gate)
    add_small()
    land([*attn, small_sum], gate_own)
    for half in attn:
        half.back_pair()
    land(up, attn[0].kept)
    up_own, up_got = swap_cores(up)
    gate_grad = assemble(gate, *tie([gate_own, gate_got], up_own))
    add_small()
    land([*attn, small_sum], gate_grad)
    attn_own, attn_got = swap_cores(attn)
    up_grad = assemble(up, *tie([up_own, up_got], attn_own))
    while small_sum.moving is not None:
        add_small()
    flat = small_sum.kept
    qkv_grad, out_grad = assemble_attention(attn, *tie([attn_own, attn_got], up_grad))

    flat = flat.reshape(-1)
    outs = []
    start = 0
    for whole in ((D, EXPERTS), (D, 2), (HEADS, BUCKETS)):
        size = whole[0] * whole[1]
        rows_here = whole[0] // groups
        outs.append(
            lax.dynamic_slice_in_dim(
                flat[start : start + size].reshape(whole), place * rows_here, rows_here, 0
            )
        )
        start += size
    return (
        jnp.stack([u[0] for u in un]),
        token_grads,
        qkv_grad,
        out_grad,
        outs[0],
        outs[1],
        outs[2],
        gate_grad[None],
        up_grad[None],
        down_grad[None],
    )


def solution(mesh):
    placed = (
        P(None, ("rep", "grp"), None),
        P("grp", None),
        P("grp", None),
        P("grp", None),
        P("grp", None),
        P("grp", None),
        P("grp", None, None),
        P("grp", None, None),
        P("grp", None, None),
        P(None, ("rep", "grp")),
        P(None, ("rep", "grp"), None),
        P(None, ("rep", "grp")),
        P(None, ("rep", "grp"), None),
    )
    return jax.shard_map(
        per_device,
        mesh=mesh,
        in_specs=placed,
        out_specs=(
            P(None, ("rep", "grp"), None),
            P(None, ("rep", "grp"), None),
            P("grp", None),
            P("grp", None),
            P("grp", None),
            P("grp", None),
            P("grp", None),
            P("grp", None, None),
            P("grp", None, None),
            P("grp", None, None),
        ),
        check_vma=False,
    )
```

```python
import functools

import jax
import jax.numpy as jnp
import numpy as np
from jax import lax
from jax.experimental import pallas as pl
from jax.experimental.pallas import tpu as pltpu
from jax.sharding import PartitionSpec as P

D = 1024
HEADS = 16
HEAD_DIM = 64
EXPERTS = 4
BUCKETS = 32
MAX_DIST = 128
MICRO = 2
SLOT = 192
CAP = 120
VMEM_LIMIT = 56 * 1024 * 1024
PART = 0.001


def lasts(us):
    return pl.CostEstimate(flops=int(us * PART * 1.15e9), bytes_accessed=1, transcendentals=0)


VMEM = pl.BlockSpec(memory_space=pltpu.VMEM)
SMEM = pl.BlockSpec(memory_space=pltpu.SMEM)
ANY = pl.BlockSpec(memory_space=pl.ANY)


def params():
    return pltpu.CompilerParams(vmem_limit_bytes=VMEM_LIMIT)


def bucket_matrix():
    distance = np.arange(SLOT)
    exact_count = BUCKETS // 2
    safe_span = np.maximum(distance, 1) / exact_count
    log_bucket = exact_count + np.floor(
        np.log(safe_span) / np.log(MAX_DIST / exact_count) * (BUCKETS - exact_count)
    ).astype(np.int32)
    bucket_of = np.where(distance < exact_count, distance, np.minimum(log_bucket, BUCKETS - 1))
    offsets = np.maximum(distance[:, None] - distance[None, :], 0)
    return bucket_of[offsets].astype(np.int32)


def dot(left, right):
    return jnp.dot(left, right, preferred_element_type=jnp.float32)


def contract_last(left, right):
    return lax.dot_general(
        left, right, (((1,), (1,)), ((), ())), preferred_element_type=jnp.float32
    )


def contract_first(left, right):
    return lax.dot_general(
        left, right, (((0,), (0,)), ((), ())), preferred_element_type=jnp.float32
    )


def expert_slots(expert_pick, priority_row, length):
    live_mask = (jnp.arange(SLOT) < length).astype(jnp.float32)
    pick_hits = (expert_pick[:, :, None] == jnp.arange(EXPERTS)[None, None, :]).astype(jnp.float32)
    expert_hits = jnp.sum(pick_hits, axis=1) * live_mask[:, None]
    before = (priority_row[None, :] < priority_row[:, None]).astype(jnp.bfloat16)
    ahead_count = dot(before, expert_hits.astype(jnp.bfloat16))
    place_pos = jnp.sum(pick_hits * ahead_count[:, None, :], axis=2)
    kept_mask = live_mask[:, None] * (place_pos < CAP - 0.5).astype(jnp.float32)
    slot_index = jnp.where(
        kept_mask > 0.5, expert_pick * CAP + place_pos.astype(jnp.int32), EXPERTS * CAP
    )
    return (pick_hits, kept_mask, slot_index)


def exchange(block, axis, mask):
    return lax.ppermute(block, axis, [(i, i ^ mask) for i in range(lax.axis_size(axis))])


def masks_of(count):
    return [1 << bit for bit in range(count.bit_length() - 1)]


def spread(own, axis, masks):
    held = [(0, own)]
    for mask in masks:
        held += [(far ^ mask, exchange(block, axis, mask)) for far, block in held]
    return held


def to_experts(blocks):
    return lax.all_to_all(blocks, "grp", split_axis=0, concat_axis=0, tiled=True)


def bit_of(index, mask):
    return (index & mask) // mask


def tie(values, *after):
    return lax.optimization_barrier((tuple(values), after))[0]


def rep_masks():
    masks = masks_of(lax.axis_size("rep"))
    return masks[3:], masks[:3]


def order_of(which):
    masks = rep_masks()[1]
    return masks[:1] + (masks[1:] if which == 0 else masks[:0:-1])


def halves_of(block, mask, dim):
    half = block.shape[dim] // 2
    bit = bit_of(lax.axis_index("rep"), mask)
    return (
        lax.dynamic_slice_in_dim(block, (1 - bit) * half, half, dim),
        lax.dynamic_slice_in_dim(block, bit * half, half, dim),
    )


def add_low(left, right):
    return (left.astype(jnp.float32) + right.astype(jnp.float32)).astype(jnp.bfloat16)


class Halving:
    def __init__(self, which, dim):
        self.which, self.dim = which, dim
        self.masks = order_of(which)
        self.kept = self.moving = None
        self.held = None

    def start(self, send, keep, at):
        self.kept, self.moving = keep, exchange(send, "rep", self.masks[at])

    def halve(self, at):
        kept, got = (halves_of(x, self.masks[at], self.dim) for x in (self.kept, self.moving))
        self.start(*(add_low(k, g) for k, g in zip(kept, got)), at)

    def own(self):
        total = add_low(self.kept, self.moving)
        for mask in rep_masks()[0]:
            total = add_low(total, exchange(total, "rep", mask))
        self.kept, self.moving = total, None

    def back(self):
        self.moving = exchange(self.kept, "rep", self.masks[-1])

    def back_pair(self):
        self.kept = jnp.stack([self.kept, self.moving])
        self.moving = exchange(self.kept, "rep", self.masks[-2])

    def place(self):
        index = 0
        for mask in self.masks:
            index = 2 * index + bit_of(lax.axis_index("rep"), mask)
        return index


def land(halvings, *after):
    flat = [x for h in halvings for x in (h.kept, h.moving) if x is not None]
    flat = list(tie(flat, *after))
    for h in halvings:
        h.kept = flat.pop(0)
        if h.moving is not None:
            h.moving = flat.pop(0)


def swap_cores(pair):
    own = jnp.concatenate([x for h in pair for x in (h.kept, h.moving)], axis=0)
    return own, exchange(own, "rep", 1)


def assemble(pair_of_halves, own, got):
    places = jnp.stack([half.place() for half in pair_of_halves]).astype(jnp.int32)
    pieces, rows, cols = own.shape
    deep = pieces // 4
    cut_cores = cols % 128 != 0

    def body(place_ref, own_ref, got_ref, out_ref):
        half, core, step = (pl.program_id(i) for i in range(3))
        place = place_ref[half]
        far = (core * deep + step) ^ (place // 2)
        at = 2 * (half * deep + far % deep)
        out = out_ref.at[0] if cut_cores else out_ref
        for other, ref in enumerate((own_ref, got_ref)):

            @pl.when(far // deep == other)
            def _():
                out[:rows] = ref[at + place % 2].astype(jnp.float32)
                out[rows:] = ref[at + 1 - place % 2].astype(jnp.float32)

    whole = pl.BlockSpec((pieces, rows, cols), lambda half, core, step, place_ref: (0, 0, 0))
    out_shape = (4 * deep * rows, 2 * cols)
    out_spec = pl.BlockSpec(
        (2 * rows, cols), lambda half, core, step, place_ref: (half * deep + step, core)
    )
    if cut_cores:
        out_shape = (2, 4 * deep * rows, cols)
        out_spec = pl.BlockSpec(
            (1, 2 * rows, cols), lambda half, core, step, place_ref: (core, half * deep + step, 0)
        )
    out = pl.pallas_call(
        body,
        grid_spec=pltpu.PrefetchScalarGridSpec(
            num_scalar_prefetch=1,
            grid=(2, 2, deep),
            in_specs=[whole] * 2,
            out_specs=out_spec,
        ),
        out_shape=jax.ShapeDtypeStruct(out_shape, jnp.float32),
        compiler_params=params(),
        cost_estimate=lasts(9),
        name="assemble",
    )(places, own, got)
    return jnp.concatenate([out[0], out[1]], axis=1) if cut_cores else out


def assemble_attention(pair_of_halves, own, got):
    places = jnp.stack([half.place() for half in pair_of_halves]).astype(jnp.int32)
    pieces, rows, _ = own.shape
    each = pieces // 2

    def body(place_ref, own_ref, got_ref, qkv_ref, out_ref):
        for other, ref in enumerate((own_ref, got_ref)):
            for at in range(pieces):
                where = (other * each + at % each) ^ place_ref[at // each]
                span = pl.ds(pl.multiple_of(where * rows, rows), rows)
                values = ref[at].astype(jnp.float32)
                if at < each:
                    qkv_ref[span, : 2 * D] = values
                else:
                    qkv_ref[span, 2 * D :] = values[:, :D]
                    out_ref[span, :] = values[:, D:]

    depth = 2 * each * rows
    return pl.pallas_call(
        body,
        in_specs=[SMEM] + [VMEM] * 2,
        out_specs=[VMEM] * 2,
        out_shape=[
            jax.ShapeDtypeStruct((depth, 3 * D), jnp.float32),
            jax.ShapeDtypeStruct((depth, D), jnp.float32),
        ],
        compiler_params=params(),
        cost_estimate=lasts(4),
        name="assemble_attention",
    )(places, own, got)


def gather_weights(w_qkv, w_out, small):
    slices = min(lax.axis_size("rep"), 8)
    eighth = lax.axis_index("rep") % slices
    width = D // slices
    parts = [w_qkv[:, i * D : (i + 1) * D] for i in range(3)] + [w_out]
    own = jnp.concatenate(
        [lax.dynamic_slice_in_dim(part, eighth * width, width, 1) for part in parts], axis=1
    )
    depth = own.shape[0]
    small = small.reshape(-1)
    lines = -(-small.size // (16 * own.shape[1])) * 16
    small = jnp.pad(small, (0, lines * own.shape[1] - small.size)).reshape(lines, -1)
    masks = masks_of(slices)
    held = spread(jnp.concatenate([own, small]), "grp", masks_of(lax.axis_size("grp"))[::-1])
    over_grp = [(m, block[:depth]) for m, block in held]
    half = len(over_grp) // 2
    chains = []
    for which in range(2):
        mine = over_grp[which * half : (which + 1) * half]
        order = masks[1:] if which == 0 else masks[:0:-1]
        block = jnp.stack([piece for _, piece in mine])
        chains.append(([m for m, _ in mine], spread(block, "rep", order)))
    return chains, {m: block[depth:].reshape(-1) for m, block in held}


def gather_cores(chains, *after):
    pieces = []
    for members, held in chains:
        blocks = tie([block for _, block in held], *after)
        for (far, _), block in zip(held, blocks):
            pieces += [(far, members, block), (far ^ 1, members, exchange(block, "rep", 1))]
    return pieces


def norm_rows(x, gain):
    return x * lax.rsqrt(jnp.mean(x * x, axis=-1, keepdims=True) + 1e-06) * gain


def each_piece(plan, pieces, far):
    for (this, members), piece in zip(plan, pieces):
        if this == far:
            yield from ((m, piece, at) for at, m in enumerate(members))


def project_kernel(plan, micro, place_ref, tokens_ref, gain_ref, *refs):
    pieces = refs[: len(plan)]
    xn_ref, qkv_ref, weight_ref = refs[-3:]
    depth = pieces[0].shape[1]
    width = pieces[0].shape[2] // 4
    xn_ref[...] = norm_rows(tokens_ref[0].astype(jnp.float32), gain_ref[...]).astype(jnp.bfloat16)
    for far in sorted({far for far, _ in plan}):
        column = pl.multiple_of((place_ref[0] ^ far) * width, width)
        total = None
        for m, piece, at in each_piece(plan, pieces, far):
            row = pl.multiple_of((place_ref[1] ^ m) * depth, depth)
            if micro == 0:
                weight_ref[pl.ds(row, depth), pl.ds(column, width)] = piece[at, :, 3 * width :]
            else:
                for part in range(3):
                    weight_ref[pl.ds(row, depth), pl.ds(column + part * D, width)] = piece[
                        at, :, part * width : (part + 1) * width
                    ]
            term = dot(xn_ref[:, pl.ds(row, depth)], piece[at, :, : 3 * width])
            total = term if total is None else total + term
        for part in range(3):
            low = total[:, part * width : (part + 1) * width].astype(jnp.bfloat16)
            qkv_ref[:, pl.ds(column + part * D, width)] = low


def places_of():
    slices = min(lax.axis_size("rep"), 8)
    return jnp.stack([lax.axis_index("rep") % slices, lax.axis_index("grp")]).astype(jnp.int32)


def project(micro, tokens, gain_first, pieces, waits):
    plan = [(far, m) for far, m, _ in pieces]
    whole = lambda *shape: pl.BlockSpec(shape, lambda i: (0,) * len(shape))
    out_shape = [
        jax.ShapeDtypeStruct(shape, jnp.bfloat16)
        for shape in ((SLOT, D), (SLOT, 3 * D), (D, 3 * D if micro else D))
    ]
    return pl.pallas_call(
        functools.partial(project_kernel, plan, micro),
        grid=(1,),
        in_specs=[SMEM, pl.BlockSpec((1, SLOT, D), lambda i: (micro, 0, 0)), whole(1, D)]
        + [whole(*piece.shape) for _, _, piece in pieces]
        + [ANY] * len(waits),
        out_specs=[whole(*o.shape) for o in out_shape],
        out_shape=out_shape,
        compiler_params=params(),
        cost_estimate=lasts(10),
        name="project",
    )(places_of(), tokens, gain_first.reshape(1, D), *[piece for _, _, piece in pieces], *waits)


def allowed_pairs(length):
    row = lax.broadcasted_iota(jnp.int32, (SLOT, SLOT), 0)
    column = lax.broadcasted_iota(jnp.int32, (SLOT, SLOT), 1)
    return (row <= column) & (row < length)


def attend_kernel(groups, length_ref, qkv_ref, tokens_ref, bias_ref, wout_ref, gain_ref, spots_ref, *refs):
    heads_ref, hidden_ref, xn_ref, rows_ref = refs[-4:]
    allowed = allowed_pairs(length_ref[0])
    scale = HEAD_DIM ** (-0.5)
    for pair in range(HEADS // 2):
        outs = []
        for head in (2 * pair, 2 * pair + 1):
            at = head * HEAD_DIM
            scores = contract_last(
                qkv_ref[:, D + at : D + at + HEAD_DIM], qkv_ref[:, at : at + HEAD_DIM]
            )
            scores = jnp.where(allowed, scores * scale + bias_ref[head].astype(jnp.float32), -1e30)
            weights = jnp.exp(scores - jnp.max(scores, axis=0, keepdims=True))
            probs = weights / jnp.sum(weights, axis=0, keepdims=True)
            outs.append(
                contract_first(probs.astype(jnp.bfloat16), qkv_ref[:, 2 * D + at : 2 * D + at + HEAD_DIM])
            )
        heads_ref[:, pair * 128 : (pair + 1) * 128] = jnp.concatenate(outs, axis=1).astype(jnp.bfloat16)
    hidden = tokens_ref[0].astype(jnp.float32) + dot(heads_ref[...], wout_ref[...])
    hidden_ref[...] = hidden
    xn = norm_rows(hidden, gain_ref[...]).astype(jnp.bfloat16)
    xn_ref[...] = xn
    for m in range(groups):
        rows_ref[m] = dot(spots_ref[m], xn).astype(jnp.bfloat16)


def attend(micro, length, qkv_rows, tokens, bias_full, out_weight, gain_second, spots, waits):
    groups = spots.shape[0]
    whole = lambda *shape: pl.BlockSpec(shape, lambda i: (0,) * len(shape))
    low = jax.ShapeDtypeStruct((SLOT, D), jnp.bfloat16)
    out_shape = [
        low,
        jax.ShapeDtypeStruct((SLOT, D), jnp.float32),
        low,
        jax.ShapeDtypeStruct((groups, CAP, D), jnp.bfloat16),
    ]
    return pl.pallas_call(
        functools.partial(attend_kernel, groups),
        grid=(1,),
        in_specs=[
            SMEM,
            whole(SLOT, 3 * D),
            pl.BlockSpec((1, SLOT, D), lambda i: (micro, 0, 0)),
            whole(HEADS, SLOT, SLOT),
            whole(D, D),
            whole(1, D),
            whole(groups, CAP, SLOT),
        ]
        + [ANY] * len(waits),
        out_specs=[whole(*o.shape) for o in out_shape],
        out_shape=out_shape,
        compiler_params=params(),
        cost_estimate=lasts(9.3),
        name="attend",
    )(length.reshape(1), qkv_rows, tokens, bias_full, out_weight, gain_second.reshape(1, D), spots, *waits)


def gelu_parts(v):
    c = np.float32(np.sqrt(2 / np.pi))
    t = jnp.tanh(c * (v + np.float32(0.044715) * (v * v * v)))
    half = 0.5 * (1.0 + t)
    slope = half + 0.5 * v * (1.0 - t * t) * (c * (1.0 + np.float32(3 * 0.044715) * (v * v)))
    return v * half, slope


def expert_kernel(groups, chunk, expert_ref, rows_ref, grads_ref, router_ref, wg_hbm, wu_hbm, wd_hbm, *refs):
    dout_ref, act_hbm, dgate_hbm, dup_hbm, back_ref = refs[-13:-8]
    wg, wu, wd, act, dgate, dup, came, went = refs[-8:]
    hidden = act.shape[1]
    steps = hidden // chunk

    def incoming(c):
        span = pl.ds(pl.multiple_of(c * chunk, chunk), chunk)
        return [
            pltpu.make_async_copy(wg_hbm.at[0, :, span], wg.at[:, span], came.at[0, c]),
            pltpu.make_async_copy(wu_hbm.at[0, :, span], wu.at[:, span], came.at[1, c]),
            pltpu.make_async_copy(wd_hbm.at[0, span, :], wd.at[span, :], came.at[2, c]),
        ]

    def outgoing(c):
        span = pl.ds(pl.multiple_of(c * chunk, chunk), chunk)
        return [
            pltpu.make_async_copy(vmem.at[:, span], hbm.at[:, span], went.at[i, c])
            for i, (vmem, hbm) in enumerate(((act, act_hbm), (dgate, dgate_hbm), (dup, dup_hbm)))
        ]

    @pl.loop(0, steps)
    def _(c):
        for copy in incoming(c):
            copy.start()

    logits = dot(rows_ref[...], router_ref[...])
    lane = lax.broadcasted_iota(jnp.int32, logits.shape, 1)
    logits = jnp.where(lane < EXPERTS, logits, -1e30)
    weights = jnp.exp(logits - jnp.max(logits, axis=-1, keepdims=True))
    route = weights / jnp.sum(weights, axis=-1, keepdims=True)
    gate = jnp.sum(jnp.where(lane == expert_ref[0], route, 0.0), axis=-1, keepdims=True)
    dout_ref[...] = (gate * grads_ref[...].astype(jnp.float32)).astype(jnp.bfloat16)

    @pl.loop(0, steps)
    def _(c):
        span = pl.ds(pl.multiple_of(c * chunk, chunk), chunk)
        for copy in incoming(c):
            copy.wait()
        gate_pre = dot(rows_ref[...], wg[:, span])
        up_pre = dot(rows_ref[...], wu[:, span])
        gelu, slope = gelu_parts(gate_pre)
        act[:, span] = (gelu * up_pre).astype(jnp.bfloat16)
        grad_act = contract_last(dout_ref[...], wd[span, :])
        dgate[:, span] = (grad_act * up_pre * slope).astype(jnp.bfloat16)
        dup[:, span] = (grad_act * gelu).astype(jnp.bfloat16)
        for copy in outgoing(c):
            copy.start()

    part = dot(act[...], wd[...])
    for m in range(groups):
        back_ref[m, 0] = part[m * CAP : (m + 1) * CAP].astype(jnp.bfloat16)
    grad_rows = contract_last(dgate[...], wg[...]) + contract_last(dup[...], wu[...])
    for m in range(groups):
        back_ref[m, 1] = grad_rows[m * CAP : (m + 1) * CAP].astype(jnp.bfloat16)

    @pl.loop(0, steps)
    def _(c):
        for copy in outgoing(c):
            copy.wait()


def run_expert(expert, rows, grad_rows, router_pad, w_gate, w_up, w_down, waits):
    count = rows.shape[0]
    groups = count // CAP
    hidden = w_gate.shape[2]
    chunk = 256 if hidden % 256 == 0 else 128
    steps = hidden // chunk
    wide = jax.ShapeDtypeStruct((count, hidden), jnp.bfloat16)
    low = lambda *shape: pltpu.VMEM(shape, jnp.bfloat16)
    return pl.pallas_call(
        functools.partial(expert_kernel, groups, chunk),
        in_specs=[SMEM] + [VMEM] * 3 + [ANY] * (3 + len(waits)),
        out_specs=[VMEM] + [ANY] * 3 + [VMEM],
        out_shape=[
            jax.ShapeDtypeStruct((count, D), jnp.bfloat16),
            wide,
            wide,
            wide,
            jax.ShapeDtypeStruct((groups, 2, CAP, D), jnp.bfloat16),
        ],
        scratch_shapes=[
            low(D, hidden),
            low(D, hidden),
            low(hidden, D),
            low(count, hidden),
            low(count, hidden),
            low(count, hidden),
            pltpu.SemaphoreType.DMA((3, steps)),
            pltpu.SemaphoreType.DMA((3, steps)),
        ],
        compiler_params=params(),
        cost_estimate=lasts(22),
        name="expert",
    )(jnp.reshape(expert, (1,)).astype(jnp.int32), rows, grad_rows, router_pad, w_gate, w_up, w_down, *waits)


def products_kernel(wide, bits_ref, left0, left1, right0, right1, *refs):
    total = contract_first(left0[...], right0[...]) + contract_first(left1[...], right1[...])
    for which in range(2):

        @pl.when(pl.program_id(0) == which)
        def _():
            if not wide:
                refs[which - 2][...] = total.astype(jnp.bfloat16)
                return
            total_ref = refs[-1]
            total_ref[...] = (total + refs[which][...].astype(jnp.float32)).astype(jnp.bfloat16)
            send_ref, keep_ref = refs[-5 + 2 * which : len(refs) - 3 + 2 * which]
            bit = bits_ref[1 + which]
            half = send_ref.shape[0]
            keep_ref[...] = total_ref[pl.ds(pl.multiple_of(bit * half, half), half)]
            send_ref[...] = total_ref[pl.ds(pl.multiple_of((1 - bit) * half, half), half)]


def products(left, right, arrived=None, waits=()):
    place = lax.axis_index("rep")
    wide = arrived is not None
    core = bit_of(place, 1)
    bits = jnp.stack(
        [core if wide else 1 - core] + [bit_of(place, order_of(w)[1]) for w in range(2)]
    ).astype(jnp.int32)
    count = left[0].shape[0]
    rows, cols = left[0].shape[1] // 2, right[0].shape[1] // 2
    if rows % 128 or cols % 128:
        return products_plain(left, right, arrived)
    deep, number = (rows // 2, 4) if wide else (rows, 2)
    return pl.pallas_call(
        functools.partial(products_kernel, wide),
        grid_spec=pltpu.PrefetchScalarGridSpec(
            num_scalar_prefetch=1,
            grid=(2,),
            in_specs=[pl.BlockSpec((count, rows), lambda h, b: (0, h))] * 2
            + [pl.BlockSpec((count, cols), lambda h, b: (0, b[0]))] * 2
            + ([pl.BlockSpec((rows, cols), lambda h, b: (0, 0))] * 2 if wide else [])
            + [ANY] * len(waits),
            out_specs=[pl.BlockSpec((deep, cols), lambda h, b: (0, 0))] * number,
            scratch_shapes=[pltpu.VMEM((rows, cols), jnp.bfloat16)] if wide else [],
        ),
        out_shape=[jax.ShapeDtypeStruct((deep, cols), jnp.bfloat16)] * number,
        compiler_params=params(),
        cost_estimate=lasts(8),
        name="products",
    )(bits, *left, *right, *(arrived if wide else []), *waits)


def products_plain(left, right, arrived):
    total = contract_first(left[0], right[0]) + contract_first(left[1], right[1])
    theirs, mine = halves_of(total, 1, 1)
    if arrived is None:
        return jnp.split(theirs.astype(jnp.bfloat16), 2, axis=0)
    mine = [
        (m + a.astype(jnp.float32)).astype(jnp.bfloat16)
        for m, a in zip(jnp.split(mine, 2, axis=0), arrived)
    ]
    return [cut for w in range(2) for cut in halves_of(mine[w], order_of(w)[1], 0)]


def norm_back(x, gain, grad):
    scale = lax.rsqrt(jnp.mean(x * x, axis=-1, keepdims=True) + 1e-06)
    plain = x * scale
    inner = grad * gain
    by_x = scale * (inner - plain * jnp.mean(inner * plain, axis=-1, keepdims=True))
    return by_x, jnp.sum(grad * plain, axis=0, keepdims=True)


def unwind_kernel(
    length_ref, back_ref, hit0_ref, hit1_ref, picks_ref, kept_ref, hidden_ref, xn_ref, cot_ref,
    router_ref, gain_ref, wout_ref, qkv_ref, bias_ref, *refs
):
    mixed_ref, dhidden_ref, dattn_ref, dqkv_ref, drouter_ref, dgain_ref, dscores_ref, dheads_ref = refs[-8:]
    xn = xn_ref[...]
    hidden = hidden_ref[...]
    grad_out = cot_ref[0].astype(jnp.float32)
    logits = dot(xn, router_ref[...])
    lane = lax.broadcasted_iota(jnp.int32, logits.shape, 1)
    logits = jnp.where(lane < EXPERTS, logits, -1e30)
    weights = jnp.exp(logits - jnp.max(logits, axis=-1, keepdims=True))
    route = weights / jnp.sum(weights, axis=-1, keepdims=True)
    mixed = hidden
    grad_route = jnp.zeros_like(route)
    for k, hit_ref in enumerate((hit0_ref, hit1_ref)):
        pair = sum(dot(hit_ref[m], back_ref[m, 0]) for m in range(back_ref.shape[0]))
        pick = jnp.where(lane == picks_ref[:, k : k + 1], kept_ref[:, k : k + 1], 0.0)
        mixed = mixed + jnp.sum(route * pick, axis=-1, keepdims=True) * pair
        grad_route = grad_route + pick * jnp.sum(grad_out * pair, axis=-1, keepdims=True)
    mixed_ref[...] = mixed.astype(jnp.bfloat16)
    grad_logits = route * (grad_route - jnp.sum(route * grad_route, axis=-1, keepdims=True))
    grad_logits = grad_logits.astype(jnp.bfloat16)
    drouter_ref[...] = contract_first(xn, grad_logits)
    grad_xn = contract_last(grad_logits, router_ref[...]) + sum(
        dot(hit0_ref[m] + hit1_ref[m], back_ref[m, 1]) for m in range(back_ref.shape[0])
    )
    by_hidden, by_gain = norm_back(hidden, gain_ref[...], grad_xn)
    dgain_ref[...] = by_gain
    grad_hidden = grad_out + by_hidden
    dhidden_ref[...] = grad_hidden
    grad_attn = grad_hidden.astype(jnp.bfloat16)
    dattn_ref[...] = grad_attn
    dheads_ref[...] = contract_last(grad_attn, wout_ref[...]).astype(jnp.bfloat16)
    allowed = allowed_pairs(length_ref[0])
    scale = HEAD_DIM ** (-0.5)
    for pair in range(HEADS // 2):
        outs = [[], [], []]
        for head in (2 * pair, 2 * pair + 1):
            at = head * HEAD_DIM
            query = qkv_ref[:, at : at + HEAD_DIM]
            key = qkv_ref[:, D + at : D + at + HEAD_DIM]
            value = qkv_ref[:, 2 * D + at : 2 * D + at + HEAD_DIM]
            grad_head = dheads_ref[:, at : at + HEAD_DIM]
            scores = contract_last(key, query)
            scores = jnp.where(allowed, scores * scale + bias_ref[head].astype(jnp.float32), -1e30)
            weights = jnp.exp(scores - jnp.max(scores, axis=0, keepdims=True))
            probs = weights / jnp.sum(weights, axis=0, keepdims=True)
            grad_probs = contract_last(value, grad_head)
            grad_scores = probs * (grad_probs - jnp.sum(probs * grad_probs, axis=0, keepdims=True))
            grad_scores = grad_scores.astype(jnp.bfloat16)
            dscores_ref[head] = grad_scores
            outs[0].append(contract_first(grad_scores, key) * scale)
            outs[1].append(dot(grad_scores, query) * scale)
            outs[2].append(dot(probs.astype(jnp.bfloat16), grad_head))
        for i in range(3):
            dqkv_ref[:, i * D + pair * 128 : i * D + (pair + 1) * 128] = jnp.concatenate(
                outs[i], axis=1
            ).astype(jnp.bfloat16)


def unwind(
    micro, length, back, hits, picks, kept, hidden, xn_second, cotangent, router_pad, gain_second,
    out_weight, qkv_rows, bias_full, waits
):
    whole = lambda a: pl.BlockSpec(a.shape, lambda i: (0,) * a.ndim)
    gain_row = gain_second.reshape(1, D)
    ins = [back, hits[0], hits[1], picks, kept, hidden, xn_second, cotangent, router_pad, gain_row, out_weight, qkv_rows, bias_full]
    specs = [whole(a) for a in ins]
    specs[7] = pl.BlockSpec((1, SLOT, D), lambda i: (micro, 0, 0))
    out_shape = [
        jax.ShapeDtypeStruct((SLOT, D), jnp.bfloat16),
        jax.ShapeDtypeStruct((SLOT, D), jnp.float32),
        jax.ShapeDtypeStruct((SLOT, D), jnp.bfloat16),
        jax.ShapeDtypeStruct((SLOT, 3 * D), jnp.bfloat16),
        jax.ShapeDtypeStruct((D, 128), jnp.float32),
        jax.ShapeDtypeStruct((1, D), jnp.float32),
        jax.ShapeDtypeStruct((HEADS, SLOT, SLOT), jnp.bfloat16),
    ]
    return pl.pallas_call(
        unwind_kernel,
        grid=(1,),
        in_specs=[SMEM] + specs + [ANY] * len(waits),
        out_specs=[whole(o) for o in out_shape],
        out_shape=out_shape,
        scratch_shapes=[pltpu.VMEM((SLOT, D), jnp.bfloat16)],
        compiler_params=params(),
        cost_estimate=lasts(17),
        name="unwind",
    )(length.reshape(1), *ins, *waits)


def weights_kernel(groups, wide, bits_ref, xn0, xn1, dqkv0, dqkv1, heads0, heads1, dattn0, dattn1, *refs):
    count = D // groups // 2

    def rows_of(ref):
        return jnp.concatenate(
            [
                ref[:, pl.ds(pl.multiple_of((2 * g + bits_ref[0]) * count, count), count)]
                for g in range(groups)
            ],
            axis=1,
        )

    left = [rows_of(xn0), rows_of(xn1)]
    heads = [rows_of(heads0), rows_of(heads1)]
    half = count // 2
    for part in range(4):
        if part < 3:
            span = slice(part * D, (part + 1) * D)
            total = contract_first(left[0], dqkv0[:, span]) + contract_first(left[1], dqkv1[:, span])
        else:
            total = contract_first(heads[0], dattn0[...]) + contract_first(heads[1], dattn1[...])
        total = total.reshape(groups, count, D)
        which, span = part // 2, slice(part % 2 * D, (part % 2 + 1) * D)
        if not wide:
            refs[-1][which, :, :, span] = total.astype(jnp.bfloat16)
            continue
        total = total + refs[0][which, :, :, span].astype(jnp.float32)
        total_ref = refs[-1]
        total_ref[...] = total.astype(jnp.bfloat16)
        send_ref, keep_ref = refs[-5 + 2 * which : len(refs) - 3 + 2 * which]
        bit = bits_ref[1 + which]
        keep_ref[:, :, span] = total_ref[:, pl.ds(pl.multiple_of(bit * half, half), half)]
        send_ref[:, :, span] = total_ref[:, pl.ds(pl.multiple_of((1 - bit) * half, half), half)]


def weight_grads(groups, xn_all, dqkv, heads, dattn, arrived=None):
    place = lax.axis_index("rep")
    wide = arrived is not None
    core = bit_of(place, 1)
    bits = jnp.stack(
        [core if wide else 1 - core] + [bit_of(place, order_of(w)[1]) for w in range(2)]
    ).astype(jnp.int32)
    count = D // groups // 2
    if count % 128:
        return weight_grads_plain(groups, xn_all, dqkv, heads, dattn, arrived)
    shapes = [(groups, count // 2, 2 * D)] * 4 if wide else [(2, groups, count, 2 * D)]
    return pl.pallas_call(
        functools.partial(weights_kernel, groups, wide),
        in_specs=[SMEM] + [VMEM] * (9 if wide else 8),
        out_specs=[VMEM] * len(shapes),
        out_shape=[jax.ShapeDtypeStruct(shape, jnp.bfloat16) for shape in shapes],
        scratch_shapes=[pltpu.VMEM((groups, count, D), jnp.bfloat16)] if wide else [],
        compiler_params=params(),
        cost_estimate=lasts(6),
        name="weights",
    )(bits, *xn_all, *dqkv, *heads, *dattn, *([arrived] if wide else []))


def weight_grads_plain(groups, xn_all, dqkv, heads, dattn, arrived):
    total = jnp.concatenate(
        [
            contract_first(jnp.concatenate(xn_all, axis=0), jnp.concatenate(dqkv, axis=0)),
            contract_first(jnp.concatenate(heads, axis=0), jnp.concatenate(dattn, axis=0)),
        ],
        axis=1,
    ).reshape(groups, D // groups, 4 * D)
    theirs, mine = halves_of(total, 1, 1)
    if arrived is None:
        return [jnp.stack(jnp.split(theirs.astype(jnp.bfloat16), 2, axis=2))]
    mine = [
        (m + a.astype(jnp.float32)).astype(jnp.bfloat16)
        for m, a in zip(jnp.split(mine, 2, axis=2), arrived)
    ]
    return [cut for w in range(2) for cut in halves_of(mine[w], order_of(w)[1], 1)]


def finish_kernel(tokens_ref, gain_ref, wqkv_ref, dqkv0, dqkv1, dhidden0, dhidden1, out_ref, dgain_ref):
    total = None
    for micro, (dqkv, dhidden) in enumerate(((dqkv0, dhidden0), (dqkv1, dhidden1))):
        grad = contract_last(dqkv[...], wqkv_ref[...])
        by_x, by_gain = norm_back(tokens_ref[micro].astype(jnp.float32), gain_ref[...], grad)
        out_ref[micro] = dhidden[...] + by_x
        total = by_gain if total is None else total + by_gain
    dgain_ref[...] = total


def finish(tokens, gain_first, qkv_weight, dqkv, dhidden):
    return pl.pallas_call(
        finish_kernel,
        in_specs=[VMEM] * 7,
        out_specs=[VMEM] * 2,
        out_shape=[
            jax.ShapeDtypeStruct((MICRO, SLOT, D), jnp.float32),
            jax.ShapeDtypeStruct((1, D), jnp.float32),
        ],
        compiler_params=params(),
        cost_estimate=lasts(10),
        name="finish",
    )(tokens, gain_first.reshape(1, D), qkv_weight, *dqkv, *dhidden)


def join_small(by_distance, router, gains, rel_bias):
    groups = lax.axis_size("grp")
    place = lax.axis_index("grp")
    a, b = router.size, router.size + gains.size
    size = b + rel_bias.size
    blocks = [by_distance[m][:size].astype(jnp.float32) for m in range(groups)]
    rows = []
    for at in range(groups):
        row = blocks[0]
        for m in range(1, groups):
            row = jnp.where(place ^ m == at, blocks[m], row)
        rows.append(row)
    every = jnp.stack(rows)
    return (
        every[:, :a].reshape(-1, router.shape[1]).astype(jnp.bfloat16),
        every[:, a:b].reshape(-1, gains.shape[1]),
        every[:, b:].reshape(-1, rel_bias.shape[1]),
    )


def per_device(
    tokens,
    w_qkv,
    w_out,
    router,
    gains,
    rel_bias,
    w_gate,
    w_up,
    w_down,
    lengths,
    choices,
    priority,
    cotangent,
):
    groups = lax.axis_size("grp")
    split_count = groups // EXPERTS
    place = lax.axis_index("grp")
    my_expert = place // split_count
    small = jnp.concatenate([router.reshape(-1), gains.reshape(-1), rel_bias.reshape(-1)])
    chains, came_along = gather_weights(w_qkv, w_out, small)
    after = [chains[1][1][0][1]]
    router_weight, gain_full, bias_table = join_small(came_along, router, gains, rel_bias)
    router_pad = jnp.pad(router_weight, ((0, 0), (0, 128 - EXPERTS)))
    bucket_hits = (
        jnp.asarray(np.ascontiguousarray(bucket_matrix().T))[:, :, None] == jnp.arange(BUCKETS)[None, None, :]
    ).astype(jnp.bfloat16)
    bias_full = jnp.einsum(
        "hk,ijk->hij", bias_table.astype(jnp.bfloat16), bucket_hits, preferred_element_type=jnp.float32
    ).astype(jnp.bfloat16)

    target = (
        (jnp.arange(groups) // split_count)[:, None] * CAP + jnp.arange(CAP)[None, :]
    ).reshape(-1)
    routes = []
    for micro in range(MICRO):
        _, kept_mask, slot_index = expert_slots(choices[micro], priority[micro], lengths[micro, 0])
        hits = [
            (slot_index[None, :, k, None] == target.reshape(groups, 1, CAP)).astype(jnp.bfloat16)
            for k in range(2)
        ]
        spots = (
            (target[:, None] == slot_index[None, :, 0]) | (target[:, None] == slot_index[None, :, 1])
        ).astype(jnp.bfloat16)
        routes.append([kept_mask, hits, spots])
    spots1 = routes[1][2]
    pieces = gather_cores(chains, bias_full, router_pad, gain_full, spots1)
    for micro in range(MICRO):
        spots = routes[micro][2]
        (sent,) = tie([cotangent[micro]], *after)
        blocks = dot(spots, sent).astype(jnp.bfloat16).reshape(groups, CAP, D)
        routes[micro][2] = spots.reshape(groups, CAP, SLOT)
        routes[micro].append(to_experts(blocks).reshape(groups * CAP, D))
        after = [bias_full, router_pad, *[block for _, held in chains for _, block in held]]

    xn0, qkv0, out_weight = project(0, tokens, gain_full[:, 0], pieces, [routes[0][-1], bias_full, router_pad])

    def attended(micro, qkv_rows, waits):
        return attend(
            micro, lengths[micro], qkv_rows, tokens, bias_full, out_weight, gain_full[:, 1], routes[micro][2], waits
        )

    forward = [attended(0, qkv0, [])]
    rows0 = to_experts(forward[0][3]).reshape(groups * CAP, D)
    xn1, qkv1, qkv_weight = project(1, tokens, gain_full[:, 0], pieces, [forward[0][0], routes[1][-1]])
    forward.append(attended(1, qkv1, []))
    xn_all, qkv_all = [xn0, xn1], [qkv0, qkv1]
    blocks1, _ = tie([forward[1][3], rows0])
    rows = [rows0, to_experts(blocks1).reshape(groups * CAP, D)]

    def expert(micro, waits):
        return run_expert(
            my_expert, rows[micro], routes[micro][-1], router_pad, w_gate, w_up, w_down, waits
        )

    inner = [expert(0, [qkv_weight])]
    home0 = to_experts(inner[0][4])
    inner.append(expert(1, [inner[0][0]]))
    home1 = to_experts(inner[1][4])
    doutput, act, dgate, dup = ([inner[micro][i] for micro in range(MICRO)] for i in range(4))

    def launch(left, right, waits):
        theirs = products(left, right, None, waits)
        return theirs[0], [exchange(half, "rep", 1) for half in theirs]

    def settle(left, right, arrived, waits):
        outs = products(left, right, arrived, waits)
        pair = [Halving(w, 0) for w in range(2)]
        for w in range(2):
            pair[w].start(outs[2 * w], outs[2 * w + 1], 1)
        return pair, outs[1]

    def unwound(micro, home, waits):
        kept_mask, hits, _, _ = routes[micro]
        heads, hidden, xn_second, _ = forward[micro]
        return unwind(
            micro, lengths[micro], home, hits, choices[micro], kept_mask, hidden, xn_second, cotangent,
            router_pad, gain_full[:, 1], out_weight, qkv_all[micro], bias_full, waits,
        )

    tok, down_came = launch(act, doutput, [])
    tok, gate_came = launch(rows, dgate, [tok])
    down, tok = settle(act, doutput, down_came, [tok, home0])
    tok, up_came = launch(rows, dup, [tok])
    gate, tok = settle(rows, dgate, gate_came, [tok])
    land(down, tok)
    for half in down:
        half.halve(2)
    up, tok = settle(rows, dup, up_came, [half.kept for half in down])
    land([*gate, *down], tok)
    for half in gate:
        half.halve(2)
    for half in down:
        half.own()
        half.back()
    un0 = unwound(0, home0, [half.kept for half in (*gate, *down)])
    land([*up, *down, *gate], un0[0])
    for half in up:
        half.halve(2)
    for half in down:
        half.back_pair()
    for half in gate:
        half.own()
    un1 = unwound(1, home1, [half.kept for half in (*up, *down, *gate)])
    un = (un0, un1)

    def attention_grads(xn_in, arrived=None):
        return weight_grads(
            groups, xn_in, [u[3] for u in un], [forward[m][0] for m in range(MICRO)], [u[2] for u in un], arrived
        )

    (theirs,) = attention_grads(xn_all)
    land([*up, *down], theirs)
    came = exchange(tie([theirs], up[0].kept)[0], "rep", 1)
    for half in up:
        half.own()
        half.back()
    for half in gate:
        half.back()
    dscores = tie([u[6] for u in un], *[half.kept for half in up])
    bias_grad = sum(
        jnp.einsum("hij,ijk->hk", d, bucket_hits, preferred_element_type=jnp.float32) for d in dscores
    )
    outs = attention_grads(tie(xn_all, bias_grad, *[half.kept for half in (*up, *gate)]), came)
    attn = [Halving(w, 1) for w in range(2)]
    for w in range(2):
        attn[w].start(outs[2 * w], outs[2 * w + 1], 1)
    land([*up, *gate, *down], outs[0])
    down_own, down_got = swap_cores(down)
    token_grads, dgain_first = finish(
        tie([tokens], down_own)[0], gain_full[:, 0], qkv_weight, [u[3] for u in un], [u[1] for u in un]
    )

    small = [
        (un0[4] + un1[4])[:, :EXPERTS].reshape(-1),
        jnp.stack([dgain_first[0], un0[5][0] + un1[5][0]], axis=1).reshape(-1),
        bias_grad.reshape(-1),
    ]
    flat = jnp.concatenate(small)
    flat = jnp.pad(flat, (0, -flat.size % 1024)).reshape(-1, 128)
    steps = [("rep", m) for m in masks_of(lax.axis_size("rep"))] + [("grp", m) for m in masks_of(groups)]
    small_sum = Halving(0, 0)
    small_sum.kept = flat

    def add_small():
        if small_sum.moving is not None:
            small_sum.kept, small_sum.moving = small_sum.kept + small_sum.moving, None
        if steps:
            small_sum.moving = exchange(small_sum.kept, *steps.pop(0))

    add_small()
    down_grad = assemble(down, *tie([down_own, down_got], small_sum.kept))
    land([*attn, small_sum], down_grad)
    for half in attn:
        half.halve(2)
    add_small()
    land([*attn, small_sum])
    for half in attn:
        half.own()
    zsum = Halving(0, 0)
    zsum.kept = to_experts(jnp.stack([half.kept for half in attn], axis=1))
    for half in (*gate, *up):
        half.kept, half.moving = tie([half.kept, half.moving], *[a.kept for a in attn])
        half.back_pair()
    add_small()
    land([zsum, *gate, *up, small_sum])
    total = jnp.sum(zsum.kept.astype(jnp.float32), axis=0).astype(jnp.bfloat16)
    for w in range(2):
        attn[w].kept = total[w]
        attn[w].back()
    land([*gate, *up], total)
    gate_own, gate_got = swap_cores(gate)
    add_small()
    land([*attn, small_sum], gate_own)
    for half in attn:
        half.back_pair()
    land(up, attn[0].kept)
    up_own, up_got = swap_cores(up)
    gate_grad = assemble(gate, *tie([gate_own, gate_got], up_own))
    add_small()
    land([*attn, small_sum], gate_grad)
    attn_own, attn_got = swap_cores(attn)
    up_grad = assemble(up, *tie([up_own, up_got], attn_own))
    while small_sum.moving is not None:
        add_small()
    flat = small_sum.kept
    qkv_grad, out_grad = assemble_attention(attn, *tie([attn_own, attn_got], up_grad))

    flat = flat.reshape(-1)
    outs = []
    start = 0
    for whole in ((D, EXPERTS), (D, 2), (HEADS, BUCKETS)):
        size = whole[0] * whole[1]
        rows_here = whole[0] // groups
        outs.append(
            lax.dynamic_slice_in_dim(
                flat[start : start + size].reshape(whole), place * rows_here, rows_here, 0
            )
        )
        start += size
    return (
        jnp.stack([u[0] for u in un]),
        token_grads,
        qkv_grad,
        out_grad,
        outs[0],
        outs[1],
        outs[2],
        gate_grad[None],
        up_grad[None],
        down_grad[None],
    )


def solution(mesh):
    placed = (
        P(None, ("rep", "grp"), None),
        P("grp", None),
        P("grp", None),
        P("grp", None),
        P("grp", None),
        P("grp", None),
        P("grp", None, None),
        P("grp", None, None),
        P("grp", None, None),
        P(None, ("rep", "grp")),
        P(None, ("rep", "grp"), None),
        P(None, ("rep", "grp")),
        P(None, ("rep", "grp"), None),
    )
    return jax.shard_map(
        per_device,
        mesh=mesh,
        in_specs=placed,
        out_specs=(
            P(None, ("rep", "grp"), None),
            P(None, ("rep", "grp"), None),
            P("grp", None),
            P("grp", None),
            P("grp", None),
            P("grp", None),
            P("grp", None),
            P("grp", None, None),
            P("grp", None, None),
            P("grp", None, None),
        ),
        check_vma=False,
    )
```

```python
import functools

import jax
import jax.numpy as jnp
import numpy as np
from jax import lax
from jax.experimental import pallas as pl
from jax.experimental.pallas import tpu as pltpu
from jax.sharding import PartitionSpec as P

D = 1024
HEADS = 16
HEAD_DIM = 64
EXPERTS = 4
BUCKETS = 32
MAX_DIST = 128
MICRO = 2
SLOT = 192
CAP = 120
VMEM_LIMIT = 56 * 1024 * 1024
PART = 0.001


def lasts(us):
    return pl.CostEstimate(flops=int(us * PART * 1.15e9), bytes_accessed=1, transcendentals=0)


VMEM = pl.BlockSpec(memory_space=pltpu.VMEM)
SMEM = pl.BlockSpec(memory_space=pltpu.SMEM)
ANY = pl.BlockSpec(memory_space=pl.ANY)


def params():
    return pltpu.CompilerParams(vmem_limit_bytes=VMEM_LIMIT)


def bucket_matrix():
    distance = np.arange(SLOT)
    exact_count = BUCKETS // 2
    safe_span = np.maximum(distance, 1) / exact_count
    log_bucket = exact_count + np.floor(
        np.log(safe_span) / np.log(MAX_DIST / exact_count) * (BUCKETS - exact_count)
    ).astype(np.int32)
    bucket_of = np.where(distance < exact_count, distance, np.minimum(log_bucket, BUCKETS - 1))
    offsets = np.maximum(distance[:, None] - distance[None, :], 0)
    return bucket_of[offsets].astype(np.int32)


def dot(left, right):
    return jnp.dot(left, right, preferred_element_type=jnp.float32)


def contract_last(left, right):
    return lax.dot_general(
        left, right, (((1,), (1,)), ((), ())), preferred_element_type=jnp.float32
    )


def contract_first(left, right):
    return lax.dot_general(
        left, right, (((0,), (0,)), ((), ())), preferred_element_type=jnp.float32
    )


def expert_slots(expert_pick, priority_row, length):
    live_mask = (jnp.arange(SLOT) < length).astype(jnp.float32)
    pick_hits = (expert_pick[:, :, None] == jnp.arange(EXPERTS)[None, None, :]).astype(jnp.float32)
    expert_hits = jnp.sum(pick_hits, axis=1) * live_mask[:, None]
    before = (priority_row[None, :] < priority_row[:, None]).astype(jnp.bfloat16)
    ahead_count = dot(before, expert_hits.astype(jnp.bfloat16))
    place_pos = jnp.sum(pick_hits * ahead_count[:, None, :], axis=2)
    kept_mask = live_mask[:, None] * (place_pos < CAP - 0.5).astype(jnp.float32)
    slot_index = jnp.where(
        kept_mask > 0.5, expert_pick * CAP + place_pos.astype(jnp.int32), EXPERTS * CAP
    )
    return (pick_hits, kept_mask, slot_index)


def exchange(block, axis, mask):
    return lax.ppermute(block, axis, [(i, i ^ mask) for i in range(lax.axis_size(axis))])


def masks_of(count):
    return [1 << bit for bit in range(count.bit_length() - 1)]


def spread(own, axis, masks):
    held = [(0, own)]
    for mask in masks:
        held += [(far ^ mask, exchange(block, axis, mask)) for far, block in held]
    return held


def to_experts(blocks):
    return lax.all_to_all(blocks, "grp", split_axis=0, concat_axis=0, tiled=True)


def bit_of(index, mask):
    return (index & mask) // mask


def tie(values, *after):
    return lax.optimization_barrier((tuple(values), after))[0]


def rep_masks():
    masks = masks_of(lax.axis_size("rep"))
    return masks[3:], masks[:3]


def order_of(which):
    masks = rep_masks()[1]
    return masks[:1] + (masks[1:] if which == 0 else masks[:0:-1])


def halves_of(block, mask, dim):
    half = block.shape[dim] // 2
    bit = bit_of(lax.axis_index("rep"), mask)
    return (
        lax.dynamic_slice_in_dim(block, (1 - bit) * half, half, dim),
        lax.dynamic_slice_in_dim(block, bit * half, half, dim),
    )


def add_low(left, right):
    return (left.astype(jnp.float32) + right.astype(jnp.float32)).astype(jnp.bfloat16)


class Halving:
    def __init__(self, which, dim):
        self.which, self.dim = which, dim
        self.masks = order_of(which)
        self.kept = self.moving = None
        self.held = None

    def start(self, send, keep, at):
        self.kept, self.moving = keep, exchange(send, "rep", self.masks[at])

    def halve(self, at):
        kept, got = (halves_of(x, self.masks[at], self.dim) for x in (self.kept, self.moving))
        self.start(*(add_low(k, g) for k, g in zip(kept, got)), at)

    def own(self):
        total = add_low(self.kept, self.moving)
        for mask in rep_masks()[0]:
            total = add_low(total, exchange(total, "rep", mask))
        self.kept, self.moving = total, None

    def back(self):
        self.moving = exchange(self.kept, "rep", self.masks[-1])

    def back_pair(self):
        self.kept = jnp.stack([self.kept, self.moving])
        self.moving = exchange(self.kept, "rep", self.masks[-2])

    def place(self):
        index = 0
        for mask in self.masks:
            index = 2 * index + bit_of(lax.axis_index("rep"), mask)
        return index


def land(halvings, *after):
    flat = [x for h in halvings for x in (h.kept, h.moving) if x is not None]
    flat = list(tie(flat, *after))
    for h in halvings:
        h.kept = flat.pop(0)
        if h.moving is not None:
            h.moving = flat.pop(0)


def swap_cores(pair):
    own = jnp.concatenate([x for h in pair for x in (h.kept, h.moving)], axis=0)
    return own, exchange(own, "rep", 1)


def assemble(pair_of_halves, own, got):
    places = jnp.stack([half.place() for half in pair_of_halves]).astype(jnp.int32)
    pieces, rows, cols = own.shape
    deep = pieces // 4
    cut_cores = cols % 128 != 0

    def body(place_ref, own_ref, got_ref, out_ref):
        half, core, step = (pl.program_id(i) for i in range(3))
        place = place_ref[half]
        far = (core * deep + step) ^ (place // 2)
        out = out_ref.at[0] if cut_cores else out_ref
        for other, ref in enumerate((own_ref, got_ref)):

            @pl.when(far // deep == other)
            def _():
                out[:rows] = ref[place % 2].astype(jnp.float32)
                out[rows:] = ref[1 - place % 2].astype(jnp.float32)

    def pair_spec(other):
        def index(half, core, step, place_ref):
            base = place_ref[half] // 2
            far = (core * deep + step) ^ base
            chosen = far // deep == other
            return (half * deep + jnp.where(chosen, far, base) % deep, 0, 0)

        return pl.BlockSpec((2, rows, cols), index)

    out_shape = (4 * deep * rows, 2 * cols)
    out_spec = pl.BlockSpec(
        (2 * rows, cols), lambda half, core, step, place_ref: (half * deep + step, core)
    )
    if cut_cores:
        out_shape = (2, 4 * deep * rows, cols)
        out_spec = pl.BlockSpec(
            (1, 2 * rows, cols), lambda half, core, step, place_ref: (core, half * deep + step, 0)
        )
    out = pl.pallas_call(
        body,
        grid_spec=pltpu.PrefetchScalarGridSpec(
            num_scalar_prefetch=1,
            grid=(2, 2, deep),
            in_specs=[pair_spec(0), pair_spec(1)],
            out_specs=out_spec,
        ),
        out_shape=jax.ShapeDtypeStruct(out_shape, jnp.float32),
        compiler_params=params(),
        cost_estimate=lasts(9),
        name="assemble",
    )(places, own, got)
    return jnp.concatenate([out[0], out[1]], axis=1) if cut_cores else out


def assemble_attention(pair_of_halves, own, got):
    places = jnp.stack([half.place() for half in pair_of_halves]).astype(jnp.int32)
    pieces, rows, _ = own.shape
    each = pieces // 2

    def body(place_ref, own_ref, got_ref, qkv_ref, out_ref):
        for other, ref in enumerate((own_ref, got_ref)):
            for at in range(pieces):
                where = (other * each + at % each) ^ place_ref[at // each]
                span = pl.ds(pl.multiple_of(where * rows, rows), rows)
                values = ref[at].astype(jnp.float32)
                if at < each:
                    qkv_ref[span, : 2 * D] = values
                else:
                    qkv_ref[span, 2 * D :] = values[:, :D]
                    out_ref[span, :] = values[:, D:]

    depth = 2 * each * rows
    return pl.pallas_call(
        body,
        in_specs=[SMEM] + [VMEM] * 2,
        out_specs=[VMEM] * 2,
        out_shape=[
            jax.ShapeDtypeStruct((depth, 3 * D), jnp.float32),
            jax.ShapeDtypeStruct((depth, D), jnp.float32),
        ],
        compiler_params=params(),
        cost_estimate=lasts(4),
        name="assemble_attention",
    )(places, own, got)


def gather_weights(w_qkv, w_out, small):
    slices = min(lax.axis_size("rep"), 8)
    eighth = lax.axis_index("rep") % slices
    width = D // slices
    parts = [w_qkv[:, i * D : (i + 1) * D] for i in range(3)] + [w_out]
    own = jnp.concatenate(
        [lax.dynamic_slice_in_dim(part, eighth * width, width, 1) for part in parts], axis=1
    )
    depth = own.shape[0]
    small = small.reshape(-1)
    lines = -(-small.size // (16 * own.shape[1])) * 16
    small = jnp.pad(small, (0, lines * own.shape[1] - small.size)).reshape(lines, -1)
    masks = masks_of(slices)
    held = spread(jnp.concatenate([own, small]), "grp", masks_of(lax.axis_size("grp"))[::-1])
    over_grp = [(m, block[:depth]) for m, block in held]
    half = len(over_grp) // 2
    chains = []
    for which in range(2):
        mine = over_grp[which * half : (which + 1) * half]
        order = masks[1:] if which == 0 else masks[:0:-1]
        block = jnp.stack([piece for _, piece in mine])
        chains.append(([m for m, _ in mine], spread(block, "rep", order)))
    return chains, {m: block[depth:].reshape(-1) for m, block in held}


def gather_cores(chains, *after):
    pieces = []
    for members, held in chains:
        blocks = tie([block for _, block in held], *after)
        for (far, _), block in zip(held, blocks):
            pieces += [(far, members, block), (far ^ 1, members, exchange(block, "rep", 1))]
    return pieces


def norm_rows(x, gain):
    return x * lax.rsqrt(jnp.mean(x * x, axis=-1, keepdims=True) + 1e-06) * gain


def each_piece(plan, pieces, far):
    for (this, members), piece in zip(plan, pieces):
        if this == far:
            yield from ((m, piece, at) for at, m in enumerate(members))


def project_kernel(plan, micro, place_ref, tokens_ref, gain_ref, *refs):
    pieces = refs[: len(plan)]
    xn_ref, qkv_ref, weight_ref = refs[-3:]
    depth = pieces[0].shape[1]
    width = pieces[0].shape[2] // 4
    xn_ref[...] = norm_rows(tokens_ref[0].astype(jnp.float32), gain_ref[...]).astype(jnp.bfloat16)
    for far in sorted({far for far, _ in plan}):
        column = pl.multiple_of((place_ref[0] ^ far) * width, width)
        total = None
        for m, piece, at in each_piece(plan, pieces, far):
            row = pl.multiple_of((place_ref[1] ^ m) * depth, depth)
            if micro == 0:
                weight_ref[pl.ds(row, depth), pl.ds(column, width)] = piece[at, :, 3 * width :]
            else:
                for part in range(3):
                    weight_ref[pl.ds(row, depth), pl.ds(column + part * D, width)] = piece[
                        at, :, part * width : (part + 1) * width
                    ]
            term = dot(xn_ref[:, pl.ds(row, depth)], piece[at, :, : 3 * width])
            total = term if total is None else total + term
        for part in range(3):
            low = total[:, part * width : (part + 1) * width].astype(jnp.bfloat16)
            qkv_ref[:, pl.ds(column + part * D, width)] = low


def places_of():
    slices = min(lax.axis_size("rep"), 8)
    return jnp.stack([lax.axis_index("rep") % slices, lax.axis_index("grp")]).astype(jnp.int32)


def project(micro, tokens, gain_first, pieces, waits):
    plan = [(far, m) for far, m, _ in pieces]
    whole = lambda *shape: pl.BlockSpec(shape, lambda i: (0,) * len(shape))
    out_shape = [
        jax.ShapeDtypeStruct(shape, jnp.bfloat16)
        for shape in ((SLOT, D), (SLOT, 3 * D), (D, 3 * D if micro else D))
    ]
    return pl.pallas_call(
        functools.partial(project_kernel, plan, micro),
        grid=(1,),
        in_specs=[SMEM, pl.BlockSpec((1, SLOT, D), lambda i: (micro, 0, 0)), whole(1, D)]
        + [whole(*piece.shape) for _, _, piece in pieces]
        + [ANY] * len(waits),
        out_specs=[whole(*o.shape) for o in out_shape],
        out_shape=out_shape,
        compiler_params=params(),
        cost_estimate=lasts(10),
        name="project",
    )(places_of(), tokens, gain_first.reshape(1, D), *[piece for _, _, piece in pieces], *waits)


def allowed_pairs(length):
    row = lax.broadcasted_iota(jnp.int32, (SLOT, SLOT), 0)
    column = lax.broadcasted_iota(jnp.int32, (SLOT, SLOT), 1)
    return (row <= column) & (row < length)


def attend_kernel(groups, length_ref, qkv_ref, tokens_ref, bias_ref, wout_ref, gain_ref, spots_ref, *refs):
    heads_ref, hidden_ref, xn_ref, rows_ref = refs[-4:]
    allowed = allowed_pairs(length_ref[0])
    scale = HEAD_DIM ** (-0.5)
    for pair in range(HEADS // 2):
        outs = []
        for head in (2 * pair, 2 * pair + 1):
            at = head * HEAD_DIM
            scores = contract_last(
                qkv_ref[:, D + at : D + at + HEAD_DIM], qkv_ref[:, at : at + HEAD_DIM]
            )
            scores = jnp.where(allowed, scores * scale + bias_ref[head].astype(jnp.float32), -1e30)
            weights = jnp.exp(scores - jnp.max(scores, axis=0, keepdims=True))
            probs = weights / jnp.sum(weights, axis=0, keepdims=True)
            outs.append(
                contract_first(probs.astype(jnp.bfloat16), qkv_ref[:, 2 * D + at : 2 * D + at + HEAD_DIM])
            )
        heads_ref[:, pair * 128 : (pair + 1) * 128] = jnp.concatenate(outs, axis=1).astype(jnp.bfloat16)
    hidden = tokens_ref[0].astype(jnp.float32) + dot(heads_ref[...], wout_ref[...])
    hidden_ref[...] = hidden
    xn = norm_rows(hidden, gain_ref[...]).astype(jnp.bfloat16)
    xn_ref[...] = xn
    for m in range(groups):
        rows_ref[m] = dot(spots_ref[m], xn).astype(jnp.bfloat16)


def attend(micro, length, qkv_rows, tokens, bias_full, out_weight, gain_second, spots, waits):
    groups = spots.shape[0]
    whole = lambda *shape: pl.BlockSpec(shape, lambda i: (0,) * len(shape))
    low = jax.ShapeDtypeStruct((SLOT, D), jnp.bfloat16)
    out_shape = [
        low,
        jax.ShapeDtypeStruct((SLOT, D), jnp.float32),
        low,
        jax.ShapeDtypeStruct((groups, CAP, D), jnp.bfloat16),
    ]
    return pl.pallas_call(
        functools.partial(attend_kernel, groups),
        grid=(1,),
        in_specs=[
            SMEM,
            whole(SLOT, 3 * D),
            pl.BlockSpec((1, SLOT, D), lambda i: (micro, 0, 0)),
            whole(HEADS, SLOT, SLOT),
            whole(D, D),
            whole(1, D),
            whole(groups, CAP, SLOT),
        ]
        + [ANY] * len(waits),
        out_specs=[whole(*o.shape) for o in out_shape],
        out_shape=out_shape,
        compiler_params=params(),
        cost_estimate=lasts(9.3),
        name="attend",
    )(length.reshape(1), qkv_rows, tokens, bias_full, out_weight, gain_second.reshape(1, D), spots, *waits)


def gelu_parts(v):
    c = np.float32(np.sqrt(2 / np.pi))
    t = jnp.tanh(c * (v + np.float32(0.044715) * (v * v * v)))
    half = 0.5 * (1.0 + t)
    slope = half + 0.5 * v * (1.0 - t * t) * (c * (1.0 + np.float32(3 * 0.044715) * (v * v)))
    return v * half, slope


def expert_kernel(groups, chunk, expert_ref, rows_ref, grads_ref, router_ref, wg_hbm, wu_hbm, wd_hbm, *refs):
    dout_ref, act_hbm, dgate_hbm, dup_hbm, back_ref = refs[-13:-8]
    wg, wu, wd, act, dgate, dup, came, went = refs[-8:]
    hidden = act.shape[1]
    steps = hidden // chunk

    def incoming(c):
        span = pl.ds(pl.multiple_of(c * chunk, chunk), chunk)
        return [
            pltpu.make_async_copy(wg_hbm.at[0, :, span], wg.at[:, span], came.at[0, c]),
            pltpu.make_async_copy(wu_hbm.at[0, :, span], wu.at[:, span], came.at[1, c]),
            pltpu.make_async_copy(wd_hbm.at[0, span, :], wd.at[span, :], came.at[2, c]),
        ]

    def outgoing(c):
        span = pl.ds(pl.multiple_of(c * chunk, chunk), chunk)
        return [
            pltpu.make_async_copy(vmem.at[:, span], hbm.at[:, span], went.at[i, c])
            for i, (vmem, hbm) in enumerate(((act, act_hbm), (dgate, dgate_hbm), (dup, dup_hbm)))
        ]

    @pl.loop(0, steps)
    def _(c):
        for copy in incoming(c):
            copy.start()

    logits = dot(rows_ref[...], router_ref[...])
    lane = lax.broadcasted_iota(jnp.int32, logits.shape, 1)
    logits = jnp.where(lane < EXPERTS, logits, -1e30)
    weights = jnp.exp(logits - jnp.max(logits, axis=-1, keepdims=True))
    route = weights / jnp.sum(weights, axis=-1, keepdims=True)
    gate = jnp.sum(jnp.where(lane == expert_ref[0], route, 0.0), axis=-1, keepdims=True)
    dout_ref[...] = (gate * grads_ref[...].astype(jnp.float32)).astype(jnp.bfloat16)

    @pl.loop(0, steps)
    def _(c):
        span = pl.ds(pl.multiple_of(c * chunk, chunk), chunk)
        for copy in incoming(c):
            copy.wait()
        gate_pre = dot(rows_ref[...], wg[:, span])
        up_pre = dot(rows_ref[...], wu[:, span])
        gelu, slope = gelu_parts(gate_pre)
        act[:, span] = (gelu * up_pre).astype(jnp.bfloat16)
        grad_act = contract_last(dout_ref[...], wd[span, :])
        dgate[:, span] = (grad_act * up_pre * slope).astype(jnp.bfloat16)
        dup[:, span] = (grad_act * gelu).astype(jnp.bfloat16)
        for copy in outgoing(c):
            copy.start()

    part = dot(act[...], wd[...])
    for m in range(groups):
        back_ref[m, 0] = part[m * CAP : (m + 1) * CAP].astype(jnp.bfloat16)
    grad_rows = contract_last(dgate[...], wg[...]) + contract_last(dup[...], wu[...])
    for m in range(groups):
        back_ref[m, 1] = grad_rows[m * CAP : (m + 1) * CAP].astype(jnp.bfloat16)

    @pl.loop(0, steps)
    def _(c):
        for copy in outgoing(c):
            copy.wait()


def run_expert(expert, rows, grad_rows, router_pad, w_gate, w_up, w_down, waits):
    count = rows.shape[0]
    groups = count // CAP
    hidden = w_gate.shape[2]
    chunk = 256 if hidden % 256 == 0 else 128
    steps = hidden // chunk
    wide = jax.ShapeDtypeStruct((count, hidden), jnp.bfloat16)
    low = lambda *shape: pltpu.VMEM(shape, jnp.bfloat16)
    return pl.pallas_call(
        functools.partial(expert_kernel, groups, chunk),
        in_specs=[SMEM] + [VMEM] * 3 + [ANY] * (3 + len(waits)),
        out_specs=[VMEM] + [ANY] * 3 + [VMEM],
        out_shape=[
            jax.ShapeDtypeStruct((count, D), jnp.bfloat16),
            wide,
            wide,
            wide,
            jax.ShapeDtypeStruct((groups, 2, CAP, D), jnp.bfloat16),
        ],
        scratch_shapes=[
            low(D, hidden),
            low(D, hidden),
            low(hidden, D),
            low(count, hidden),
            low(count, hidden),
            low(count, hidden),
            pltpu.SemaphoreType.DMA((3, steps)),
            pltpu.SemaphoreType.DMA((3, steps)),
        ],
        compiler_params=params(),
        cost_estimate=lasts(22),
        name="expert",
    )(jnp.reshape(expert, (1,)).astype(jnp.int32), rows, grad_rows, router_pad, w_gate, w_up, w_down, *waits)


def products_kernel(wide, bits_ref, left0, left1, right0, right1, *refs):
    total = contract_first(left0[...], right0[...]) + contract_first(left1[...], right1[...])
    for which in range(2):

        @pl.when(pl.program_id(0) == which)
        def _():
            if not wide:
                refs[which - 2][...] = total.astype(jnp.bfloat16)
                return
            total_ref = refs[-1]
            total_ref[...] = (total + refs[which][...].astype(jnp.float32)).astype(jnp.bfloat16)
            send_ref, keep_ref = refs[-5 + 2 * which : len(refs) - 3 + 2 * which]
            bit = bits_ref[1 + which]
            half = send_ref.shape[0]
            keep_ref[...] = total_ref[pl.ds(pl.multiple_of(bit * half, half), half)]
            send_ref[...] = total_ref[pl.ds(pl.multiple_of((1 - bit) * half, half), half)]


def products(left, right, arrived=None, waits=()):
    place = lax.axis_index("rep")
    wide = arrived is not None
    core = bit_of(place, 1)
    bits = jnp.stack(
        [core if wide else 1 - core] + [bit_of(place, order_of(w)[1]) for w in range(2)]
    ).astype(jnp.int32)
    count = left[0].shape[0]
    rows, cols = left[0].shape[1] // 2, right[0].shape[1] // 2
    if rows % 128 or cols % 128:
        return products_plain(left, right, arrived)
    deep, number = (rows // 2, 4) if wide else (rows, 2)
    return pl.pallas_call(
        functools.partial(products_kernel, wide),
        grid_spec=pltpu.PrefetchScalarGridSpec(
            num_scalar_prefetch=1,
            grid=(2,),
            in_specs=[pl.BlockSpec((count, rows), lambda h, b: (0, h))] * 2
            + [pl.BlockSpec((count, cols), lambda h, b: (0, b[0]))] * 2
            + ([pl.BlockSpec((rows, cols), lambda h, b: (0, 0))] * 2 if wide else [])
            + [ANY] * len(waits),
            out_specs=[pl.BlockSpec((deep, cols), lambda h, b: (0, 0))] * number,
            scratch_shapes=[pltpu.VMEM((rows, cols), jnp.bfloat16)] if wide else [],
        ),
        out_shape=[jax.ShapeDtypeStruct((deep, cols), jnp.bfloat16)] * number,
        compiler_params=params(),
        cost_estimate=lasts(8),
        name="products",
    )(bits, *left, *right, *(arrived if wide else []), *waits)


def products_plain(left, right, arrived):
    total = contract_first(left[0], right[0]) + contract_first(left[1], right[1])
    theirs, mine = halves_of(total, 1, 1)
    if arrived is None:
        return jnp.split(theirs.astype(jnp.bfloat16), 2, axis=0)
    mine = [
        (m + a.astype(jnp.float32)).astype(jnp.bfloat16)
        for m, a in zip(jnp.split(mine, 2, axis=0), arrived)
    ]
    return [cut for w in range(2) for cut in halves_of(mine[w], order_of(w)[1], 0)]


def norm_back(x, gain, grad):
    scale = lax.rsqrt(jnp.mean(x * x, axis=-1, keepdims=True) + 1e-06)
    plain = x * scale
    inner = grad * gain
    by_x = scale * (inner - plain * jnp.mean(inner * plain, axis=-1, keepdims=True))
    return by_x, jnp.sum(grad * plain, axis=0, keepdims=True)


def unwind_kernel(
    length_ref, back_ref, hit0_ref, hit1_ref, picks_ref, kept_ref, hidden_ref, xn_ref, cot_ref,
    router_ref, gain_ref, wout_ref, qkv_ref, bias_ref, *refs
):
    mixed_ref, dhidden_ref, dattn_ref, dqkv_ref, drouter_ref, dgain_ref, dscores_ref, dheads_ref = refs[-8:]
    xn = xn_ref[...]
    hidden = hidden_ref[...]
    grad_out = cot_ref[0].astype(jnp.float32)
    logits = dot(xn, router_ref[...])
    lane = lax.broadcasted_iota(jnp.int32, logits.shape, 1)
    logits = jnp.where(lane < EXPERTS, logits, -1e30)
    weights = jnp.exp(logits - jnp.max(logits, axis=-1, keepdims=True))
    route = weights / jnp.sum(weights, axis=-1, keepdims=True)
    mixed = hidden
    grad_route = jnp.zeros_like(route)
    for k, hit_ref in enumerate((hit0_ref, hit1_ref)):
        pair = sum(dot(hit_ref[m], back_ref[m, 0]) for m in range(back_ref.shape[0]))
        pick = jnp.where(lane == picks_ref[:, k : k + 1], kept_ref[:, k : k + 1], 0.0)
        mixed = mixed + jnp.sum(route * pick, axis=-1, keepdims=True) * pair
        grad_route = grad_route + pick * jnp.sum(grad_out * pair, axis=-1, keepdims=True)
    mixed_ref[...] = mixed.astype(jnp.bfloat16)
    grad_logits = route * (grad_route - jnp.sum(route * grad_route, axis=-1, keepdims=True))
    grad_logits = grad_logits.astype(jnp.bfloat16)
    drouter_ref[...] = contract_first(xn, grad_logits)
    grad_xn = contract_last(grad_logits, router_ref[...]) + sum(
        dot(hit0_ref[m] + hit1_ref[m], back_ref[m, 1]) for m in range(back_ref.shape[0])
    )
    by_hidden, by_gain = norm_back(hidden, gain_ref[...], grad_xn)
    dgain_ref[...] = by_gain
    grad_hidden = grad_out + by_hidden
    dhidden_ref[...] = grad_hidden
    grad_attn = grad_hidden.astype(jnp.bfloat16)
    dattn_ref[...] = grad_attn
    dheads_ref[...] = contract_last(grad_attn, wout_ref[...]).astype(jnp.bfloat16)
    allowed = allowed_pairs(length_ref[0])
    scale = HEAD_DIM ** (-0.5)
    for pair in range(HEADS // 2):
        outs = [[], [], []]
        for head in (2 * pair, 2 * pair + 1):
            at = head * HEAD_DIM
            query = qkv_ref[:, at : at + HEAD_DIM]
            key = qkv_ref[:, D + at : D + at + HEAD_DIM]
            value = qkv_ref[:, 2 * D + at : 2 * D + at + HEAD_DIM]
            grad_head = dheads_ref[:, at : at + HEAD_DIM]
            scores = contract_last(key, query)
            scores = jnp.where(allowed, scores * scale + bias_ref[head].astype(jnp.float32), -1e30)
            weights = jnp.exp(scores - jnp.max(scores, axis=0, keepdims=True))
            probs = weights / jnp.sum(weights, axis=0, keepdims=True)
            grad_probs = contract_last(value, grad_head)
            grad_scores = probs * (grad_probs - jnp.sum(probs * grad_probs, axis=0, keepdims=True))
            grad_scores = grad_scores.astype(jnp.bfloat16)
            dscores_ref[head] = grad_scores
            outs[0].append(contract_first(grad_scores, key) * scale)
            outs[1].append(dot(grad_scores, query) * scale)
            outs[2].append(dot(probs.astype(jnp.bfloat16), grad_head))
        for i in range(3):
            dqkv_ref[:, i * D + pair * 128 : i * D + (pair + 1) * 128] = jnp.concatenate(
                outs[i], axis=1
            ).astype(jnp.bfloat16)


def unwind(
    micro, length, back, hits, picks, kept, hidden, xn_second, cotangent, router_pad, gain_second,
    out_weight, qkv_rows, bias_full, waits
):
    whole = lambda a: pl.BlockSpec(a.shape, lambda i: (0,) * a.ndim)
    gain_row = gain_second.reshape(1, D)
    ins = [back, hits[0], hits[1], picks, kept, hidden, xn_second, cotangent, router_pad, gain_row, out_weight, qkv_rows, bias_full]
    specs = [whole(a) for a in ins]
    specs[7] = pl.BlockSpec((1, SLOT, D), lambda i: (micro, 0, 0))
    out_shape = [
        jax.ShapeDtypeStruct((SLOT, D), jnp.bfloat16),
        jax.ShapeDtypeStruct((SLOT, D), jnp.float32),
        jax.ShapeDtypeStruct((SLOT, D), jnp.bfloat16),
        jax.ShapeDtypeStruct((SLOT, 3 * D), jnp.bfloat16),
        jax.ShapeDtypeStruct((D, 128), jnp.float32),
        jax.ShapeDtypeStruct((1, D), jnp.float32),
        jax.ShapeDtypeStruct((HEADS, SLOT, SLOT), jnp.bfloat16),
    ]
    return pl.pallas_call(
        unwind_kernel,
        grid=(1,),
        in_specs=[SMEM] + specs + [ANY] * len(waits),
        out_specs=[whole(o) for o in out_shape],
        out_shape=out_shape,
        scratch_shapes=[pltpu.VMEM((SLOT, D), jnp.bfloat16)],
        compiler_params=params(),
        cost_estimate=lasts(17),
        name="unwind",
    )(length.reshape(1), *ins, *waits)


def weights_kernel(groups, wide, bits_ref, xn0, xn1, dqkv0, dqkv1, heads0, heads1, dattn0, dattn1, *refs):
    count = D // groups // 2

    def rows_of(ref):
        return jnp.concatenate(
            [
                ref[:, pl.ds(pl.multiple_of((2 * g + bits_ref[0]) * count, count), count)]
                for g in range(groups)
            ],
            axis=1,
        )

    left = [rows_of(xn0), rows_of(xn1)]
    heads = [rows_of(heads0), rows_of(heads1)]
    half = count // 2
    for part in range(4):
        if part < 3:
            span = slice(part * D, (part + 1) * D)
            total = contract_first(left[0], dqkv0[:, span]) + contract_first(left[1], dqkv1[:, span])
        else:
            total = contract_first(heads[0], dattn0[...]) + contract_first(heads[1], dattn1[...])
        total = total.reshape(groups, count, D)
        which, span = part // 2, slice(part % 2 * D, (part % 2 + 1) * D)
        if not wide:
            refs[-1][which, :, :, span] = total.astype(jnp.bfloat16)
            continue
        total = total + refs[0][which, :, :, span].astype(jnp.float32)
        total_ref = refs[-1]
        total_ref[...] = total.astype(jnp.bfloat16)
        send_ref, keep_ref = refs[-5 + 2 * which : len(refs) - 3 + 2 * which]
        bit = bits_ref[1 + which]
        keep_ref[:, :, span] = total_ref[:, pl.ds(pl.multiple_of(bit * half, half), half)]
        send_ref[:, :, span] = total_ref[:, pl.ds(pl.multiple_of((1 - bit) * half, half), half)]


def weight_grads(groups, xn_all, dqkv, heads, dattn, arrived=None):
    place = lax.axis_index("rep")
    wide = arrived is not None
    core = bit_of(place, 1)
    bits = jnp.stack(
        [core if wide else 1 - core] + [bit_of(place, order_of(w)[1]) for w in range(2)]
    ).astype(jnp.int32)
    count = D // groups // 2
    if count % 128:
        return weight_grads_plain(groups, xn_all, dqkv, heads, dattn, arrived)
    shapes = [(groups, count // 2, 2 * D)] * 4 if wide else [(2, groups, count, 2 * D)]
    return pl.pallas_call(
        functools.partial(weights_kernel, groups, wide),
        in_specs=[SMEM] + [VMEM] * (9 if wide else 8),
        out_specs=[VMEM] * len(shapes),
        out_shape=[jax.ShapeDtypeStruct(shape, jnp.bfloat16) for shape in shapes],
        scratch_shapes=[pltpu.VMEM((groups, count, D), jnp.bfloat16)] if wide else [],
        compiler_params=params(),
        cost_estimate=lasts(6),
        name="weights",
    )(bits, *xn_all, *dqkv, *heads, *dattn, *([arrived] if wide else []))


def weight_grads_plain(groups, xn_all, dqkv, heads, dattn, arrived):
    total = jnp.concatenate(
        [
            contract_first(jnp.concatenate(xn_all, axis=0), jnp.concatenate(dqkv, axis=0)),
            contract_first(jnp.concatenate(heads, axis=0), jnp.concatenate(dattn, axis=0)),
        ],
        axis=1,
    ).reshape(groups, D // groups, 4 * D)
    theirs, mine = halves_of(total, 1, 1)
    if arrived is None:
        return [jnp.stack(jnp.split(theirs.astype(jnp.bfloat16), 2, axis=2))]
    mine = [
        (m + a.astype(jnp.float32)).astype(jnp.bfloat16)
        for m, a in zip(jnp.split(mine, 2, axis=2), arrived)
    ]
    return [cut for w in range(2) for cut in halves_of(mine[w], order_of(w)[1], 1)]


def finish_kernel(tokens_ref, gain_ref, wqkv_ref, dqkv0, dqkv1, dhidden0, dhidden1, out_ref, dgain_ref):
    total = None
    for micro, (dqkv, dhidden) in enumerate(((dqkv0, dhidden0), (dqkv1, dhidden1))):
        grad = contract_last(dqkv[...], wqkv_ref[...])
        by_x, by_gain = norm_back(tokens_ref[micro].astype(jnp.float32), gain_ref[...], grad)
        out_ref[micro] = dhidden[...] + by_x
        total = by_gain if total is None else total + by_gain
    dgain_ref[...] = total


def finish(tokens, gain_first, qkv_weight, dqkv, dhidden):
    return pl.pallas_call(
        finish_kernel,
        in_specs=[VMEM] * 7,
        out_specs=[VMEM] * 2,
        out_shape=[
            jax.ShapeDtypeStruct((MICRO, SLOT, D), jnp.float32),
            jax.ShapeDtypeStruct((1, D), jnp.float32),
        ],
        compiler_params=params(),
        cost_estimate=lasts(10),
        name="finish",
    )(tokens, gain_first.reshape(1, D), qkv_weight, *dqkv, *dhidden)


def join_small(by_distance, router, gains, rel_bias):
    groups = lax.axis_size("grp")
    place = lax.axis_index("grp")
    a, b = router.size, router.size + gains.size
    size = b + rel_bias.size
    blocks = [by_distance[m][:size].astype(jnp.float32) for m in range(groups)]
    rows = []
    for at in range(groups):
        row = blocks[0]
        for m in range(1, groups):
            row = jnp.where(place ^ m == at, blocks[m], row)
        rows.append(row)
    every = jnp.stack(rows)
    return (
        every[:, :a].reshape(-1, router.shape[1]).astype(jnp.bfloat16),
        every[:, a:b].reshape(-1, gains.shape[1]),
        every[:, b:].reshape(-1, rel_bias.shape[1]),
    )


def per_device(
    tokens,
    w_qkv,
    w_out,
    router,
    gains,
    rel_bias,
    w_gate,
    w_up,
    w_down,
    lengths,
    choices,
    priority,
    cotangent,
):
    groups = lax.axis_size("grp")
    split_count = groups // EXPERTS
    place = lax.axis_index("grp")
    my_expert = place // split_count
    small = jnp.concatenate([router.reshape(-1), gains.reshape(-1), rel_bias.reshape(-1)])
    chains, came_along = gather_weights(w_qkv, w_out, small)
    after = [chains[1][1][0][1]]
    router_weight, gain_full, bias_table = join_small(came_along, router, gains, rel_bias)
    router_pad = jnp.pad(router_weight, ((0, 0), (0, 128 - EXPERTS)))
    bucket_hits = (
        jnp.asarray(np.ascontiguousarray(bucket_matrix().T))[:, :, None] == jnp.arange(BUCKETS)[None, None, :]
    ).astype(jnp.bfloat16)
    bias_full = jnp.einsum(
        "hk,ijk->hij", bias_table.astype(jnp.bfloat16), bucket_hits, preferred_element_type=jnp.float32
    ).astype(jnp.bfloat16)

    target = (
        (jnp.arange(groups) // split_count)[:, None] * CAP + jnp.arange(CAP)[None, :]
    ).reshape(-1)
    routes = []
    for micro in range(MICRO):
        _, kept_mask, slot_index = expert_slots(choices[micro], priority[micro], lengths[micro, 0])
        hits = [
            (slot_index[None, :, k, None] == target.reshape(groups, 1, CAP)).astype(jnp.bfloat16)
            for k in range(2)
        ]
        spots = (
            (target[:, None] == slot_index[None, :, 0]) | (target[:, None] == slot_index[None, :, 1])
        ).astype(jnp.bfloat16)
        routes.append([kept_mask, hits, spots])
    spots1 = routes[1][2]
    pieces = gather_cores(chains, bias_full, router_pad, gain_full, spots1)
    for micro in range(MICRO):
        spots = routes[micro][2]
        (sent,) = tie([cotangent[micro]], *after)
        blocks = dot(spots, sent).astype(jnp.bfloat16).reshape(groups, CAP, D)
        routes[micro][2] = spots.reshape(groups, CAP, SLOT)
        routes[micro].append(to_experts(blocks).reshape(groups * CAP, D))
        after = [bias_full, router_pad, *[block for _, held in chains for _, block in held]]

    xn0, qkv0, out_weight = project(0, tokens, gain_full[:, 0], pieces, [routes[0][-1], bias_full, router_pad])

    def attended(micro, qkv_rows, waits):
        return attend(
            micro, lengths[micro], qkv_rows, tokens, bias_full, out_weight, gain_full[:, 1], routes[micro][2], waits
        )

    forward = [attended(0, qkv0, [])]
    rows0 = to_experts(forward[0][3]).reshape(groups * CAP, D)
    xn1, qkv1, qkv_weight = project(1, tokens, gain_full[:, 0], pieces, [forward[0][0], routes[1][-1]])
    forward.append(attended(1, qkv1, []))
    xn_all, qkv_all = [xn0, xn1], [qkv0, qkv1]
    blocks1, _ = tie([forward[1][3], rows0])
    rows = [rows0, to_experts(blocks1).reshape(groups * CAP, D)]

    def expert(micro, waits):
        return run_expert(
            my_expert, rows[micro], routes[micro][-1], router_pad, w_gate, w_up, w_down, waits
        )

    inner = [expert(0, [qkv_weight])]
    home0 = to_experts(inner[0][4])
    inner.append(expert(1, [inner[0][0]]))
    home1 = to_experts(inner[1][4])
    doutput, act, dgate, dup = ([inner[micro][i] for micro in range(MICRO)] for i in range(4))

    def launch(left, right, waits):
        theirs = products(left, right, None, waits)
        return theirs[0], [exchange(half, "rep", 1) for half in theirs]

    def settle(left, right, arrived, waits):
        outs = products(left, right, arrived, waits)
        pair = [Halving(w, 0) for w in range(2)]
        for w in range(2):
            pair[w].start(outs[2 * w], outs[2 * w + 1], 1)
        return pair, outs[1]

    def unwound(micro, home, waits):
        kept_mask, hits, _, _ = routes[micro]
        heads, hidden, xn_second, _ = forward[micro]
        return unwind(
            micro, lengths[micro], home, hits, choices[micro], kept_mask, hidden, xn_second, cotangent,
            router_pad, gain_full[:, 1], out_weight, qkv_all[micro], bias_full, waits,
        )

    tok, down_came = launch(act, doutput, [])
    tok, gate_came = launch(rows, dgate, [tok])
    down, tok = settle(act, doutput, down_came, [tok, home0])
    tok, up_came = launch(rows, dup, [tok])
    gate, tok = settle(rows, dgate, gate_came, [tok])
    land(down, tok)
    for half in down:
        half.halve(2)
    up, tok = settle(rows, dup, up_came, [half.kept for half in down])
    land([*gate, *down], tok)
    for half in gate:
        half.halve(2)
    for half in down:
        half.own()
        half.back()
    un0 = unwound(0, home0, [half.kept for half in (*gate, *down)])
    land([*up, *down, *gate], un0[0])
    for half in up:
        half.halve(2)
    for half in down:
        half.back_pair()
    for half in gate:
        half.own()
    un1 = unwound(1, home1, [half.kept for half in (*up, *down, *gate)])
    un = (un0, un1)

    def attention_grads(xn_in, arrived=None):
        return weight_grads(
            groups, xn_in, [u[3] for u in un], [forward[m][0] for m in range(MICRO)], [u[2] for u in un], arrived
        )

    (theirs,) = attention_grads(xn_all)
    land([*up, *down], theirs)
    came = exchange(tie([theirs], up[0].kept)[0], "rep", 1)
    for half in up:
        half.own()
        half.back()
    for half in gate:
        half.back()
    dscores = tie([u[6] for u in un], *[half.kept for half in up])
    bias_grad = sum(
        jnp.einsum("hij,ijk->hk", d, bucket_hits, preferred_element_type=jnp.float32) for d in dscores
    )
    outs = attention_grads(tie(xn_all, bias_grad, *[half.kept for half in (*up, *gate)]), came)
    attn = [Halving(w, 1) for w in range(2)]
    for w in range(2):
        attn[w].start(outs[2 * w], outs[2 * w + 1], 1)
    land([*up, *gate, *down], outs[0])
    down_own, down_got = swap_cores(down)
    token_grads, dgain_first = finish(
        tie([tokens], down_own)[0], gain_full[:, 0], qkv_weight, [u[3] for u in un], [u[1] for u in un]
    )

    small = [
        (un0[4] + un1[4])[:, :EXPERTS].reshape(-1),
        jnp.stack([dgain_first[0], un0[5][0] + un1[5][0]], axis=1).reshape(-1),
        bias_grad.reshape(-1),
    ]
    flat = jnp.concatenate(small)
    flat = jnp.pad(flat, (0, -flat.size % 1024)).reshape(-1, 128)
    steps = [("rep", m) for m in masks_of(lax.axis_size("rep"))] + [("grp", m) for m in masks_of(groups)]
    small_sum = Halving(0, 0)
    small_sum.kept = flat

    def add_small():
        if small_sum.moving is not None:
            small_sum.kept, small_sum.moving = small_sum.kept + small_sum.moving, None
        if steps:
            small_sum.moving = exchange(small_sum.kept, *steps.pop(0))

    add_small()
    down_grad = assemble(down, *tie([down_own, down_got], small_sum.kept))
    land([*attn, small_sum], down_grad)
    for half in attn:
        half.halve(2)
    add_small()
    land([*attn, small_sum])
    for half in attn:
        half.own()
    zsum = Halving(0, 0)
    zsum.kept = to_experts(jnp.stack([half.kept for half in attn], axis=1))
    for half in (*gate, *up):
        half.kept, half.moving = tie([half.kept, half.moving], *[a.kept for a in attn])
        half.back_pair()
    add_small()
    land([zsum, *gate, *up, small_sum])
    total = jnp.sum(zsum.kept.astype(jnp.float32), axis=0).astype(jnp.bfloat16)
    for w in range(2):
        attn[w].kept = total[w]
        attn[w].back()
    land([*gate, *up], total)
    gate_own, gate_got = swap_cores(gate)
    add_small()
    land([*attn, small_sum], gate_own)
    for half in attn:
        half.back_pair()
    land(up, attn[0].kept)
    up_own, up_got = swap_cores(up)
    gate_grad = assemble(gate, *tie([gate_own, gate_got], up_own))
    add_small()
    land([*attn, small_sum], gate_grad)
    attn_own, attn_got = swap_cores(attn)
    up_grad = assemble(up, *tie([up_own, up_got], attn_own))
    while small_sum.moving is not None:
        add_small()
    flat = small_sum.kept
    qkv_grad, out_grad = assemble_attention(attn, *tie([attn_own, attn_got], up_grad))

    flat = flat.reshape(-1)
    outs = []
    start = 0
    for whole in ((D, EXPERTS), (D, 2), (HEADS, BUCKETS)):
        size = whole[0] * whole[1]
        rows_here = whole[0] // groups
        outs.append(
            lax.dynamic_slice_in_dim(
                flat[start : start + size].reshape(whole), place * rows_here, rows_here, 0
            )
        )
        start += size
    return (
        jnp.stack([u[0] for u in un]),
        token_grads,
        qkv_grad,
        out_grad,
        outs[0],
        outs[1],
        outs[2],
        gate_grad[None],
        up_grad[None],
        down_grad[None],
    )


def solution(mesh):
    placed = (
        P(None, ("rep", "grp"), None),
        P("grp", None),
        P("grp", None),
        P("grp", None),
        P("grp", None),
        P("grp", None),
        P("grp", None, None),
        P("grp", None, None),
        P("grp", None, None),
        P(None, ("rep", "grp")),
        P(None, ("rep", "grp"), None),
        P(None, ("rep", "grp")),
        P(None, ("rep", "grp"), None),
    )
    return jax.shard_map(
        per_device,
        mesh=mesh,
        in_specs=placed,
        out_specs=(
            P(None, ("rep", "grp"), None),
            P(None, ("rep", "grp"), None),
            P("grp", None),
            P("grp", None),
            P("grp", None),
            P("grp", None),
            P("grp", None),
            P("grp", None, None),
            P("grp", None, None),
            P("grp", None, None),
        ),
        check_vma=False,
    )
```

```python
import functools

import jax
import jax.numpy as jnp
import numpy as np
from jax import lax
from jax.experimental import pallas as pl
from jax.experimental.pallas import tpu as pltpu
from jax.sharding import PartitionSpec as P

D = 1024
HEADS = 16
HEAD_DIM = 64
EXPERTS = 4
BUCKETS = 32
MAX_DIST = 128
MICRO = 2
SLOT = 192
CAP = 120
VMEM_LIMIT = 56 * 1024 * 1024
PART = 0.001


def lasts(us):
    return pl.CostEstimate(flops=int(us * PART * 1.15e9), bytes_accessed=1, transcendentals=0)


VMEM = pl.BlockSpec(memory_space=pltpu.VMEM)
SMEM = pl.BlockSpec(memory_space=pltpu.SMEM)
ANY = pl.BlockSpec(memory_space=pl.ANY)


def params():
    return pltpu.CompilerParams(vmem_limit_bytes=VMEM_LIMIT)


def bucket_matrix():
    distance = np.arange(SLOT)
    exact_count = BUCKETS // 2
    safe_span = np.maximum(distance, 1) / exact_count
    log_bucket = exact_count + np.floor(
        np.log(safe_span) / np.log(MAX_DIST / exact_count) * (BUCKETS - exact_count)
    ).astype(np.int32)
    bucket_of = np.where(distance < exact_count, distance, np.minimum(log_bucket, BUCKETS - 1))
    offsets = np.maximum(distance[:, None] - distance[None, :], 0)
    return bucket_of[offsets].astype(np.int32)


def dot(left, right):
    return jnp.dot(left, right, preferred_element_type=jnp.float32)


def contract_last(left, right):
    return lax.dot_general(
        left, right, (((1,), (1,)), ((), ())), preferred_element_type=jnp.float32
    )


def contract_first(left, right):
    return lax.dot_general(
        left, right, (((0,), (0,)), ((), ())), preferred_element_type=jnp.float32
    )


def expert_slots(expert_pick, priority_row, length):
    live_mask = (jnp.arange(SLOT) < length).astype(jnp.float32)
    pick_hits = (expert_pick[:, :, None] == jnp.arange(EXPERTS)[None, None, :]).astype(jnp.float32)
    expert_hits = jnp.sum(pick_hits, axis=1) * live_mask[:, None]
    before = (priority_row[None, :] < priority_row[:, None]).astype(jnp.bfloat16)
    ahead_count = dot(before, expert_hits.astype(jnp.bfloat16))
    place_pos = jnp.sum(pick_hits * ahead_count[:, None, :], axis=2)
    kept_mask = live_mask[:, None] * (place_pos < CAP - 0.5).astype(jnp.float32)
    slot_index = jnp.where(
        kept_mask > 0.5, expert_pick * CAP + place_pos.astype(jnp.int32), EXPERTS * CAP
    )
    return (pick_hits, kept_mask, slot_index)


def exchange(block, axis, mask):
    return lax.ppermute(block, axis, [(i, i ^ mask) for i in range(lax.axis_size(axis))])


def masks_of(count):
    return [1 << bit for bit in range(count.bit_length() - 1)]


def spread(own, axis, masks):
    held = [(0, own)]
    for mask in masks:
        held += [(far ^ mask, exchange(block, axis, mask)) for far, block in held]
    return held


def to_experts(blocks):
    return lax.all_to_all(blocks, "grp", split_axis=0, concat_axis=0, tiled=True)


def bit_of(index, mask):
    return (index & mask) // mask


def tie(values, *after):
    return lax.optimization_barrier((tuple(values), after))[0]


def rep_masks():
    masks = masks_of(lax.axis_size("rep"))
    return masks[3:], masks[:3]


def order_of(which):
    masks = rep_masks()[1]
    return masks[:1] + (masks[1:] if which == 0 else masks[:0:-1])


def halves_of(block, mask, dim):
    half = block.shape[dim] // 2
    bit = bit_of(lax.axis_index("rep"), mask)
    return (
        lax.dynamic_slice_in_dim(block, (1 - bit) * half, half, dim),
        lax.dynamic_slice_in_dim(block, bit * half, half, dim),
    )


def add_low(left, right):
    return (left.astype(jnp.float32) + right.astype(jnp.float32)).astype(jnp.bfloat16)


class Halving:
    def __init__(self, which, dim):
        self.which, self.dim = which, dim
        self.masks = order_of(which)
        self.kept = self.moving = None
        self.held = None

    def start(self, send, keep, at):
        self.kept, self.moving = keep, exchange(send, "rep", self.masks[at])

    def halve(self, at):
        kept, got = (halves_of(x, self.masks[at], self.dim) for x in (self.kept, self.moving))
        self.start(*(add_low(k, g) for k, g in zip(kept, got)), at)

    def own(self):
        total = add_low(self.kept, self.moving)
        for mask in rep_masks()[0]:
            total = add_low(total, exchange(total, "rep", mask))
        self.kept, self.moving = total, None

    def back(self):
        self.moving = exchange(self.kept, "rep", self.masks[-1])

    def back_pair(self):
        self.kept = jnp.stack([self.kept, self.moving])
        self.moving = exchange(self.kept, "rep", self.masks[-2])

    def place(self):
        index = 0
        for mask in self.masks:
            index = 2 * index + bit_of(lax.axis_index("rep"), mask)
        return index


def land(halvings, *after):
    flat = [x for h in halvings for x in (h.kept, h.moving) if x is not None]
    flat = list(tie(flat, *after))
    for h in halvings:
        h.kept = flat.pop(0)
        if h.moving is not None:
            h.moving = flat.pop(0)


def swap_cores(pair):
    own = jnp.concatenate([x for h in pair for x in (h.kept, h.moving)], axis=0)
    return own, exchange(own, "rep", 1)


def assemble(pair_of_halves, own, got):
    places = jnp.stack([half.place() for half in pair_of_halves]).astype(jnp.int32)
    pieces, rows, cols = own.shape
    deep = pieces // 4
    cut_cores = cols % 128 != 0

    def body(place_ref, own_ref, got_ref, out_ref):
        half, core, step = (pl.program_id(i) for i in range(3))
        place = place_ref[half]
        far = (core * deep + step) ^ (place // 2)
        at = 2 * (half * deep + far % deep)
        out = out_ref.at[0] if cut_cores else out_ref
        for other, ref in enumerate((own_ref, got_ref)):

            @pl.when(far // deep == other)
            def _():
                out[:rows] = ref[at + place % 2].astype(jnp.float32)
                out[rows:] = ref[at + 1 - place % 2].astype(jnp.float32)

    whole = pl.BlockSpec((pieces, rows, cols), lambda half, core, step, place_ref: (0, 0, 0))
    out_shape = (4 * deep * rows, 2 * cols)
    out_spec = pl.BlockSpec(
        (2 * rows, cols), lambda half, core, step, place_ref: (half * deep + step, core)
    )
    if cut_cores:
        out_shape = (2, 4 * deep * rows, cols)
        out_spec = pl.BlockSpec(
            (1, 2 * rows, cols), lambda half, core, step, place_ref: (core, half * deep + step, 0)
        )
    out = pl.pallas_call(
        body,
        grid_spec=pltpu.PrefetchScalarGridSpec(
            num_scalar_prefetch=1,
            grid=(2, 2, deep),
            in_specs=[whole] * 2,
            out_specs=out_spec,
        ),
        out_shape=jax.ShapeDtypeStruct(out_shape, jnp.float32),
        compiler_params=params(),
        cost_estimate=lasts(9),
        name="assemble",
    )(places, own, got)
    return jnp.concatenate([out[0], out[1]], axis=1) if cut_cores else out


def assemble_attention(pair_of_halves, own, got):
    places = jnp.stack([half.place() for half in pair_of_halves]).astype(jnp.int32)
    pieces, rows, _ = own.shape
    each = pieces // 2

    def body(place_ref, own_ref, got_ref, qkv_ref, out_ref):
        for other, ref in enumerate((own_ref, got_ref)):
            for at in range(pieces):
                where = (other * each + at % each) ^ place_ref[at // each]
                span = pl.ds(pl.multiple_of(where * rows, rows), rows)
                values = ref[at].astype(jnp.float32)
                if at < each:
                    qkv_ref[span, : 2 * D] = values
                else:
                    qkv_ref[span, 2 * D :] = values[:, :D]
                    out_ref[span, :] = values[:, D:]

    depth = 2 * each * rows
    return pl.pallas_call(
        body,
        in_specs=[SMEM] + [VMEM] * 2,
        out_specs=[VMEM] * 2,
        out_shape=[
            jax.ShapeDtypeStruct((depth, 3 * D), jnp.float32),
            jax.ShapeDtypeStruct((depth, D), jnp.float32),
        ],
        compiler_params=params(),
        cost_estimate=lasts(4),
        name="assemble_attention",
    )(places, own, got)


def gather_weights(w_qkv, w_out, small):
    slices = min(lax.axis_size("rep"), 8)
    eighth = lax.axis_index("rep") % slices
    width = D // slices
    parts = [w_qkv[:, i * D : (i + 1) * D] for i in range(3)] + [w_out]
    own = jnp.concatenate(
        [lax.dynamic_slice_in_dim(part, eighth * width, width, 1) for part in parts], axis=1
    )
    depth = own.shape[0]
    small = small.reshape(-1)
    lines = -(-small.size // (16 * own.shape[1])) * 16
    small = jnp.pad(small, (0, lines * own.shape[1] - small.size)).reshape(lines, -1)
    masks = masks_of(slices)
    held = spread(jnp.concatenate([own, small]), "grp", masks_of(lax.axis_size("grp"))[::-1])
    over_grp = [(m, block[:depth]) for m, block in held]
    half = len(over_grp) // 2
    chains = []
    for which in range(2):
        mine = over_grp[which * half : (which + 1) * half]
        order = masks[1:] if which == 0 else masks[:0:-1]
        block = jnp.stack([piece for _, piece in mine])
        chains.append(([m for m, _ in mine], spread(block, "rep", order)))
    return chains, {m: block[depth:].reshape(-1) for m, block in held}


def gather_cores(chains, *after):
    pieces = []
    for members, held in chains:
        blocks = tie([block for _, block in held], *after)
        for (far, _), block in zip(held, blocks):
            pieces += [(far, members, block), (far ^ 1, members, exchange(block, "rep", 1))]
    return pieces


def norm_rows(x, gain):
    return x * lax.rsqrt(jnp.mean(x * x, axis=-1, keepdims=True) + 1e-06) * gain


def each_piece(plan, pieces, far):
    for (this, members), piece in zip(plan, pieces):
        if this == far:
            yield from ((m, piece, at) for at, m in enumerate(members))


def project_kernel(plan, micro, place_ref, tokens_ref, gain_ref, *refs):
    pieces = refs[: len(plan)]
    xn_ref, qkv_ref, weight_ref = refs[-3:]
    depth = pieces[0].shape[1]
    width = pieces[0].shape[2] // 4
    xn_ref[...] = norm_rows(tokens_ref[0].astype(jnp.float32), gain_ref[...]).astype(jnp.bfloat16)
    for far in sorted({far for far, _ in plan}):
        column = pl.multiple_of((place_ref[0] ^ far) * width, width)
        total = None
        for m, piece, at in each_piece(plan, pieces, far):
            row = pl.multiple_of((place_ref[1] ^ m) * depth, depth)
            if micro == 0:
                weight_ref[pl.ds(row, depth), pl.ds(column, width)] = piece[at, :, 3 * width :]
            else:
                for part in range(3):
                    weight_ref[pl.ds(row, depth), pl.ds(column + part * D, width)] = piece[
                        at, :, part * width : (part + 1) * width
                    ]
            term = dot(xn_ref[:, pl.ds(row, depth)], piece[at, :, : 3 * width])
            total = term if total is None else total + term
        for part in range(3):
            low = total[:, part * width : (part + 1) * width].astype(jnp.bfloat16)
            qkv_ref[:, pl.ds(column + part * D, width)] = low


def places_of():
    slices = min(lax.axis_size("rep"), 8)
    return jnp.stack([lax.axis_index("rep") % slices, lax.axis_index("grp")]).astype(jnp.int32)


def project(micro, tokens, gain_first, pieces, waits):
    plan = [(far, m) for far, m, _ in pieces]
    whole = lambda *shape: pl.BlockSpec(shape, lambda i: (0,) * len(shape))
    out_shape = [
        jax.ShapeDtypeStruct(shape, jnp.bfloat16)
        for shape in ((SLOT, D), (SLOT, 3 * D), (D, 3 * D if micro else D))
    ]
    return pl.pallas_call(
        functools.partial(project_kernel, plan, micro),
        grid=(1,),
        in_specs=[SMEM, pl.BlockSpec((1, SLOT, D), lambda i: (micro, 0, 0)), whole(1, D)]
        + [whole(*piece.shape) for _, _, piece in pieces]
        + [ANY] * len(waits),
        out_specs=[whole(*o.shape) for o in out_shape],
        out_shape=out_shape,
        compiler_params=params(),
        cost_estimate=lasts(10),
        name="project",
    )(places_of(), tokens, gain_first.reshape(1, D), *[piece for _, _, piece in pieces], *waits)


def allowed_pairs(length):
    row = lax.broadcasted_iota(jnp.int32, (SLOT, SLOT), 0)
    column = lax.broadcasted_iota(jnp.int32, (SLOT, SLOT), 1)
    return (row <= column) & (row < length)


def attend_kernel(groups, length_ref, qkv_ref, tokens_ref, bias_ref, wout_ref, gain_ref, spots_ref, *refs):
    heads_ref, hidden_ref, xn_ref, rows_ref = refs[-4:]
    allowed = allowed_pairs(length_ref[0])
    scale = HEAD_DIM ** (-0.5)
    for pair in range(HEADS // 2):
        outs = []
        for head in (2 * pair, 2 * pair + 1):
            at = head * HEAD_DIM
            scores = contract_last(
                qkv_ref[:, D + at : D + at + HEAD_DIM], qkv_ref[:, at : at + HEAD_DIM]
            )
            scores = jnp.where(allowed, scores * scale + bias_ref[head].astype(jnp.float32), -1e30)
            weights = jnp.exp(scores - jnp.max(scores, axis=0, keepdims=True))
            probs = weights / jnp.sum(weights, axis=0, keepdims=True)
            outs.append(
                contract_first(probs.astype(jnp.bfloat16), qkv_ref[:, 2 * D + at : 2 * D + at + HEAD_DIM])
            )
        heads_ref[:, pair * 128 : (pair + 1) * 128] = jnp.concatenate(outs, axis=1).astype(jnp.bfloat16)
    hidden = tokens_ref[0].astype(jnp.float32) + dot(heads_ref[...], wout_ref[...])
    hidden_ref[...] = hidden
    xn = norm_rows(hidden, gain_ref[...]).astype(jnp.bfloat16)
    xn_ref[...] = xn
    for m in range(groups):
        rows_ref[m] = dot(spots_ref[m], xn).astype(jnp.bfloat16)


def attend(micro, length, qkv_rows, tokens, bias_full, out_weight, gain_second, spots, waits):
    groups = spots.shape[0]
    whole = lambda *shape: pl.BlockSpec(shape, lambda i: (0,) * len(shape))
    low = jax.ShapeDtypeStruct((SLOT, D), jnp.bfloat16)
    out_shape = [
        low,
        jax.ShapeDtypeStruct((SLOT, D), jnp.float32),
        low,
        jax.ShapeDtypeStruct((groups, CAP, D), jnp.bfloat16),
    ]
    return pl.pallas_call(
        functools.partial(attend_kernel, groups),
        grid=(1,),
        in_specs=[
            SMEM,
            whole(SLOT, 3 * D),
            pl.BlockSpec((1, SLOT, D), lambda i: (micro, 0, 0)),
            whole(HEADS, SLOT, SLOT),
            whole(D, D),
            whole(1, D),
            whole(groups, CAP, SLOT),
        ]
        + [ANY] * len(waits),
        out_specs=[whole(*o.shape) for o in out_shape],
        out_shape=out_shape,
        compiler_params=params(),
        cost_estimate=lasts(9.3),
        name="attend",
    )(length.reshape(1), qkv_rows, tokens, bias_full, out_weight, gain_second.reshape(1, D), spots, *waits)


def gelu_parts(v):
    c = np.float32(np.sqrt(2 / np.pi))
    t = jnp.tanh(c * (v + np.float32(0.044715) * (v * v * v)))
    half = 0.5 * (1.0 + t)
    slope = half + 0.5 * v * (1.0 - t * t) * (c * (1.0 + np.float32(3 * 0.044715) * (v * v)))
    return v * half, slope


def expert_kernel(groups, chunk, expert_ref, rows_ref, grads_ref, router_ref, wg_hbm, wu_hbm, wd_hbm, *refs):
    dout_ref, act_hbm, dgate_hbm, dup_hbm, back_ref = refs[-13:-8]
    wg, wu, wd, act, dgate, dup, came, went = refs[-8:]
    hidden = act.shape[1]
    steps = hidden // chunk

    def incoming(c):
        span = pl.ds(pl.multiple_of(c * chunk, chunk), chunk)
        return [
            pltpu.make_async_copy(wg_hbm.at[0, :, span], wg.at[:, span], came.at[0, c]),
            pltpu.make_async_copy(wu_hbm.at[0, :, span], wu.at[:, span], came.at[1, c]),
            pltpu.make_async_copy(wd_hbm.at[0, span, :], wd.at[span, :], came.at[2, c]),
        ]

    def outgoing(c):
        span = pl.ds(pl.multiple_of(c * chunk, chunk), chunk)
        return [
            pltpu.make_async_copy(vmem.at[:, span], hbm.at[:, span], went.at[i, c])
            for i, (vmem, hbm) in enumerate(((act, act_hbm), (dgate, dgate_hbm), (dup, dup_hbm)))
        ]

    @pl.loop(0, steps)
    def _(c):
        for copy in incoming(c):
            copy.start()

    logits = dot(rows_ref[...], router_ref[...])
    lane = lax.broadcasted_iota(jnp.int32, logits.shape, 1)
    logits = jnp.where(lane < EXPERTS, logits, -1e30)
    weights = jnp.exp(logits - jnp.max(logits, axis=-1, keepdims=True))
    route = weights / jnp.sum(weights, axis=-1, keepdims=True)
    gate = jnp.sum(jnp.where(lane == expert_ref[0], route, 0.0), axis=-1, keepdims=True)
    dout_ref[...] = (gate * grads_ref[...].astype(jnp.float32)).astype(jnp.bfloat16)

    @pl.loop(0, steps)
    def _(c):
        span = pl.ds(pl.multiple_of(c * chunk, chunk), chunk)
        for copy in incoming(c):
            copy.wait()
        gate_pre = dot(rows_ref[...], wg[:, span])
        up_pre = dot(rows_ref[...], wu[:, span])
        gelu, slope = gelu_parts(gate_pre)
        act[:, span] = (gelu * up_pre).astype(jnp.bfloat16)
        grad_act = contract_last(dout_ref[...], wd[span, :])
        dgate[:, span] = (grad_act * up_pre * slope).astype(jnp.bfloat16)
        dup[:, span] = (grad_act * gelu).astype(jnp.bfloat16)
        for copy in outgoing(c):
            copy.start()

    part = dot(act[...], wd[...])
    for m in range(groups):
        back_ref[m, 0] = part[m * CAP : (m + 1) * CAP].astype(jnp.bfloat16)
    grad_rows = contract_last(dgate[...], wg[...]) + contract_last(dup[...], wu[...])
    for m in range(groups):
        back_ref[m, 1] = grad_rows[m * CAP : (m + 1) * CAP].astype(jnp.bfloat16)

    @pl.loop(0, steps)
    def _(c):
        for copy in outgoing(c):
            copy.wait()


def run_expert(expert, rows, grad_rows, router_pad, w_gate, w_up, w_down, waits):
    count = rows.shape[0]
    groups = count // CAP
    hidden = w_gate.shape[2]
    chunk = 256 if hidden % 256 == 0 else 128
    steps = hidden // chunk
    wide = jax.ShapeDtypeStruct((count, hidden), jnp.bfloat16)
    low = lambda *shape: pltpu.VMEM(shape, jnp.bfloat16)
    return pl.pallas_call(
        functools.partial(expert_kernel, groups, chunk),
        in_specs=[SMEM] + [VMEM] * 3 + [ANY] * (3 + len(waits)),
        out_specs=[VMEM] + [ANY] * 3 + [VMEM],
        out_shape=[
            jax.ShapeDtypeStruct((count, D), jnp.bfloat16),
            wide,
            wide,
            wide,
            jax.ShapeDtypeStruct((groups, 2, CAP, D), jnp.bfloat16),
        ],
        scratch_shapes=[
            low(D, hidden),
            low(D, hidden),
            low(hidden, D),
            low(count, hidden),
            low(count, hidden),
            low(count, hidden),
            pltpu.SemaphoreType.DMA((3, steps)),
            pltpu.SemaphoreType.DMA((3, steps)),
        ],
        compiler_params=params(),
        cost_estimate=lasts(22),
        name="expert",
    )(jnp.reshape(expert, (1,)).astype(jnp.int32), rows, grad_rows, router_pad, w_gate, w_up, w_down, *waits)


def products_kernel(wide, bits_ref, left0, left1, right0, right1, *refs):
    total = contract_first(left0[...], right0[...]) + contract_first(left1[...], right1[...])
    for which in range(2):

        @pl.when(pl.program_id(0) == which)
        def _():
            if not wide:
                refs[which - 2][...] = total.astype(jnp.bfloat16)
                return
            total_ref = refs[-1]
            total_ref[...] = (total + refs[which][...].astype(jnp.float32)).astype(jnp.bfloat16)
            send_ref, keep_ref = refs[-5 + 2 * which : len(refs) - 3 + 2 * which]
            bit = bits_ref[1 + which]
            half = send_ref.shape[0]
            keep_ref[...] = total_ref[pl.ds(pl.multiple_of(bit * half, half), half)]
            send_ref[...] = total_ref[pl.ds(pl.multiple_of((1 - bit) * half, half), half)]


def products(left, right, arrived=None, waits=()):
    place = lax.axis_index("rep")
    wide = arrived is not None
    core = bit_of(place, 1)
    bits = jnp.stack(
        [core if wide else 1 - core] + [bit_of(place, order_of(w)[1]) for w in range(2)]
    ).astype(jnp.int32)
    count = left[0].shape[0]
    rows, cols = left[0].shape[1] // 2, right[0].shape[1] // 2
    if rows % 128 or cols % 128:
        return products_plain(left, right, arrived)
    deep, number = (rows // 2, 4) if wide else (rows, 2)
    return pl.pallas_call(
        functools.partial(products_kernel, wide),
        grid_spec=pltpu.PrefetchScalarGridSpec(
            num_scalar_prefetch=1,
            grid=(2,),
            in_specs=[pl.BlockSpec((count, rows), lambda h, b: (0, h))] * 2
            + [pl.BlockSpec((count, cols), lambda h, b: (0, b[0]))] * 2
            + ([pl.BlockSpec((rows, cols), lambda h, b: (0, 0))] * 2 if wide else [])
            + [ANY] * len(waits),
            out_specs=[pl.BlockSpec((deep, cols), lambda h, b: (0, 0))] * number,
            scratch_shapes=[pltpu.VMEM((rows, cols), jnp.bfloat16)] if wide else [],
        ),
        out_shape=[jax.ShapeDtypeStruct((deep, cols), jnp.bfloat16)] * number,
        compiler_params=params(),
        cost_estimate=lasts(8),
        name="products",
    )(bits, *left, *right, *(arrived if wide else []), *waits)


def products_plain(left, right, arrived):
    total = contract_first(left[0], right[0]) + contract_first(left[1], right[1])
    theirs, mine = halves_of(total, 1, 1)
    if arrived is None:
        return jnp.split(theirs.astype(jnp.bfloat16), 2, axis=0)
    mine = [
        (m + a.astype(jnp.float32)).astype(jnp.bfloat16)
        for m, a in zip(jnp.split(mine, 2, axis=0), arrived)
    ]
    return [cut for w in range(2) for cut in halves_of(mine[w], order_of(w)[1], 0)]


def norm_back(x, gain, grad):
    scale = lax.rsqrt(jnp.mean(x * x, axis=-1, keepdims=True) + 1e-06)
    plain = x * scale
    inner = grad * gain
    by_x = scale * (inner - plain * jnp.mean(inner * plain, axis=-1, keepdims=True))
    return by_x, jnp.sum(grad * plain, axis=0, keepdims=True)


def unwind_kernel(
    length_ref, back_ref, hit0_ref, hit1_ref, picks_ref, kept_ref, hidden_ref, xn_ref, cot_ref,
    router_ref, gain_ref, wout_ref, qkv_ref, bias_ref, *refs
):
    mixed_ref, dhidden_ref, dattn_ref, dqkv_ref, drouter_ref, dgain_ref, dscores_ref, dheads_ref = refs[-8:]
    xn = xn_ref[...]
    hidden = hidden_ref[...]
    grad_out = cot_ref[0].astype(jnp.float32)
    logits = dot(xn, router_ref[...])
    lane = lax.broadcasted_iota(jnp.int32, logits.shape, 1)
    logits = jnp.where(lane < EXPERTS, logits, -1e30)
    weights = jnp.exp(logits - jnp.max(logits, axis=-1, keepdims=True))
    route = weights / jnp.sum(weights, axis=-1, keepdims=True)
    mixed = hidden
    grad_route = jnp.zeros_like(route)
    for k, hit_ref in enumerate((hit0_ref, hit1_ref)):
        pair = sum(dot(hit_ref[m], back_ref[m, 0]) for m in range(back_ref.shape[0]))
        pick = jnp.where(lane == picks_ref[:, k : k + 1], kept_ref[:, k : k + 1], 0.0)
        mixed = mixed + jnp.sum(route * pick, axis=-1, keepdims=True) * pair
        grad_route = grad_route + pick * jnp.sum(grad_out * pair, axis=-1, keepdims=True)
    mixed_ref[...] = mixed.astype(jnp.bfloat16)
    grad_logits = route * (grad_route - jnp.sum(route * grad_route, axis=-1, keepdims=True))
    grad_logits = grad_logits.astype(jnp.bfloat16)
    drouter_ref[...] = contract_first(xn, grad_logits)
    grad_xn = contract_last(grad_logits, router_ref[...]) + sum(
        dot(hit0_ref[m] + hit1_ref[m], back_ref[m, 1]) for m in range(back_ref.shape[0])
    )
    by_hidden, by_gain = norm_back(hidden, gain_ref[...], grad_xn)
    dgain_ref[...] = by_gain
    grad_hidden = grad_out + by_hidden
    dhidden_ref[...] = grad_hidden
    grad_attn = grad_hidden.astype(jnp.bfloat16)
    dattn_ref[...] = grad_attn
    dheads_ref[...] = contract_last(grad_attn, wout_ref[...]).astype(jnp.bfloat16)
    allowed = allowed_pairs(length_ref[0])
    scale = HEAD_DIM ** (-0.5)
    for pair in range(HEADS // 2):
        outs = [[], [], []]
        for head in (2 * pair, 2 * pair + 1):
            at = head * HEAD_DIM
            query = qkv_ref[:, at : at + HEAD_DIM]
            key = qkv_ref[:, D + at : D + at + HEAD_DIM]
            value = qkv_ref[:, 2 * D + at : 2 * D + at + HEAD_DIM]
            grad_head = dheads_ref[:, at : at + HEAD_DIM]
            scores = contract_last(key, query)
            scores = jnp.where(allowed, scores * scale + bias_ref[head].astype(jnp.float32), -1e30)
            weights = jnp.exp(scores - jnp.max(scores, axis=0, keepdims=True))
            probs = weights / jnp.sum(weights, axis=0, keepdims=True)
            grad_probs = contract_last(value, grad_head)
            grad_scores = probs * (grad_probs - jnp.sum(probs * grad_probs, axis=0, keepdims=True))
            grad_scores = grad_scores.astype(jnp.bfloat16)
            dscores_ref[head] = grad_scores
            outs[0].append(contract_first(grad_scores, key) * scale)
            outs[1].append(dot(grad_scores, query) * scale)
            outs[2].append(dot(probs.astype(jnp.bfloat16), grad_head))
        for i in range(3):
            dqkv_ref[:, i * D + pair * 128 : i * D + (pair + 1) * 128] = jnp.concatenate(
                outs[i], axis=1
            ).astype(jnp.bfloat16)


def unwind(
    micro, length, back, hits, picks, kept, hidden, xn_second, cotangent, router_pad, gain_second,
    out_weight, qkv_rows, bias_full, waits
):
    whole = lambda a: pl.BlockSpec(a.shape, lambda i: (0,) * a.ndim)
    gain_row = gain_second.reshape(1, D)
    ins = [back, hits[0], hits[1], picks, kept, hidden, xn_second, cotangent, router_pad, gain_row, out_weight, qkv_rows, bias_full]
    specs = [whole(a) for a in ins]
    specs[7] = pl.BlockSpec((1, SLOT, D), lambda i: (micro, 0, 0))
    out_shape = [
        jax.ShapeDtypeStruct((SLOT, D), jnp.bfloat16),
        jax.ShapeDtypeStruct((SLOT, D), jnp.float32),
        jax.ShapeDtypeStruct((SLOT, D), jnp.bfloat16),
        jax.ShapeDtypeStruct((SLOT, 3 * D), jnp.bfloat16),
        jax.ShapeDtypeStruct((D, 128), jnp.float32),
        jax.ShapeDtypeStruct((1, D), jnp.float32),
        jax.ShapeDtypeStruct((HEADS, SLOT, SLOT), jnp.bfloat16),
    ]
    return pl.pallas_call(
        unwind_kernel,
        grid=(1,),
        in_specs=[SMEM] + specs + [ANY] * len(waits),
        out_specs=[whole(o) for o in out_shape],
        out_shape=out_shape,
        scratch_shapes=[pltpu.VMEM((SLOT, D), jnp.bfloat16)],
        compiler_params=params(),
        cost_estimate=lasts(17),
        name="unwind",
    )(length.reshape(1), *ins, *waits)


def weights_kernel(groups, wide, bits_ref, xn0, xn1, dqkv0, dqkv1, heads0, heads1, dattn0, dattn1, *refs):
    count = D // groups // 2

    def rows_of(ref):
        return jnp.concatenate(
            [
                ref[:, pl.ds(pl.multiple_of((2 * g + bits_ref[0]) * count, count), count)]
                for g in range(groups)
            ],
            axis=1,
        )

    left = [rows_of(xn0), rows_of(xn1)]
    heads = [rows_of(heads0), rows_of(heads1)]
    half = count // 2
    for part in range(4):
        if part < 3:
            span = slice(part * D, (part + 1) * D)
            total = contract_first(left[0], dqkv0[:, span]) + contract_first(left[1], dqkv1[:, span])
        else:
            total = contract_first(heads[0], dattn0[...]) + contract_first(heads[1], dattn1[...])
        total = total.reshape(groups, count, D)
        which, span = part // 2, slice(part % 2 * D, (part % 2 + 1) * D)
        if not wide:
            refs[-1][which, :, :, span] = total.astype(jnp.bfloat16)
            continue
        total = total + refs[0][which, :, :, span].astype(jnp.float32)
        total_ref = refs[-1]
        total_ref[...] = total.astype(jnp.bfloat16)
        send_ref, keep_ref = refs[-5 + 2 * which : len(refs) - 3 + 2 * which]
        bit = bits_ref[1 + which]
        keep_ref[:, :, span] = total_ref[:, pl.ds(pl.multiple_of(bit * half, half), half)]
        send_ref[:, :, span] = total_ref[:, pl.ds(pl.multiple_of((1 - bit) * half, half), half)]


def weight_grads(groups, xn_all, dqkv, heads, dattn, arrived=None):
    place = lax.axis_index("rep")
    wide = arrived is not None
    core = bit_of(place, 1)
    bits = jnp.stack(
        [core if wide else 1 - core] + [bit_of(place, order_of(w)[1]) for w in range(2)]
    ).astype(jnp.int32)
    count = D // groups // 2
    if count % 128:
        return weight_grads_plain(groups, xn_all, dqkv, heads, dattn, arrived)
    shapes = [(groups, count // 2, 2 * D)] * 4 if wide else [(2, groups, count, 2 * D)]
    return pl.pallas_call(
        functools.partial(weights_kernel, groups, wide),
        in_specs=[SMEM] + [VMEM] * (9 if wide else 8),
        out_specs=[VMEM] * len(shapes),
        out_shape=[jax.ShapeDtypeStruct(shape, jnp.bfloat16) for shape in shapes],
        scratch_shapes=[pltpu.VMEM((groups, count, D), jnp.bfloat16)] if wide else [],
        compiler_params=params(),
        cost_estimate=lasts(6),
        name="weights",
    )(bits, *xn_all, *dqkv, *heads, *dattn, *([arrived] if wide else []))


def weight_grads_plain(groups, xn_all, dqkv, heads, dattn, arrived):
    total = jnp.concatenate(
        [
            contract_first(jnp.concatenate(xn_all, axis=0), jnp.concatenate(dqkv, axis=0)),
            contract_first(jnp.concatenate(heads, axis=0), jnp.concatenate(dattn, axis=0)),
        ],
        axis=1,
    ).reshape(groups, D // groups, 4 * D)
    theirs, mine = halves_of(total, 1, 1)
    if arrived is None:
        return [jnp.stack(jnp.split(theirs.astype(jnp.bfloat16), 2, axis=2))]
    mine = [
        (m + a.astype(jnp.float32)).astype(jnp.bfloat16)
        for m, a in zip(jnp.split(mine, 2, axis=2), arrived)
    ]
    return [cut for w in range(2) for cut in halves_of(mine[w], order_of(w)[1], 1)]


def finish_kernel(tokens_ref, gain_ref, wqkv_ref, dqkv0, dqkv1, dhidden0, dhidden1, out_ref, dgain_ref):
    total = None
    for micro, (dqkv, dhidden) in enumerate(((dqkv0, dhidden0), (dqkv1, dhidden1))):
        grad = contract_last(dqkv[...], wqkv_ref[...])
        by_x, by_gain = norm_back(tokens_ref[micro].astype(jnp.float32), gain_ref[...], grad)
        out_ref[micro] = dhidden[...] + by_x
        total = by_gain if total is None else total + by_gain
    dgain_ref[...] = total


def finish(tokens, gain_first, qkv_weight, dqkv, dhidden):
    return pl.pallas_call(
        finish_kernel,
        in_specs=[VMEM] * 7,
        out_specs=[VMEM] * 2,
        out_shape=[
            jax.ShapeDtypeStruct((MICRO, SLOT, D), jnp.float32),
            jax.ShapeDtypeStruct((1, D), jnp.float32),
        ],
        compiler_params=params(),
        cost_estimate=lasts(10),
        name="finish",
    )(tokens, gain_first.reshape(1, D), qkv_weight, *dqkv, *dhidden)


def join_small(by_distance, router, gains, rel_bias):
    groups = lax.axis_size("grp")
    place = lax.axis_index("grp")
    a, b = router.size, router.size + gains.size
    size = b + rel_bias.size
    blocks = [by_distance[m][:size].astype(jnp.float32) for m in range(groups)]
    rows = []
    for at in range(groups):
        row = blocks[0]
        for m in range(1, groups):
            row = jnp.where(place ^ m == at, blocks[m], row)
        rows.append(row)
    every = jnp.stack(rows)
    return (
        every[:, :a].reshape(-1, router.shape[1]).astype(jnp.bfloat16),
        every[:, a:b].reshape(-1, gains.shape[1]),
        every[:, b:].reshape(-1, rel_bias.shape[1]),
    )


def per_device(
    tokens,
    w_qkv,
    w_out,
    router,
    gains,
    rel_bias,
    w_gate,
    w_up,
    w_down,
    lengths,
    choices,
    priority,
    cotangent,
):
    groups = lax.axis_size("grp")
    split_count = groups // EXPERTS
    place = lax.axis_index("grp")
    my_expert = place // split_count
    small = jnp.concatenate([router.reshape(-1), gains.reshape(-1), rel_bias.reshape(-1)])
    chains, came_along = gather_weights(w_qkv, w_out, small)
    after = [chains[1][1][0][1]]
    router_weight, gain_full, bias_table = join_small(came_along, router, gains, rel_bias)
    router_pad = jnp.pad(router_weight, ((0, 0), (0, 128 - EXPERTS)))
    bucket_hits = (
        jnp.asarray(np.ascontiguousarray(bucket_matrix().T))[:, :, None] == jnp.arange(BUCKETS)[None, None, :]
    ).astype(jnp.bfloat16)
    bias_full = jnp.einsum(
        "hk,ijk->hij", bias_table.astype(jnp.bfloat16), bucket_hits, preferred_element_type=jnp.float32
    ).astype(jnp.bfloat16)

    target = (
        (jnp.arange(groups) // split_count)[:, None] * CAP + jnp.arange(CAP)[None, :]
    ).reshape(-1)
    routes = []
    for micro in range(MICRO):
        _, kept_mask, slot_index = expert_slots(choices[micro], priority[micro], lengths[micro, 0])
        hits = [
            (slot_index[None, :, k, None] == target.reshape(groups, 1, CAP)).astype(jnp.bfloat16)
            for k in range(2)
        ]
        spots = (
            (target[:, None] == slot_index[None, :, 0]) | (target[:, None] == slot_index[None, :, 1])
        ).astype(jnp.bfloat16)
        routes.append([kept_mask, hits, spots])
    spots1 = routes[1][2]
    pieces = gather_cores(chains, bias_full, router_pad, gain_full, spots1)
    for micro in range(MICRO):
        spots = routes[micro][2]
        (sent,) = tie([cotangent[micro]], *after)
        blocks = dot(spots, sent).astype(jnp.bfloat16).reshape(groups, CAP, D)
        routes[micro][2] = spots.reshape(groups, CAP, SLOT)
        routes[micro].append(to_experts(blocks).reshape(groups * CAP, D))
        after = [bias_full, router_pad, *[block for _, held in chains for _, block in held]]

    xn0, qkv0, out_weight = project(0, tokens, gain_full[:, 0], pieces, [routes[0][-1], bias_full, router_pad])

    def attended(micro, qkv_rows, waits):
        return attend(
            micro, lengths[micro], qkv_rows, tokens, bias_full, out_weight, gain_full[:, 1], routes[micro][2], waits
        )

    forward = [attended(0, qkv0, [])]
    rows0 = to_experts(forward[0][3]).reshape(groups * CAP, D)
    xn1, qkv1, qkv_weight = project(1, tokens, gain_full[:, 0], pieces, [forward[0][0], routes[1][-1]])
    forward.append(attended(1, qkv1, []))
    xn_all, qkv_all = [xn0, xn1], [qkv0, qkv1]
    blocks1, _ = tie([forward[1][3], rows0])
    rows = [rows0, to_experts(blocks1).reshape(groups * CAP, D)]

    def expert(micro, waits):
        return run_expert(
            my_expert, rows[micro], routes[micro][-1], router_pad, w_gate, w_up, w_down, waits
        )

    inner = [expert(0, [qkv_weight])]
    home0 = to_experts(inner[0][4])
    inner.append(expert(1, [inner[0][0]]))
    home1 = to_experts(inner[1][4])
    doutput, act, dgate, dup = ([inner[micro][i] for micro in range(MICRO)] for i in range(4))

    def launch(left, right, waits):
        theirs = products(left, right, None, waits)
        return theirs[0], [exchange(half, "rep", 1) for half in theirs]

    def settle(left, right, arrived, waits):
        outs = products(left, right, arrived, waits)
        pair = [Halving(w, 0) for w in range(2)]
        for w in range(2):
            pair[w].start(outs[2 * w], outs[2 * w + 1], 1)
        return pair, outs[1]

    def unwound(micro, home, waits):
        kept_mask, hits, _, _ = routes[micro]
        heads, hidden, xn_second, _ = forward[micro]
        return unwind(
            micro, lengths[micro], home, hits, choices[micro], kept_mask, hidden, xn_second, cotangent,
            router_pad, gain_full[:, 1], out_weight, qkv_all[micro], bias_full, waits,
        )

    tok, down_came = launch(act, doutput, [])
    tok, gate_came = launch(rows, dgate, [tok])
    tok, up_came = launch(rows, dup, [tok])
    down, tok = settle(act, doutput, down_came, [tok, home0])
    gate, tok = settle(rows, dgate, gate_came, [tok])
    land(down, tok)
    for half in down:
        half.halve(2)
    up, tok = settle(rows, dup, up_came, [half.kept for half in down])
    land([*gate, *down], tok)
    for half in gate:
        half.halve(2)
    for half in down:
        half.own()
    down[0].back()
    un0 = unwound(0, home0, [half.kept for half in (*gate, *down)])
    land([*up, *down, *gate], un0[0])
    for half in up:
        half.halve(2)
    down[0].back_pair()
    down[1].back()
    for half in gate:
        half.own()
    gate[0].back()
    un1 = unwound(1, home1, [half.kept for half in (*up, *down, *gate)])
    un = (un0, un1)

    def attention_grads(xn_in, arrived=None):
        return weight_grads(
            groups, xn_in, [u[3] for u in un], [forward[m][0] for m in range(MICRO)], [u[2] for u in un], arrived
        )

    (theirs,) = attention_grads(xn_all)
    land([*up, *down, gate[0]], theirs)
    came = exchange(tie([theirs], up[0].kept)[0], "rep", 1)
    for half in up:
        half.own()
        half.back()
    down[1].back_pair()
    gate[1].back()
    dscores = tie([u[6] for u in un], *[half.kept for half in up])
    bias_grad = sum(
        jnp.einsum("hij,ijk->hk", d, bucket_hits, preferred_element_type=jnp.float32) for d in dscores
    )
    outs = attention_grads(tie(xn_all, bias_grad, *[half.kept for half in (*up, *gate)]), came)
    attn = [Halving(w, 1) for w in range(2)]
    for w in range(2):
        attn[w].start(outs[2 * w], outs[2 * w + 1], 1)
    land([*up, *gate, *down], outs[0])
    down_own, down_got = swap_cores(down)
    token_grads, dgain_first = finish(
        tie([tokens], down_own)[0], gain_full[:, 0], qkv_weight, [u[3] for u in un], [u[1] for u in un]
    )

    small = [
        (un0[4] + un1[4])[:, :EXPERTS].reshape(-1),
        jnp.stack([dgain_first[0], un0[5][0] + un1[5][0]], axis=1).reshape(-1),
        bias_grad.reshape(-1),
    ]
    flat = jnp.concatenate(small)
    flat = jnp.pad(flat, (0, -flat.size % 1024)).reshape(-1, 128)
    steps = [("rep", m) for m in masks_of(lax.axis_size("rep"))] + [("grp", m) for m in masks_of(groups)]
    small_sum = Halving(0, 0)
    small_sum.kept = flat

    def add_small():
        if small_sum.moving is not None:
            small_sum.kept, small_sum.moving = small_sum.kept + small_sum.moving, None
        if steps:
            small_sum.moving = exchange(small_sum.kept, *steps.pop(0))

    add_small()
    down_grad = assemble(down, *tie([down_own, down_got], small_sum.kept))
    land([*attn, small_sum], down_grad)
    for half in attn:
        half.halve(2)
    add_small()
    land([*attn, small_sum])
    for half in attn:
        half.own()
    zsum = Halving(0, 0)
    zsum.kept = to_experts(jnp.stack([half.kept for half in attn], axis=1))
    for half in (*gate, *up):
        half.kept, half.moving = tie([half.kept, half.moving], *[a.kept for a in attn])
        half.back_pair()
    add_small()
    land([zsum, *gate, *up, small_sum])
    total = jnp.sum(zsum.kept.astype(jnp.float32), axis=0).astype(jnp.bfloat16)
    for w in range(2):
        attn[w].kept = total[w]
        attn[w].back()
    land([*gate, *up], total)
    gate_own, gate_got = swap_cores(gate)
    add_small()
    land([*attn, small_sum], gate_own)
    for half in attn:
        half.back_pair()
    land(up, attn[0].kept)
    up_own, up_got = swap_cores(up)
    gate_grad = assemble(gate, *tie([gate_own, gate_got], up_own))
    add_small()
    land([*attn, small_sum], gate_grad)
    attn_own, attn_got = swap_cores(attn)
    up_grad = assemble(up, *tie([up_own, up_got], attn_own))
    while small_sum.moving is not None:
        add_small()
    flat = small_sum.kept
    qkv_grad, out_grad = assemble_attention(attn, *tie([attn_own, attn_got], up_grad))

    flat = flat.reshape(-1)
    outs = []
    start = 0
    for whole in ((D, EXPERTS), (D, 2), (HEADS, BUCKETS)):
        size = whole[0] * whole[1]
        rows_here = whole[0] // groups
        outs.append(
            lax.dynamic_slice_in_dim(
                flat[start : start + size].reshape(whole), place * rows_here, rows_here, 0
            )
        )
        start += size
    return (
        jnp.stack([u[0] for u in un]),
        token_grads,
        qkv_grad,
        out_grad,
        outs[0],
        outs[1],
        outs[2],
        gate_grad[None],
        up_grad[None],
        down_grad[None],
    )


def solution(mesh):
    placed = (
        P(None, ("rep", "grp"), None),
        P("grp", None),
        P("grp", None),
        P("grp", None),
        P("grp", None),
        P("grp", None),
        P("grp", None, None),
        P("grp", None, None),
        P("grp", None, None),
        P(None, ("rep", "grp")),
        P(None, ("rep", "grp"), None),
        P(None, ("rep", "grp")),
        P(None, ("rep", "grp"), None),
    )
    return jax.shard_map(
        per_device,
        mesh=mesh,
        in_specs=placed,
        out_specs=(
            P(None, ("rep", "grp"), None),
            P(None, ("rep", "grp"), None),
            P("grp", None),
            P("grp", None),
            P("grp", None),
            P("grp", None),
            P("grp", None),
            P("grp", None, None),
            P("grp", None, None),
            P("grp", None, None),
        ),
        check_vma=False,
    )
```
